32 devices in a mesh: group: 4 (over z), dp: 2 (over x), tensor: 4 (over y, core).
Axes of the slice: x: 2, y: 2, z: 4, core: 2. Of those that a mesh axis runs over, the one named last changes fastest.
Arguments:
- block_input: bfloat16 [20480, 2048], P(('group', 'dp', 'tensor')), may hold values from -6 to 6
- cotangent: bfloat16 [20480, 2048], P(('group', 'dp', 'tensor')), may hold values from -6 to 6
- lengths: int32 [8, 8], P(('group', 'dp')), may hold values from 0 to 2560, as said below
- weight_heads: float32 [2048, 8192], P(('dp', 'group'), 'tensor')
- weight_hidden: float32 [2, 2048, 8192], P(None, ('dp', 'group'), 'tensor')
- norm_gains: float32 [2, 2048], P(None, 'group'), may hold values from 0.5 to 1.5
- momentum_heads: float32 [2048, 8192], P(('dp', 'group'), 'tensor'), may hold values from -0.15625 to 0.15625
- momentum_hidden: float32 [2, 2048, 8192], P(None, ('dp', 'group'), 'tensor'), may hold values from -0.15625 to 0.15625
- momentum_gains: float32 [2, 2048], P(None, 'group'), may hold values from -3 to 3
- average_heads: float32 [2048, 8192], P(('dp', 'group'), 'tensor'), may hold values from -0.125 to 0.125
- average_hidden: float32 [2, 2048, 8192], P(None, ('dp', 'group'), 'tensor'), may hold values from -0.125 to 0.125
- average_gains: float32 [2, 2048], P(None, 'group'), may hold values from 0.5 to 1.5
- first_heads: float32 [4, 2048, 8192], P('group', 'dp', 'tensor'), may hold values from -24 to 24
- first_hidden: float32 [4, 2, 2048, 8192], P('group', None, 'dp', 'tensor'), may hold values from -24 to 24
- first_gains: float32 [4, 2, 2048], P('group'), may hold values from -48 to 48
- second_heads: float32 [4, 2048, 8192], P('group', 'dp', 'tensor'), may hold values from 66.56 to 271.36
- second_hidden: float32 [4, 2, 2048, 8192], P('group', None, 'dp', 'tensor'), may hold values from 66.56 to 271.36
- second_gains: float32 [4, 2, 2048], P('group'), may hold values from 256 to 1024
Outputs:
- block_output: bfloat16 [20480, 2048], P(('group', 'dp', 'tensor'))
- input_grad: float32 [20480, 2048], P(('group', 'dp', 'tensor'))
- moment_heads: float32 [4, 2048, 8192], P('group', 'dp', 'tensor')
- moment_hidden: float32 [4, 2, 2048, 8192], P('group', None, 'dp', 'tensor')
- moment_gains: float32 [4, 2, 2048], P('group')
- square_heads: float32 [4, 2048, 8192], P('group', 'dp', 'tensor')
- square_hidden: float32 [4, 2, 2048, 8192], P('group', None, 'dp', 'tensor')
- square_gains: float32 [4, 2, 2048], P('group')
- change_heads: float32 [2048, 8192], P(('dp', 'group'), 'tensor')
- change_hidden: float32 [2, 2048, 8192], P(None, ('dp', 'group'), 'tensor')
- change_gains: float32 [2, 2048], P(None, 'group')
- velocity_heads: float32 [2048, 8192], P(('dp', 'group'), 'tensor')
- velocity_hidden: float32 [2, 2048, 8192], P(None, ('dp', 'group'), 'tensor')
- velocity_gains: float32 [2, 2048], P(None, 'group')
- trail_heads: float32 [2048, 8192], P(('dp', 'group'), 'tensor')
- trail_hidden: float32 [2, 2048, 8192], P(None, ('dp', 'group'), 'tensor')
- trail_gains: float32 [2, 2048], P(None, 'group')
- master_heads: float32 [2048, 8192], P(('dp', 'group'), 'tensor')
- master_hidden: float32 [2, 2048, 8192], P(None, ('dp', 'group'), 'tensor')
- master_gains: float32 [2, 2048], P(None, 'group')
- copy_heads: bfloat16 [2048, 8192], P(('dp', 'group'), 'tensor')
- copy_hidden: bfloat16 [2, 2048, 8192], P(None, ('dp', 'group'), 'tensor')
The draws below stay inside these ranges and needn't reach their ends.
Inputs may be any that keep to these rules, and one draw needn't show every extreme that they name: `lengths`: each row sums to 2560; items may be empty. In every draw one row is a single item of 2560 tokens, and every other row holds one item of 640 to 1280 tokens beside others.
All inputs are finite; a program needn't handle non-finite values.
Results may differ from the reference program's by a relative error of at most 0.028.
Values may be sent and summed in bfloat16 or wider, within the bound.
No kernel may reach another device: no remote copies, remote signals or barrier semaphores. Data moves between devices by JAX's collectives and lax.ppermute only.
A program may use at most 448 MiB of HBM per device.

```python
import math
import jax
import jax.numpy as jnp
from jax import lax

D = 2048
HEADS = 16
HEAD_DIM = 128
FF = 8192
TOK_DEV = 2560
ITEMS = 8
STEP = 8
SHARDS = 8
TOK_GROUP = 5120
TOKENS = 20480
N_GROUP = 4
N_DP = 2


def draw_lengths(key, part):
    key = jax.random.fold_in(key, 11)
    key_long, key_full, key_cuts, key_turn = jax.random.split(key, 4)
    longest = jax.random.randint(key_long, (SHARDS,), TOK_DEV // 4, TOK_DEV // 2 + 1)
    full_row = jax.random.randint(key_full, (), 0, SHARDS)
    longest = jnp.where(jnp.arange(SHARDS) == full_row, TOK_DEV, longest)
    rest = TOK_DEV - longest
    cuts = jax.random.randint(key_cuts, (SHARDS, ITEMS - 2), 0, rest[:, None] + 1)
    cuts = jnp.sort(cuts, axis=1)
    bounds = jnp.concatenate([jnp.zeros((SHARDS, 1), jnp.int32), cuts, rest[:, None]], axis=1)
    pieces = bounds[:, 1:] - bounds[:, :-1]
    joined = jnp.concatenate([longest[:, None], pieces], axis=1)
    turns = jax.random.randint(key_turn, (SHARDS, 1), 0, ITEMS)
    places = (jnp.arange(ITEMS)[None, :] - turns) % ITEMS
    return jnp.take_along_axis(joined, places, axis=1).astype(jnp.int32)


def draw_weight_heads(key, part):
    key = jax.random.fold_in(key, 3)
    base = jax.random.normal(key, (D, 4 * D), jnp.float32)
    kinds = jnp.arange(4 * D) // HEAD_DIM % 4
    scale = jnp.where(kinds == 3, 4.0, 1.0) * D ** (-0.5)
    return base * scale[None, :]


def draw_weight_hidden(key, part):
    key = jax.random.fold_in(key, 5)
    base = jax.random.normal(key, (2, D, FF), jnp.float32)
    scale = jnp.where(jnp.arange(2) == 0, D ** (-0.5), FF ** (-0.5))
    return base * scale[:, None, None]


def levels(rng, extent, shards, least, largest):
    level, own = 1.0, jax.random.fold_in(rng, 6)
    for dim, blocks in shards:
        heights = jnp.exp(jax.random.uniform(jax.random.fold_in(own, dim), (blocks,), jnp.float32, least / len(shards), largest / len(shards)))
        level = level * jnp.repeat(heights, extent[dim] // blocks).reshape([-1 if axis == dim else 1 for axis in range(len(extent))])
    return level


def bell_draw(own_key, dims, deviation, most, cuts=(), held_as=jnp.bfloat16):
    values = deviation * jax.random.normal(own_key, dims, jnp.float32)
    if cuts:
        values = values * levels(own_key, dims, cuts, -0.22, 0.18)
    return jnp.clip(values, -most, most).astype(held_as)


def setup_inputs(seed: int = 0) -> dict:
    arg_keys = jax.random.split(jax.random.key(seed), 19)
    block_input = bell_draw(arg_keys[0], (TOKENS, D), 1.0, 6.0, ((0, 32),))
    cotangent = bell_draw(arg_keys[1], (TOKENS, D), 1.0, 6.0, ((0, 32),))
    lengths = draw_lengths(jax.random.fold_in(arg_keys[18], 71), 0)
    weight_heads = draw_weight_heads(jax.random.fold_in(arg_keys[18], 71), 0)
    weight_hidden = draw_weight_hidden(jax.random.fold_in(arg_keys[18], 71), 0)
    norm_gains = jnp.clip(1.0 + 0.1 * jax.random.normal(arg_keys[5], (2, D), jnp.float32), 0.5, 1.5)
    momentum_heads = bell_draw(arg_keys[6], (D, 4 * D), 0.01, 0.15625, ((0, 8), (1, 4)), jnp.float32)
    momentum_hidden = bell_draw(arg_keys[7], (2, D, FF), 0.01, 0.15625, ((1, 8), (2, 4)), jnp.float32)
    momentum_gains = bell_draw(arg_keys[8], (2, D), 0.2, 3.0, ((1, 4),), jnp.float32)
    average_heads = bell_draw(arg_keys[9], (D, 4 * D), D ** -0.5, 0.125, ((0, 8), (1, 4)), jnp.float32)
    average_hidden = bell_draw(arg_keys[10], (2, D, FF), D ** -0.5, 0.125, ((1, 8), (2, 4)), jnp.float32)
    average_gains = jnp.clip(1.0 + 0.1 * jax.random.normal(arg_keys[11], (2, D), jnp.float32), 0.5, 1.5)
    first_heads = bell_draw(arg_keys[12], (N_GROUP, D, 4 * D), (0.055 * TOK_GROUP ** 0.5), 24.0, ((0, 4), (1, 2), (2, 4)), jnp.float32)
    first_hidden = bell_draw(arg_keys[13], (N_GROUP, 2, D, FF), (0.055 * TOK_GROUP ** 0.5), 24.0, ((0, 4), (2, 2), (3, 4)), jnp.float32)
    first_gains = bell_draw(arg_keys[14], (N_GROUP, 2, D), (0.11 * TOK_GROUP ** 0.5), 48.0, ((0, 4),), jnp.float32)
    second_heads = jnp.clip(jnp.exp(math.log(271.36) - 1.40534254 * jax.random.uniform(arg_keys[15], (N_GROUP, D, 4 * D), jnp.float32) ** levels(arg_keys[15], (N_GROUP, D, 4 * D), ((0, 4), (1, 2), (2, 4)), -0.2, 0.2)), 66.56, 271.36)
    second_hidden = jnp.clip(jnp.exp(math.log(271.36) - 1.40534254 * jax.random.uniform(arg_keys[16], (N_GROUP, 2, D, FF), jnp.float32) ** levels(arg_keys[16], (N_GROUP, 2, D, FF), ((0, 4), (2, 2), (3, 4)), -0.2, 0.2)), 66.56, 271.36)
    second_gains = jnp.clip(jnp.exp(math.log(1024.0) - 1.3862944 * jax.random.uniform(arg_keys[17], (N_GROUP, 2, D), jnp.float32) ** levels(arg_keys[17], (N_GROUP, 2, D), ((0, 4),), -0.2, 0.2)), 256.0, 1024.0)
    return dict(block_input=block_input, cotangent=cotangent, lengths=lengths, weight_heads=weight_heads, weight_hidden=weight_hidden, norm_gains=norm_gains, momentum_heads=momentum_heads, momentum_hidden=momentum_hidden, momentum_gains=momentum_gains, average_heads=average_heads, average_hidden=average_hidden, average_gains=average_gains, first_heads=first_heads, first_hidden=first_hidden, first_gains=first_gains, second_heads=second_heads, second_hidden=second_hidden, second_gains=second_gains)


@jax.custom_vjp
def low(v):
    return lax.optimization_barrier(v.astype(jnp.bfloat16)).astype(jnp.float32)

@jax.custom_vjp
def low_back(v):
    return v

def low_keep(v):
    return (low(v), None)

def low_pass(kept, grad):
    return (grad,)

def back_keep(v):
    return (v, None)

def back_low(kept, grad):
    return (low(grad),)
low.defvjp(low_keep, low_pass)
low_back.defvjp(back_keep, back_low)
NORM_EPS = 1e-05
INNER_RATE = 0.02
GAIN_RATE = 0.5
BETA_ONE = 0.9
BETA_TWO = 0.95
ADAM_EPS = 1e-08
WEIGHT_DECAY = 0.1
OUTER_RATE = 0.7
OUTER_MOMENTUM = 0.9
EMA_KEEP = 0.5

def highest(left, right):
    return jnp.dot(left, right, precision=lax.Precision.HIGHEST)

def layer_norm(rows, gain):
    mean = lax.optimization_barrier(jnp.mean(rows, axis=-1, keepdims=True))
    centred = rows - mean
    var = lax.optimization_barrier(jnp.mean(centred * centred, axis=-1, keepdims=True))
    return centred * lax.rsqrt(var + NORM_EPS) * gain

def item_ids(lengths, total):
    ends = jnp.cumsum(lengths).astype(jnp.int32)
    places = jnp.arange(total, dtype=jnp.int32)
    return lax.optimization_barrier(jnp.sum((places[:, None] >= ends[None, :]).astype(jnp.int32), axis=1)).astype(jnp.int32)

def attend(query, key_rows, value, items):
    count = query.shape[0]
    scores = low_back(highest(query, key_rows.T) * HEAD_DIM ** (-0.5))
    places = jnp.arange(count, dtype=jnp.int32)
    live = (places[:, None] >= places[None, :]) & (items[:, None] == items[None, :])
    scores = jnp.where(live, scores, -1e+30)
    weights = jax.nn.softmax(scores, axis=-1)
    return highest(low(weights), value)

def shard_forward(rows, items, split_heads, split_hidden, gains):
    normed = low(layer_norm(rows, gains[0]))
    triple = jnp.einsum('td,dhce->chte', normed, split_heads[:, :, :3, :], precision=lax.Precision.HIGHEST)
    triple = low(low_back(triple))
    head_fn = jax.checkpoint(lambda trio: attend(trio[0], trio[1], trio[2], items))
    mixed = lax.map(head_fn, (triple[0], triple[1], triple[2]))
    mixed = low(low_back(mixed))
    branch = low_back(jnp.einsum('hte,dhe->td', mixed, split_heads[:, :, 3, :], precision=lax.Precision.HIGHEST))
    middle = rows + branch
    second = low(layer_norm(middle, gains[1]))
    before = low_back(highest(second, split_hidden[0]))
    hidden = low(jax.nn.gelu(before, approximate=False))
    branch_two = low_back(jnp.einsum('tf,df->td', hidden, split_hidden[1], precision=lax.Precision.HIGHEST))
    return middle + branch_two

def group_forward(rows, items, weight_heads, weight_hidden, gains):
    split_heads = low(weight_heads).reshape(D, HEADS, 4, HEAD_DIM)
    split_hidden = low(weight_hidden)
    shard_fn = jax.checkpoint(lambda pair: shard_forward(pair[0], pair[1], split_heads, split_hidden, gains))
    return lax.map(shard_fn, (rows, items))

def adam_step(weight, grad, first, second, rate, decay):
    first = BETA_ONE * first + (1.0 - BETA_ONE) * grad
    second = BETA_TWO * second + (1.0 - BETA_TWO) * grad * grad
    scaled_first = first / (1.0 - BETA_ONE ** STEP)
    scaled_second = second / (1.0 - BETA_TWO ** STEP)
    update = scaled_first / (jnp.sqrt(scaled_second) + ADAM_EPS) + decay * weight
    return (first, second, rate * update)

def outer_step(weight, change, momentum, average):
    velocity = OUTER_MOMENTUM * momentum + change
    master = weight - OUTER_RATE * (change + OUTER_MOMENTUM * velocity)
    trail = EMA_KEEP * average + (1.0 - EMA_KEEP) * master
    return (velocity, trail, master)

def reference(block_input, cotangent, lengths, weight_heads, weight_hidden, norm_gains, momentum_heads, momentum_hidden, momentum_gains, average_heads, average_hidden, average_gains, first_heads, first_hidden, first_gains, second_heads, second_hidden, second_gains):
    group_rows = N_DP * TOK_DEV
    outputs = []
    input_grads = []
    moments = [[], [], []]
    squares = [[], [], []]
    deltas = [[], [], []]
    for group in range(N_GROUP):
        start = group * group_rows
        rows = block_input[start:start + group_rows].astype(jnp.float32).reshape(N_DP, TOK_DEV, D)
        back = cotangent[start:start + group_rows].astype(jnp.float32).reshape(N_DP, TOK_DEV, D)
        items = jnp.stack([item_ids(lengths[group * N_DP + shard], TOK_DEV) for shard in range(N_DP)])

        def forward(inputs, heads_w, hidden_w, gains_w):
            return group_forward(inputs, items, heads_w, hidden_w, gains_w)
        result, pull = jax.vjp(forward, rows, weight_heads, weight_hidden, norm_gains)
        grad_rows, grad_heads, grad_hidden, grad_gains = pull(back)
        outputs.append(result.reshape(group_rows, D).astype(jnp.bfloat16))
        input_grads.append(grad_rows.reshape(group_rows, D))
        sets = [adam_step(weight_heads, grad_heads, first_heads[group], second_heads[group], INNER_RATE, WEIGHT_DECAY), adam_step(weight_hidden, grad_hidden, first_hidden[group], second_hidden[group], INNER_RATE, WEIGHT_DECAY), adam_step(norm_gains, grad_gains, first_gains[group], second_gains[group], GAIN_RATE, 0.0)]
        for index in range(3):
            moments[index].append(sets[index][0])
            squares[index].append(sets[index][1])
            deltas[index].append(sets[index][2])
    changes = [sum(deltas[index][1:], deltas[index][0]) / N_GROUP for index in range(3)]
    velocity_heads, trail_heads, master_heads = outer_step(weight_heads, changes[0], momentum_heads, average_heads)
    velocity_hidden, trail_hidden, master_hidden = outer_step(weight_hidden, changes[1], momentum_hidden, average_hidden)
    velocity_gains, trail_gains, master_gains = outer_step(norm_gains, changes[2], momentum_gains, average_gains)
    return (jnp.concatenate(outputs, axis=0), jnp.concatenate(input_grads, axis=0), jnp.stack(moments[0]), jnp.stack(moments[1]), jnp.stack(moments[2]), jnp.stack(squares[0]), jnp.stack(squares[1]), jnp.stack(squares[2]), changes[0], changes[1], changes[2], velocity_heads, velocity_hidden, velocity_gains, trail_heads, trail_hidden, trail_gains, master_heads, master_hidden, master_gains, master_heads.astype(jnp.bfloat16), master_hidden.astype(jnp.bfloat16))
```

```python
import functools
import math

import jax
import jax.numpy as jnp
from jax import lax
from jax.experimental import pallas as pl
from jax.experimental.pallas import tpu as pltpu
from jax.sharding import PartitionSpec as P

HEAD_DIM = 128
STEP = 8

NORM_EPS = 1e-05
INNER_RATE = 0.02
GAIN_RATE = 0.5
BETA_ONE = 0.9
BETA_TWO = 0.95
ADAM_EPS = 1e-08
WEIGHT_DECAY = 0.1
OUTER_RATE = 0.7
OUTER_MOMENTUM = 0.9
EMA_KEEP = 0.5

BF16 = jnp.bfloat16
F32 = jnp.float32
SCALE = HEAD_DIM ** (-0.5)
LOG2E = math.log2(math.e)
SCALE_LOG2 = SCALE * LOG2E
NEGATIVE = -1e30


def swap(value, axis, bit, size):
    return lax.ppermute(value, axis, [(i, i ^ bit) for i in range(size)])


ANYWHERE = pl.BlockSpec(memory_space=pl.ANY)
LIMIT = 60 * 2**20
line = []


def run(kernel, name, grid, meta, ins, outs, scratch=(), after=(), alias=None):
    arrays = [a for a, _ in ins]
    extra = [a for a in line + list(after) if all(a is not b for b in arrays)]
    count, skip = len(ins), len(extra)

    def body(*refs):
        kernel(*refs[: 1 + count], *refs[1 + count + skip :])

    result = pl.pallas_call(
        body,
        grid_spec=pltpu.PrefetchScalarGridSpec(
            num_scalar_prefetch=1,
            grid=grid,
            in_specs=[s for _, s in ins] + [ANYWHERE] * skip,
            out_specs=[s for _, _, s in outs],
            scratch_shapes=list(scratch),
        ),
        out_shape=[jax.ShapeDtypeStruct(s, d) for s, d, _ in outs],
        input_output_aliases={1 + a: b for a, b in (alias or {}).items()},
        compiler_params=pltpu.CompilerParams(vmem_limit_bytes=LIMIT),
        cost_estimate=pl.CostEstimate(flops=10**12, bytes_accessed=1, transcendentals=0),
        name=name,
    )(meta, *arrays, *extra)
    line[:] = [result[0]]
    return result


def dot_last(left, right):
    return lax.dot_general(
        left, right, (((1,), (1,)), ((), ())), preferred_element_type=F32
    )


def dot_first(left, right):
    return lax.dot_general(
        left, right, (((0,), (0,)), ((), ())), preferred_element_type=F32
    )


def dot(left, right):
    return jnp.dot(left, right, preferred_element_type=F32)


def normalize(rows):
    mean = jnp.mean(rows, axis=-1, keepdims=True)
    centred = rows - mean
    var = jnp.mean(centred * centred, axis=-1, keepdims=True)
    inverse = lax.rsqrt(var + NORM_EPS)
    return centred * inverse, inverse


def normalize_back(back, normed, inverse, gain):
    scaled = back * gain
    first = jnp.mean(scaled, axis=-1, keepdims=True)
    second = jnp.mean(scaled * normed, axis=-1, keepdims=True)
    terms = (back * normed).reshape(-1, 8, back.shape[-1])
    return inverse * (scaled - first - normed * second), jnp.sum(terms, axis=0)


def gelu_parts(u):
    size = jnp.abs(u) * (0.5**0.5)
    t = 1.0 / (1.0 + 0.3275911 * size)
    poly = t * (
        0.254829592
        + t * (-0.284496736 + t * (1.421413741 + t * (-1.453152027 + t * 1.061405429)))
    )
    bell = jnp.exp(-0.5 * u * u)
    tail = 0.5 * poly * bell
    below = jnp.where(u >= 0.0, 1.0 - tail, tail)
    return below, bell * (1.0 / math.sqrt(2.0 * math.pi))


def item_start(places, meta, items):
    start = jnp.zeros_like(places)
    for k in range(items):
        start = jnp.where(places >= meta[k], meta[k], start)
    return start


def copy_in(meta, items, source, target, rows, step, total):
    for s in range(total // step):
        owner, offset = (s * step) // rows, (s * step) % rows
        local = pl.multiple_of((owner ^ meta[items]) * rows + offset, step)
        target[s * step : (s + 1) * step, :] = source[pl.ds(local, step), :]


def local_row(meta, items, chunk, rows, step):
    per = rows // step
    owner, offset = chunk // per, chunk % per
    return pl.multiple_of((owner ^ meta[items]) * rows + offset * step, step)


def attend_kernel(items, rows, step, block, meta, qkv, mixed, logs, nat, acc, top, weight):
    total = qkv.shape[0]
    index = pl.program_id(1)

    @pl.when(index == 0)
    def _():
        copy_in(meta, items, qkv, nat, rows, step, total)

    first_row = index * block
    q = nat[pl.ds(pl.multiple_of(first_row, block), block), 0:HEAD_DIM]
    acc[...] = jnp.zeros_like(acc)
    top[...] = jnp.full_like(top, NEGATIVE)
    weight[...] = jnp.zeros_like(weight)
    low_start = item_start(first_row, meta, items)
    high_start = item_start(first_row + block - 1, meta, items)

    def tile(j, masked):
        at = pl.ds(pl.multiple_of(j * block, block), block)
        k = nat[at, HEAD_DIM : 2 * HEAD_DIM]
        v = nat[at, 2 * HEAD_DIM : 3 * HEAD_DIM]
        s = dot_last(q, k)
        if masked:
            q_place = first_row + lax.broadcasted_iota(jnp.int32, (block, 1), 0)
            k_place = j * block + lax.broadcasted_iota(jnp.int32, (1, block), 1)
            live = (k_place <= q_place) & (k_place >= item_start(q_place, meta, items))
            s = jnp.where(live, s, NEGATIVE)
        old = top[:, 0:1]
        new = jnp.maximum(old, jnp.max(s, axis=1, keepdims=True))
        p = jnp.exp2((s - new) * SCALE_LOG2)
        keep = jnp.exp2((old - new) * SCALE_LOG2)
        top[...] = jnp.broadcast_to(new, top.shape)
        weight[...] = weight[...] * keep + jnp.sum(p, axis=1, keepdims=True)
        acc[...] = acc[...] * keep + dot(p.astype(BF16), v)

    @pl.loop(low_start // block, index)
    def _(j):
        whole = high_start <= j * block

        @pl.when(whole)
        def _():
            tile(j, False)

        @pl.when(jnp.logical_not(whole))
        def _():
            tile(j, True)

    tile(index, True)
    out = (acc[...] / weight[...]).astype(BF16)
    per = block // step
    for c in range(per):
        at = local_row(meta, items, index * per + c, rows, step)
        mixed[pl.ds(at, step), :] = out[c * step : (c + 1) * step, :]
    log = top[...] * SCALE_LOG2 + jnp.log(weight[...]) * LOG2E
    logs[0, 0] = log.T[0:8, :]


def attend(meta, qkv, items, rows, heads, after=()):
    total = qkv.shape[0]
    block = min(512, total)
    step = math.gcd(rows, block)
    count = total // block
    return run(
        functools.partial(attend_kernel, items, rows, step, block),
        "attend",
        (heads, count),
        meta,
        [(qkv, pl.BlockSpec((total, 3 * HEAD_DIM), lambda h, i, m: (0, h)))],
        [
            ((total, heads * HEAD_DIM), BF16, pl.BlockSpec((total, HEAD_DIM), lambda h, i, m: (0, h))),
            ((heads, count, 8, block), F32, pl.BlockSpec((1, 1, 8, block), lambda h, i, m: (h, i, 0, 0))),
        ],
        [
            pltpu.VMEM((total, 3 * HEAD_DIM), BF16),
            pltpu.VMEM((block, HEAD_DIM), F32),
            pltpu.VMEM((block, HEAD_DIM), F32),
            pltpu.VMEM((block, HEAD_DIM), F32),
        ],
        after,
    )


def attend_back_kernel(
    items, rows, step, block, meta, qkv, mixed, back, logs, grads, nat, nat_mixed, nat_back, dq, dk, dv
):
    total = qkv.shape[0]
    index = pl.program_id(1)

    @pl.when(index == 0)
    def _():
        copy_in(meta, items, qkv, nat, rows, step, total)
        copy_in(meta, items, mixed, nat_mixed, rows, step, total)
        copy_in(meta, items, back, nat_back, rows, step, total)
        dk[...] = jnp.zeros_like(dk)
        dv[...] = jnp.zeros_like(dv)

    first_row = index * block
    here = pl.ds(pl.multiple_of(first_row, block), block)
    q = nat[here, 0:HEAD_DIM]
    g = nat_back[here, :]
    product = g.astype(F32) * nat_mixed[here, :].astype(F32)
    row_term = jnp.sum(product.T, axis=0, keepdims=True)
    log = logs[0, 0, 0:1, :]
    dq[...] = jnp.zeros_like(dq)
    low_start = item_start(first_row, meta, items)
    high_start = item_start(first_row + block - 1, meta, items)

    def tile(j, masked):
        at = pl.ds(pl.multiple_of(j * block, block), block)
        k = nat[at, HEAD_DIM : 2 * HEAD_DIM]
        v = nat[at, 2 * HEAD_DIM : 3 * HEAD_DIM]
        p = jnp.exp2(dot_last(k, q) * SCALE_LOG2 - log)
        if masked:
            k_place = j * block + lax.broadcasted_iota(jnp.int32, (block, 1), 0)
            q_place = first_row + lax.broadcasted_iota(jnp.int32, (1, block), 1)
            live = (k_place <= q_place) & (k_place >= item_start(q_place, meta, items))
            p = jnp.where(live, p, 0.0)
        s = (p * (dot_last(v, g) - row_term)).astype(BF16)
        dv[at, :] += dot(p.astype(BF16), g)
        dk[at, :] += dot(s, q)
        dq[...] += dot_first(s, k)

    @pl.loop(low_start // block, index)
    def _(j):
        whole = high_start <= j * block

        @pl.when(whole)
        def _():
            tile(j, False)

        @pl.when(jnp.logical_not(whole))
        def _():
            tile(j, True)

    tile(index, True)
    out = (dq[...] * SCALE).astype(BF16)
    per = block // step
    for c in range(per):
        to = local_row(meta, items, index * per + c, rows, step)
        grads[pl.ds(to, step), 0:HEAD_DIM] = out[c * step : (c + 1) * step, :]

    @pl.when(index == pl.num_programs(1) - 1)
    def _():
        for s in range(total // step):
            to = local_row(meta, items, s, rows, step)
            part = slice(s * step, (s + 1) * step)
            grads[pl.ds(to, step), HEAD_DIM : 2 * HEAD_DIM] = (dk[part, :] * SCALE).astype(BF16)
            grads[pl.ds(to, step), 2 * HEAD_DIM : 3 * HEAD_DIM] = dv[part, :].astype(BF16)


def attend_back(meta, qkv, mixed, back, logs, items, rows, heads, after=()):
    total = qkv.shape[0]
    block = logs.shape[-1]
    step = math.gcd(rows, block)
    count = total // block
    wide = pl.BlockSpec((total, 3 * HEAD_DIM), lambda h, i, m: (0, h))
    narrow = pl.BlockSpec((total, HEAD_DIM), lambda h, i, m: (0, h))
    return run(
        functools.partial(attend_back_kernel, items, rows, step, block),
        "attend_back",
        (heads, count),
        meta,
        [
            (qkv, wide),
            (mixed, narrow),
            (back, narrow),
            (logs, pl.BlockSpec((1, 1, 8, block), lambda h, i, m: (h, i, 0, 0))),
        ],
        [(qkv.shape, BF16, wide)],
        [
            pltpu.VMEM((total, 3 * HEAD_DIM), BF16),
            pltpu.VMEM((total, HEAD_DIM), BF16),
            pltpu.VMEM((total, HEAD_DIM), BF16),
            pltpu.VMEM((block, HEAD_DIM), F32),
            pltpu.VMEM((total, HEAD_DIM), F32),
            pltpu.VMEM((total, HEAD_DIM), F32),
        ],
        after,
    )[0]


def copies(refs, places, meta, target, sems):
    out = []
    for n, (ref, (row, column)) in enumerate(zip(refs, places)):
        tall, wide = ref.shape
        at = pl.multiple_of(row(meta), tall)
        out.append(
            pltpu.make_async_copy(ref, target.at[pl.ds(at, tall), pl.ds(column, wide)], sems.at[n])
        )
    return out


def rows_kernel(count, places, saved, finish, meta, *refs):
    parts = len(places)
    pieces, strips, refs = refs[:count], refs[count : count + parts], refs[count + parts :]
    blocks, (slots, weight, piece_sems, weight_sems) = refs[:-4], refs[-4:]
    i = pl.program_id(0)

    def fetch(n):
        return pltpu.make_async_copy(pieces[n], slots.at[n % 2], piece_sems.at[n % 2])

    @pl.when(i == 0)
    def _():
        for copy in copies(strips, places, meta, weight, weight_sems):
            copy.start()
        fetch(0).start()

    for n in range(1, count):

        @pl.when(i + 1 == n)
        def _(n=n):
            fetch(n).start()

    @pl.when(i == 0)
    def _():
        for copy in copies(strips, places, meta, weight, weight_sems):
            copy.wait()

    for n in range(count):

        @pl.when(i == n)
        def _(n=n):
            fetch(n).wait()

    if saved:
        blocks, kept = blocks[:-1], blocks[-1]
        kept[...] = weight[pl.ds(pl.multiple_of(i * kept.shape[0], kept.shape[0]), kept.shape[0]), :]
    wide = min(512, weight.shape[1])

    @pl.loop(0, weight.shape[1] // wide)
    def _(n):
        at = pl.ds(pl.multiple_of(n * wide, wide), wide)
        finish(dot(slots[i % 2], weight[:, at]), at, *blocks)


def rows_matmul(name, meta, pieces, weight, finish, extra, outs, saved=0, after=()):
    strips, places = weight
    tall, depth = pieces[0].shape
    wide = max(column + a.shape[1] for a, (_, column) in zip(strips, places))
    count, parts = len(pieces), len(strips)
    block = lambda index: pl.BlockSpec((tall, wide), lambda i, m: (index(i), 0))
    more = [((saved, wide), BF16, pl.BlockSpec((saved // count, wide), lambda i, m: (i, 0)))] if saved else []
    return run(
        functools.partial(rows_kernel, count, places, saved, finish),
        name,
        (count,),
        meta,
        [(p, ANYWHERE) for p in pieces] + [(p, ANYWHERE) for p in strips] + [(a, block(f)) for a, f in extra],
        [((count * tall, wide), d, block(f)) for d, f in outs] + more,
        [
            pltpu.VMEM((2, tall, depth), BF16),
            pltpu.VMEM((depth, wide), BF16),
            pltpu.SemaphoreType.DMA((2,)),
            pltpu.SemaphoreType.DMA((parts,)),
        ],
        after,
    )


def store_rounded(value, at, out):
    out[:, at] = value.astype(BF16)


def store_gelu(value, at, back, hidden, back_before):
    below, density = gelu_parts(value)
    hidden[:, at] = (value * below).astype(BF16)
    back_before[:, at] = (back[:, at].astype(F32) * (below + value * density)).astype(BF16)


def same(i):
    return i


def term_kernel(places, half, far, meta, x, *refs):
    strips, refs = refs[: len(places)], refs[len(places) :]
    weight, sems = refs[-2:]
    i = pl.program_id(0)

    @pl.when(i == 0)
    def _():
        for copy in copies(strips, places, meta, weight, sems):
            copy.start()
        for copy in copies(strips, places, meta, weight, sems):
            copy.wait()

    wide = min(512, weight.shape[0])

    @pl.loop(0, weight.shape[0] // wide)
    def _(n):
        at = pl.ds(pl.multiple_of(n * wide, wide), wide)
        value = dot_last(x[...], weight[at, :])
        if far:
            refs[0][:, at] = value.astype(BF16)
        else:
            received, send, keep = refs[:3]
            value = (value + received[:, at].astype(F32)).astype(BF16)

            @pl.when(i < half)
            def _():
                send[:, at] = value

            @pl.when(i >= half)
            def _():
                keep[:, at] = value


def term(name, meta, x, weight, width, part, ranks, index, received=None, after=()):
    n = x.shape[1]
    strips, places = weight
    many = ranks // 2
    half = many // 2
    wide = lambda f: pl.BlockSpec((part, width), lambda i, m: (f(i), 0))
    turn = lambda i: jnp.where(i < half, 2 * i + 1, 2 * (i - half))
    if received is None:
        owner = lambda i: 2 * i + 1
        more, outs = [], [((many * part, width), BF16, wide(same))]
    else:
        owner = lambda i: 2 * turn(i)
        more = [(received, wide(turn))]
        outs = [
            ((half * part, width), BF16, wide(lambda i: jnp.minimum(i, half - 1))),
            ((half * part, width), BF16, wide(lambda i: jnp.maximum(i - half, 0))),
        ]
    return run(
        functools.partial(term_kernel, places, half, received is None),
        name,
        (many,),
        meta,
        [(x, pl.BlockSpec((part, n), lambda i, m: (index(owner(i)), 0)))] + [(s, ANYWHERE) for s in strips] + more,
        outs,
        [pltpu.VMEM((width, n), BF16), pltpu.SemaphoreType.DMA((len(strips),))],
        after,
    )


def finish_sum(send, keep, part, ranks):
    bit = 2
    while True:
        received = swap(send, "tensor", bit, ranks)
        if keep.shape[0] == part:
            return keep, received
        total = (keep.astype(F32) + received.astype(F32)).astype(BF16).reshape(-1, 2, part, keep.shape[1])
        keep, send = (total[:, n].reshape(-1, keep.shape[1]) for n in (0, 1))
        bit *= 2


def weight_grad_kernel(rows_a, rows_b, first, meta, *refs):
    count, many = len(rows_a), len(rows_b)
    left, right, refs = refs[:count], refs[count : count + many], refs[count + many :]
    out, slots, held, left_sems, right_sems = refs
    i = pl.program_id(0)
    steps = pl.num_programs(0)
    wide = slots.shape[2]

    def fetch(step, slot):
        at = pl.ds(pl.multiple_of(first + step * wide, wide), wide)
        return [
            pltpu.make_async_copy(ref.at[:, at], slots.at[slot, pl.ds(row, ref.shape[0])], left_sems.at[slot, n])
            for n, (ref, row) in enumerate(zip(left, rows_a))
        ]

    def fetch_right():
        return [
            pltpu.make_async_copy(right[n].at[pl.ds(source, tall)], held.at[pl.ds(row, tall)], right_sems.at[n])
            for n, (source, row, tall) in enumerate(rows_b)
        ]

    @pl.when(i == 0)
    def _():
        for copy in fetch(0, 0) + fetch_right():
            copy.start()

    @pl.when(i + 1 < steps)
    def _():
        for copy in fetch(i + 1, (i + 1) % 2):
            copy.start()

    @pl.when(i == 0)
    def _():
        for copy in fetch_right():
            copy.wait()

    for copy in fetch(i, i % 2):
        copy.wait()

    tile = min(512, held.shape[1])

    @pl.loop(0, held.shape[1] // tile)
    def _(n):
        at = pl.ds(pl.multiple_of(n * tile, tile), tile)
        out[:, at] = dot_first(slots[i % 2], held[:, at]).astype(BF16)


def weight_grad(name, meta, left, right, first, half, total, after=()):
    wide = min(512, half)
    n = right[0][0].shape[1]
    return run(
        functools.partial(weight_grad_kernel, [r for _, r in left], [r[1:] for r in right], first),
        name,
        (half // wide,),
        meta,
        [(a, ANYWHERE) for a, _ in left] + [(r[0], ANYWHERE) for r in right],
        [((half, n), BF16, pl.BlockSpec((wide, n), lambda i, m: (i, 0)))],
        [
            pltpu.VMEM((2, total, wide), BF16),
            pltpu.VMEM((total, n), BF16),
            pltpu.SemaphoreType.DMA((2, len(left))),
            pltpu.SemaphoreType.DMA((len(right),)),
        ],
        after,
    )[0]


def strip_at(p, place, strip):
    return pl.ds(pl.multiple_of((p ^ place) * strip, strip), strip)


def turned(ref, place, strip):
    return jnp.concatenate([ref[:, strip_at(p, place, strip)] for p in range(ref.shape[1] // strip)], axis=1)


def store_turned(ref, value, place, strip):
    for p in range(value.shape[1] // strip):
        ref[:, strip_at(p, place, strip)] = value[:, p * strip : (p + 1) * strip].astype(ref.dtype)


def gains_kernel(items, strip, meta, *refs):
    pieces, (turned_out, plain, stack) = refs[:-3], refs[-3:]
    groups, short = len(pieces), pieces[0].shape[1]
    for k in range(groups):
        stack[k] = pieces[k][...]
    for j in range(groups):
        plain[:, j * short : (j + 1) * short] = stack[j ^ meta[items + 1]]
    turned_out[...] = turned(plain, meta[items + 2], strip)


def cast_heads_kernel(meta, weight, inward, outward):
    inward[...] = weight[:, : 3 * HEAD_DIM].astype(BF16)
    outward[...] = weight[:, 3 * HEAD_DIM :].astype(BF16)


def cast_hidden_kernel(meta, weight, *outs):
    wide = outs[0].shape[1]
    for n, out in enumerate(outs):
        at = n % 2 * wide
        out[...] = weight[n // 2, :, at : at + wide].astype(BF16)


def first_norm_kernel(items, strip, meta, rows, gains, *outs):
    normed, _ = normalize(turned(rows, meta[items + 2], strip).astype(F32))
    for out in outs:
        out[...] = (normed * gains[0:1, :]).astype(BF16)


def turn_kernel(items, strip, meta, rows, *outs):
    for out in outs:
        out[...] = turned(rows, meta[items + 2], strip)


def add_kernel(meta, left, right, out):
    out[...] = left[...] + right[...]


def second_norm_kernel(items, strip, meta, rows, keep, received, gains, middle_out, *outs):
    middle = turned(rows, meta[items + 2], strip).astype(F32) + (
        keep[...].astype(F32) + received[...].astype(F32)
    )
    normed, _ = normalize(middle)
    middle_out[...] = middle
    for out in outs:
        out[...] = (normed * gains[1:2, :]).astype(BF16)


def second_back_kernel(middle, keep, received, back, gains, out, gain_out, *lows):
    normed, inverse = normalize(middle[...])
    given = keep[...].astype(F32) + received[...].astype(F32)
    grad, gain_part = normalize_back(given, normed, inverse, gains[1:2, :])
    grad = grad + back[...].astype(F32)
    out[...] = grad
    for low in lows:
        low[...] = grad.astype(BF16)

    @pl.when(pl.program_id(0) == 0)
    def _():
        gain_out[...] = jnp.zeros_like(gain_out)

    gain_out[...] += gain_part


def first_back_kernel(items, strip, meta, rows, gains, back, keep, received, out, gain_out):
    place = meta[items + 2]

    @pl.when(pl.program_id(0) == 0)
    def _():
        gain_out[...] = jnp.zeros_like(gain_out)

    normed, inverse = normalize(turned(rows, place, strip).astype(F32))
    given = keep[...].astype(F32) + received[...].astype(F32)
    grad, gain_part = normalize_back(given, normed, inverse, gains[0:1, :])
    gain_out[...] += gain_part
    store_turned(out, grad + back[...], place, strip)


def output_kernel(items, strip, meta, middle, keep, received, out):
    value = middle[...] + (keep[...].astype(F32) + received[...].astype(F32))
    store_turned(out, value, meta[items + 2], strip)


def gain_total_kernel(items, strip, meta, first, second, out):
    both = [jnp.sum(v, axis=0, keepdims=True) for v in (first[...], second[...])]
    store_turned(out, jnp.concatenate(both, axis=0), meta[items + 2], strip)


def adam_math(weight, grad, first, second, rate, decay):
    first = BETA_ONE * first + (1.0 - BETA_ONE) * grad
    second = BETA_TWO * second + (1.0 - BETA_TWO) * grad * grad
    scaled_first = first * (1.0 / (1.0 - BETA_ONE**STEP))
    scaled_second = second * (1.0 / (1.0 - BETA_TWO**STEP))
    update = scaled_first / (jnp.sqrt(scaled_second) + ADAM_EPS) + decay * weight
    return first, second, rate * update


def adam_kernel(join, counts, meta, *refs):
    parts, at = [], 0
    for count in counts:
        parts.append(join([r[...].astype(F32) for r in refs[at : at + count]]))
        at += count
    own, far, weight = parts
    first, second = refs[at : at + 2]
    moment, square, delta = refs[-3:]
    moment[...], square[...], change = adam_math(
        weight, own + far, first[...], second[...], INNER_RATE, WEIGHT_DECAY
    )
    delta[...] = change.astype(BF16)


def side_by_side(parts):
    return parts[0] if len(parts) == 1 else jnp.concatenate(parts, axis=1)


def by_head(parts):
    inward, outward = parts
    out = []
    for h in range(outward.shape[1] // HEAD_DIM):
        out += [
            inward[:, h * 3 * HEAD_DIM : (h + 1) * 3 * HEAD_DIM],
            outward[:, h * HEAD_DIM : (h + 1) * HEAD_DIM],
        ]
    return jnp.concatenate(out, axis=1)


def adam(name, meta, join, own, far, weight, first, second, part, filled=(), after=()):
    rows, wide = first.shape[2:]
    tall = min(64, rows)
    state = pl.BlockSpec((None, None, tall, wide), lambda i, m: (0, part, i, 0))
    ins = [(v, pl.BlockSpec((tall, v.shape[1]), lambda i, m: (i, 0))) for v in own + far + weight]
    ins += [(first, state), (second, state)]
    alias = {len(ins) + n: n for n in range(len(filled))}
    ins += [(v, ANYWHERE) for v in filled]
    return run(
        functools.partial(adam_kernel, join, [len(v) for v in (own, far, weight)]),
        name,
        (rows // tall,),
        meta,
        ins,
        [(first.shape, F32, state)] * 2
        + [((rows, wide), BF16, pl.BlockSpec((tall, wide), lambda i, m: (i, 0)))],
        (),
        after,
        alias,
    )


def outer_math(weight, change, momentum, average):
    velocity = OUTER_MOMENTUM * momentum + change
    master = weight - OUTER_RATE * (change + OUTER_MOMENTUM * velocity)
    trail = EMA_KEEP * average + (1.0 - EMA_KEEP) * master
    return velocity, trail, master


def outer_kernel(groups, meta, total, weight, momentum, average, *refs):
    change_out, velocity_out, trail_out, master_out, copy_out = refs[-5:]
    change = total[...].astype(F32) * (1.0 / groups)
    velocity, trail, master = outer_math(weight[...], change, momentum[...], average[...])
    change_out[...] = change
    velocity_out[...] = velocity
    trail_out[...] = trail
    master_out[...] = master
    copy_out[...] = master.astype(BF16)


def outer(name, meta, groups, total, weight, momentum, average, part, filled=(), after=()):
    tall, wide = min(64, weight.shape[1]), weight.shape[2]
    spec = pl.BlockSpec((tall, wide), lambda i, m: (i, 0))
    state = pl.BlockSpec((None, tall, wide), lambda i, m: (part, i, 0))
    ins = [(total, spec)] + [(v, state) for v in (weight, momentum, average)]
    alias = {len(ins) + n: n for n in range(len(filled))}
    return run(
        functools.partial(outer_kernel, groups),
        name,
        (weight.shape[1] // tall,),
        meta,
        ins + [(v, ANYWHERE) for v in filled],
        [(weight.shape, F32, state)] * 4 + [(weight.shape, BF16, state)],
        (),
        after,
        alias,
    )


def pause_kernel(meta, *refs):
    refs[-1][0] = 0


def pause(meta, *values, after=()):
    token = ((1,), jnp.int32, pl.BlockSpec(memory_space=pltpu.SMEM))
    out = run(
        pause_kernel, "pause", (1,), meta, [(v, ANYWHERE) for v in values],
        [(v.shape, v.dtype, ANYWHERE) for v in values] + [token], (), after, {n: n for n in range(len(values))},
    )
    line[:] = [out[-1]]
    return out[:-1]


def local(
    block_input,
    cotangent,
    lengths,
    weight_heads,
    weight_hidden,
    norm_gains,
    momentum_heads,
    momentum_hidden,
    momentum_gains,
    average_heads,
    average_hidden,
    average_gains,
    first_heads,
    first_hidden,
    first_gains,
    second_heads,
    second_hidden,
    second_gains,
):
    line.clear()
    groups, ranks = lax.axis_size("group"), lax.axis_size("tensor")
    group = lax.axis_index("group").astype(jnp.int32)
    shard = lax.axis_index("dp").astype(jnp.int32)
    rank = lax.axis_index("tensor").astype(jnp.int32)
    rows_here, width = block_input.shape
    total = rows_here * ranks
    strip = weight_heads.shape[0]
    half = width // 2
    heads = weight_heads.shape[1] // (4 * HEAD_DIM)
    units = weight_hidden.shape[2]
    quarter = units // 2
    items = lengths.shape[1]
    ends = jnp.cumsum(lengths[0]).astype(jnp.int32)
    meta = jnp.concatenate([ends, jnp.stack([rank, group, shard])])
    tall = math.gcd(rows_here, 64)
    steps = rows_here // tall
    order = range(groups)
    wait = functools.partial(pause, meta)
    whole = lambda a: pl.BlockSpec(a.shape, lambda *i: (0,) * a.ndim)
    both = pl.BlockSpec((2, width), lambda *i: (0, 0))
    row_block = pl.BlockSpec((tall, width), lambda i, m: (i, 0))
    row_shape = (rows_here, width)
    gain_block = pl.BlockSpec((8, width), lambda i, m: (0, 0))

    def near(value):
        return swap(value, "tensor", 1, ranks)

    def across(value):
        return swap(value, "dp", 1, 2)

    def gather_far(value):
        pieces = {0: value}
        bit = ranks // 2
        while bit > 1:
            pieces |= {k | bit: swap(v, "tensor", bit, ranks) for k, v in pieces.items()}
            bit //= 2
        return [pieces[k] for k in range(0, ranks, 2)]

    def ordered(even, odd):
        return [v for pair in zip(even, odd) for v in pair]

    gain_pieces = [norm_gains] + [swap(norm_gains, "group", k, groups) for k in order[1:]]
    strip_block = lambda w: pl.BlockSpec((strip // 2, w), lambda i, m: (i, 0))
    shards = run(
        cast_hidden_kernel, "cast_hidden", (2,), meta,
        [(weight_hidden, pl.BlockSpec((2, strip // 2, units), lambda i, m: (0, i, 0)))],
        [((strip, quarter), BF16, strip_block(quarter))] * 4,
    )
    gains, plain_gains = run(
        functools.partial(gains_kernel, items, half), "gains", (1,), meta,
        [(v, whole(v)) for v in gain_pieces],
        [((2, width), F32, both)] * 2,
        [pltpu.VMEM((groups, 2, width // groups), F32)],
    )
    column = lambda n: pl.BlockSpec((strip, n * HEAD_DIM), lambda h, m: (0, h))
    inward, outward = run(
        cast_heads_kernel, "cast_heads", (heads,), meta,
        [(weight_heads, column(4))],
        [((strip, heads * 3 * HEAD_DIM), BF16, column(3)), ((strip, heads * HEAD_DIM), BF16, column(1))],
    )
    strips = [inward] + [swap(inward, "group", k, groups) for k in order[1:]]
    crossed = [across(inward)]

    def along(value):
        return lax.all_gather(value, "group", axis=0, tiled=True)

    out_own = along(outward)
    lower_own = [along(v) for v in shards[2:]]
    raise_own = [along(v) for v in shards[:2]]

    def gather_near(even, copy):
        return [near(v) for v in even[1:]], near(copy)

    first_norm, copy = run(
        functools.partial(first_norm_kernel, items, half), "first_norm", (steps,), meta,
        [(block_input, row_block), (gains, both)],
        [(row_shape, BF16, row_block)] * 2,
    )
    even_one = gather_far(first_norm)
    wait()
    odd_first = near(wait(copy, after=crossed)[0])
    for k in order[1:]:
        wait()
        strips[k] = wait(strips[k], after=[odd_first] if k == 1 else [])[0]
        crossed.append(across(strips[k]))
    wait()
    even_one[1:] = wait(*even_one[1:], after=crossed[1:2])
    odd_one = [odd_first] + [near(v) for v in even_one[1:]]
    back_low, copy = run(
        functools.partial(turn_kernel, items, half), "turn", (steps,), meta,
        [(cotangent, row_block)], [(row_shape, BF16, row_block)] * 2,
    )
    even_back = gather_far(back_low)
    wait()
    out_own = wait(out_own, after=odd_one[1:] + crossed[2:3])[0]
    out_far = across(out_own)
    all_one = ordered(even_one, odd_one)
    rows_of = lambda off: [(lambda m, k=k: (m[items + 1] ^ k) * strip + off, 0) for k in order]
    inward_w = (strips + crossed, rows_of(0) + rows_of(half))

    def pair(own, far):
        parts, places, at = [], [], 0
        for a, b in zip(own, far):
            parts += [a, b]
            places += [(lambda m: 0, at), (lambda m: half, at)]
            at += a.shape[1]
        return parts, places

    triple, inward_own = rows_matmul(
        "qkv", meta, all_one, inward_w, store_rounded, [], [(BF16, same)], half
    )
    lower_own[0] = wait(lower_own[0])[0]
    lower_far = [across(lower_own[0])]
    mixed, logs = attend(meta, triple, items, rows_here, heads)
    lower_own[1], copy, *even_back[1:] = wait(lower_own[1], copy, *even_back[1:], after=[out_far])
    lower_far.append(across(lower_own[1]))
    odd_back = [near(copy)] + [near(v) for v in even_back[1:]]
    outward_w = pair([out_own], [out_far])

    def scatter(name, x, weight, after=()):
        far = near(term(name + "_far", meta, x, weight, width, rows_here, ranks, same)[0])
        wait(after=after)
        send, keep = term(name, meta, x, weight, width, rows_here, ranks, same, far)
        return finish_sum(send, keep, rows_here, ranks)

    keep, received = scatter("project", mixed, outward_w, odd_back)
    raise_own[0] = wait(raise_own[0])[0]
    raise_far = [across(raise_own[0])]
    lower_w = pair(lower_own, lower_far)
    all_back = ordered(even_back, odd_back)
    back_hidden = rows_matmul("back_hidden", meta, all_back, lower_w, store_rounded, [], [(BF16, same)])[0]
    raise_own[1] = wait(raise_own[1])[0]
    raise_far.append(across(raise_own[1]))
    raise_w = pair(raise_own, raise_far)
    middle, second_norm, copy = run(
        functools.partial(second_norm_kernel, items, half), "second_norm", (steps,), meta,
        [(block_input, row_block), (keep, row_block), (received, row_block), (gains, both)],
        [(row_shape, F32, row_block)] + [(row_shape, BF16, row_block)] * 2,
    )
    even_two = gather_far(second_norm)
    odd_first = near(copy)
    wait()
    wait(after=[odd_first])
    even_two[1:] = wait(*even_two[1:])
    odd_two = [odd_first] + [near(v) for v in even_two[1:]]
    wait()
    all_two = ordered(even_two, odd_two)

    hidden, back_before = rows_matmul(
        "raise", meta, all_two, raise_w, store_gelu, [(back_hidden, same)], [(BF16, same)] * 2
    )
    pieces = lambda values: [(v, k * rows_here) for k, v in enumerate(values)]

    def grad(name, left, right, first):
        return weight_grad(name, meta, pieces(left), [(right, 0, 0, total)], first, half, total)

    grad_lower_far = across(grad("lower_far", all_back, hidden, half))
    keep, received = scatter("back_second", back_before, raise_w)
    grad_raise_far = across(grad("raise_far", all_two, back_before, half))
    grad_lower = grad("lower_own", all_back, hidden, 0)
    grad_raise = grad("raise_own", all_two, back_before, 0)
    back_middle, gain_second, back_low_middle, copy = run(
        lambda meta, *refs: second_back_kernel(*refs), "second_back", (steps,), meta,
        [(v, row_block) for v in (middle, keep, received, back_low)] + [(gains, both)],
        [(row_shape, F32, row_block), ((8, width), F32, gain_block)] + [(row_shape, BF16, row_block)] * 2,
    )
    even_middle = gather_far(back_low_middle)
    odd_middle = [near(copy)]
    out_keep, out_received = scatter("lower", hidden, lower_w, odd_middle)

    def summed(delta):
        return lax.psum_scatter(delta, "group", scatter_dimension=0, tiled=True)

    moment_hidden, square_hidden, delta = adam(
        "adam_lower", meta, side_by_side, [grad_lower], [grad_lower_far], lower_own, first_hidden, second_hidden, 1
    )
    lower_delta = summed(delta)
    even_middle[1:] = wait(*even_middle[1:])
    odd_middle += [near(v) for v in even_middle[1:]]
    moment_hidden, square_hidden, delta = adam(
        "adam_raise", meta, side_by_side, [grad_raise], [grad_raise_far], raise_own, first_hidden, second_hidden, 0,
        (moment_hidden, square_hidden),
    )
    raise_delta = summed(delta)

    all_middle = ordered(even_middle, odd_middle)
    back_mixed = rows_matmul("back_mixed", meta, all_middle, outward_w, store_rounded, [], [(BF16, same)])[0]
    grad_out_far = across(grad("out_far", all_middle, mixed, half))
    back_triple = attend_back(meta, triple, mixed, back_mixed, logs, items, rows_here, heads)
    grad_in_far = across(grad("in_far", all_one, back_triple, half))
    keep, received = scatter("back_first", back_triple, inward_w)
    grad_in = grad("in_own", all_one, back_triple, 0)
    grad_out = grad("out_own", all_middle, mixed, 0)
    block_output = run(
        functools.partial(output_kernel, items, half), "output", (steps,), meta,
        [(v, row_block) for v in (middle, out_keep, out_received)],
        [(row_shape, BF16, row_block)],
    )[0]
    hidden_out = outer(
        "outer_lower", meta, groups, lower_delta, weight_hidden, momentum_hidden, average_hidden, 1
    )
    moment_heads, square_heads, delta = adam(
        "adam_heads", meta, by_head, [grad_in, grad_out], [grad_in_far, grad_out_far], [inward_own, out_own],
        first_heads[:, None], second_heads[:, None], 0,
    )
    heads_delta = summed(delta)
    input_grad, gain_first = run(
        functools.partial(first_back_kernel, items, half), "first_back", (steps,), meta,
        [(block_input, row_block), (gains, both)] + [(v, row_block) for v in (back_middle, keep, received)],
        [(row_shape, F32, row_block), ((8, width), F32, gain_block)],
    )
    gain_grad = run(
        functools.partial(gain_total_kernel, items, half), "gain_total", (1,), meta,
        [(v, whole(v)) for v in (gain_first, gain_second)],
        [((2, width), F32, both)],
    )[0]

    def added(value, other):
        wait()
        return run(
            add_kernel, "add", (1,), meta, [(value, whole(value)), (other, whole(other))],
            [(value.shape, F32, whole(value))],
        )[0]

    gain_grad = added(gain_grad, across(gain_grad))
    bit = 1
    while bit < ranks:
        gain_grad = added(gain_grad, swap(gain_grad, "tensor", bit, ranks))
        bit *= 2
    moment_gains, square_gains, delta_gains = adam_math(
        plain_gains, gain_grad, first_gains[0], second_gains[0], GAIN_RATE, 0.0
    )
    short = width // groups

    def gain_part(k):
        return lax.dynamic_slice_in_dim(delta_gains, (group ^ k) * short, short, 1)

    change_gains = gain_part(0)
    for k in order[1:]:
        change_gains = change_gains + swap(gain_part(k), "group", k, groups)
    change_gains = change_gains / groups
    velocity_gains, trail_gains, master_gains = outer_math(
        norm_gains, change_gains, momentum_gains, average_gains
    )
    change_hidden, velocity_hidden, trail_hidden, master_hidden, copy_hidden = outer(
        "outer_raise", meta, groups, raise_delta, weight_hidden, momentum_hidden, average_hidden, 0, hidden_out
    )
    change_heads, velocity_heads, trail_heads, master_heads, copy_heads = (
        v[0]
        for v in outer(
            "outer_heads", meta, groups, heads_delta, weight_heads[None], momentum_heads[None],
            average_heads[None], 0,
        )
    )
    return (
        block_output,
        input_grad,
        moment_heads[:, 0],
        moment_hidden,
        moment_gains[None],
        square_heads[:, 0],
        square_hidden,
        square_gains[None],
        change_heads,
        change_hidden,
        change_gains,
        velocity_heads,
        velocity_hidden,
        velocity_gains,
        trail_heads,
        trail_hidden,
        trail_gains,
        master_heads,
        master_hidden,
        master_gains,
        copy_heads,
        copy_hidden,
    )


def solution(mesh):
    rows = P(("group", "dp", "tensor"), None)
    heads, hidden, gains = P(("dp", "group"), "tensor"), P(None, ("dp", "group"), "tensor"), P(None, "group")
    states = (P("group", "dp", "tensor"), P("group", None, "dp", "tensor"), P("group", None, None))
    in_specs = (rows, rows, P(("group", "dp"), None)) + (heads, hidden, gains) * 3 + states * 2
    out_specs = (rows, rows) + states * 2 + (heads, hidden, gains) * 4 + (heads, hidden)
    return jax.shard_map(local, mesh=mesh, in_specs=in_specs, out_specs=out_specs, check_vma=False)
```

```python
import functools
import math

import jax
import jax.numpy as jnp
from jax import lax
from jax.experimental import pallas as pl
from jax.experimental.pallas import tpu as pltpu
from jax.sharding import PartitionSpec as P

HEAD_DIM = 128
STEP = 8

NORM_EPS = 1e-05
INNER_RATE = 0.02
GAIN_RATE = 0.5
BETA_ONE = 0.9
BETA_TWO = 0.95
ADAM_EPS = 1e-08
WEIGHT_DECAY = 0.1
OUTER_RATE = 0.7
OUTER_MOMENTUM = 0.9
EMA_KEEP = 0.5

BF16 = jnp.bfloat16
F32 = jnp.float32
SCALE = HEAD_DIM ** (-0.5)
LOG2E = math.log2(math.e)
SCALE_LOG2 = SCALE * LOG2E
NEGATIVE = -1e30


def swap(value, axis, bit, size):
    return lax.ppermute(value, axis, [(i, i ^ bit) for i in range(size)])


ANYWHERE = pl.BlockSpec(memory_space=pl.ANY)
LIMIT = 60 * 2**20
line = []


def run(kernel, name, grid, meta, ins, outs, scratch=(), after=(), alias=None):
    arrays = [a for a, _ in ins]
    extra = [a for a in line + list(after) if all(a is not b for b in arrays)]
    count, skip = len(ins), len(extra)

    def body(*refs):
        kernel(*refs[: 1 + count], *refs[1 + count + skip :])

    result = pl.pallas_call(
        body,
        grid_spec=pltpu.PrefetchScalarGridSpec(
            num_scalar_prefetch=1,
            grid=grid,
            in_specs=[s for _, s in ins] + [ANYWHERE] * skip,
            out_specs=[s for _, _, s in outs],
            scratch_shapes=list(scratch),
        ),
        out_shape=[jax.ShapeDtypeStruct(s, d) for s, d, _ in outs],
        input_output_aliases={1 + a: b for a, b in (alias or {}).items()},
        compiler_params=pltpu.CompilerParams(vmem_limit_bytes=LIMIT),
        cost_estimate=pl.CostEstimate(flops=10**12, bytes_accessed=1, transcendentals=0),
        name=name,
    )(meta, *arrays, *extra)
    line[:] = [result[0]]
    return result


def dot_last(left, right):
    return lax.dot_general(
        left, right, (((1,), (1,)), ((), ())), preferred_element_type=F32
    )


def dot_first(left, right):
    return lax.dot_general(
        left, right, (((0,), (0,)), ((), ())), preferred_element_type=F32
    )


def dot(left, right):
    return jnp.dot(left, right, preferred_element_type=F32)


def normalize(rows):
    mean = jnp.mean(rows, axis=-1, keepdims=True)
    centred = rows - mean
    var = jnp.mean(centred * centred, axis=-1, keepdims=True)
    inverse = lax.rsqrt(var + NORM_EPS)
    return centred * inverse, inverse


def normalize_back(back, normed, inverse, gain):
    scaled = back * gain
    first = jnp.mean(scaled, axis=-1, keepdims=True)
    second = jnp.mean(scaled * normed, axis=-1, keepdims=True)
    terms = (back * normed).reshape(-1, 8, back.shape[-1])
    return inverse * (scaled - first - normed * second), jnp.sum(terms, axis=0)


def gelu_parts(u):
    size = jnp.abs(u) * (0.5**0.5)
    t = 1.0 / (1.0 + 0.3275911 * size)
    poly = t * (
        0.254829592
        + t * (-0.284496736 + t * (1.421413741 + t * (-1.453152027 + t * 1.061405429)))
    )
    bell = jnp.exp(-0.5 * u * u)
    tail = 0.5 * poly * bell
    below = jnp.where(u >= 0.0, 1.0 - tail, tail)
    return below, bell * (1.0 / math.sqrt(2.0 * math.pi))


def item_start(places, meta, items):
    start = jnp.zeros_like(places)
    for k in range(items):
        start = jnp.where(places >= meta[k], meta[k], start)
    return start


def copy_in(meta, items, source, target, rows, step, total):
    for s in range(total // step):
        owner, offset = (s * step) // rows, (s * step) % rows
        local = pl.multiple_of((owner ^ meta[items]) * rows + offset, step)
        target[s * step : (s + 1) * step, :] = source[pl.ds(local, step), :]


def local_row(meta, items, chunk, rows, step):
    per = rows // step
    owner, offset = chunk // per, chunk % per
    return pl.multiple_of((owner ^ meta[items]) * rows + offset * step, step)


def head_columns(n, c):
    return slice((3 * n + c) * HEAD_DIM, (3 * n + c + 1) * HEAD_DIM)


def attend_kernel(items, rows, step, block, pairs, meta, qkv, *refs):
    mixed, logs, nat, values, acc, top = refs[-6:]
    total = qkv.shape[0]
    index = pl.program_id(0)

    @pl.when(index == 0)
    def _():
        copy_in(meta, items, qkv, nat, rows, step, total)
        for n in range(pairs):
            values[n, :, 0:HEAD_DIM] = nat[:, head_columns(n, 2)]
            values[n, :, HEAD_DIM:] = jnp.ones((total, HEAD_DIM), BF16)

    first_row = index * block
    here = pl.ds(pl.multiple_of(first_row, block), block)
    acc[...] = jnp.zeros_like(acc)
    top[...] = jnp.full_like(top, NEGATIVE)
    low_start = item_start(first_row, meta, items)
    high_start = item_start(first_row + block - 1, meta, items)

    def tile(j, masked):
        at = pl.ds(pl.multiple_of(j * block, block), block)
        if masked:
            q_place = first_row + lax.broadcasted_iota(jnp.int32, (block, 1), 0)
            k_place = j * block + lax.broadcasted_iota(jnp.int32, (1, block), 1)
            live = (k_place <= q_place) & (k_place >= item_start(q_place, meta, items))
        scores = [dot_last(nat[here, head_columns(n, 0)], nat[at, head_columns(n, 1)]) for n in range(pairs)]
        for n in range(pairs):
            s = jnp.where(live, scores[n], NEGATIVE) if masked else scores[n]
            old = top[n]
            new = jnp.maximum(old, jnp.max(s, axis=1, keepdims=True))
            p = jnp.exp2((s - jnp.concatenate([new] * (block // HEAD_DIM), axis=1)) * SCALE_LOG2)
            keep = jnp.exp2((old - new) * SCALE_LOG2)
            top[n] = new
            acc[n] = acc[n] * jnp.concatenate([keep, keep], axis=1) + dot(p.astype(BF16), values[n, at, :])

    @pl.loop(low_start // block, index)
    def _(j):
        whole = high_start <= j * block

        @pl.when(whole)
        def _():
            tile(j, False)

        @pl.when(jnp.logical_not(whole))
        def _():
            tile(j, True)

    tile(index, True)
    per = block // step
    for n in range(pairs):
        weight = acc[n, :, HEAD_DIM:]
        out = (acc[n, :, 0:HEAD_DIM] / weight).astype(BF16)
        for c in range(per):
            at = local_row(meta, items, index * per + c, rows, step)
            mixed[pl.ds(at, step), n * HEAD_DIM : (n + 1) * HEAD_DIM] = out[c * step : (c + 1) * step, :]
        log = top[n] * SCALE_LOG2 + jnp.log(weight) * LOG2E
        logs[n, 0] = log.T[0:8, :]


def attend(meta, qkv, items, rows, heads, pairs, call, filled=(), after=()):
    total = qkv.shape[0]
    block = min(512, total)
    step = math.gcd(rows, block)
    count = total // block
    return run(
        functools.partial(attend_kernel, items, rows, step, block, pairs),
        "attend",
        (count,),
        meta,
        [(qkv, pl.BlockSpec((total, pairs * 3 * HEAD_DIM), lambda i, m: (0, call)))]
        + [(v, ANYWHERE) for v in filled],
        [
            ((total, heads * HEAD_DIM), BF16, pl.BlockSpec((total, pairs * HEAD_DIM), lambda i, m: (0, call))),
            ((heads, count, 8, block), F32, pl.BlockSpec((pairs, 1, 8, block), lambda i, m: (call, i, 0, 0))),
        ],
        [
            pltpu.VMEM((total, pairs * 3 * HEAD_DIM), BF16),
            pltpu.VMEM((pairs, total, 2 * HEAD_DIM), BF16),
            pltpu.VMEM((pairs, block, 2 * HEAD_DIM), F32),
            pltpu.VMEM((pairs, block, HEAD_DIM), F32),
        ],
        after,
        {1 + n: n for n in range(len(filled))},
    )


def attend_back_kernel(
    items, rows, step, block, pairs, meta, qkv, mixed, back, logs, grads, nat, nat_mixed, nat_back, dq, dk, dv
):
    total = qkv.shape[0]
    index = pl.program_id(0)
    own = [slice(n * HEAD_DIM, (n + 1) * HEAD_DIM) for n in range(pairs)]

    @pl.when(index == 0)
    def _():
        copy_in(meta, items, qkv, nat, rows, step, total)
        copy_in(meta, items, mixed, nat_mixed, rows, step, total)
        copy_in(meta, items, back, nat_back, rows, step, total)
        dk[...] = jnp.zeros_like(dk)
        dv[...] = jnp.zeros_like(dv)

    first_row = index * block
    here = pl.ds(pl.multiple_of(first_row, block), block)
    row_terms = []
    for n in range(pairs):
        product = nat_back[here, own[n]].astype(F32) * nat_mixed[here, own[n]].astype(F32)
        row_terms.append(jnp.sum(product.T, axis=0, keepdims=True))
    dq[...] = jnp.zeros_like(dq)
    low_start = item_start(first_row, meta, items)
    high_start = item_start(first_row + block - 1, meta, items)

    def tile(j, masked):
        at = pl.ds(pl.multiple_of(j * block, block), block)
        if masked:
            k_place = j * block + lax.broadcasted_iota(jnp.int32, (block, 1), 0)
            q_place = first_row + lax.broadcasted_iota(jnp.int32, (1, block), 1)
            live = (k_place <= q_place) & (k_place >= item_start(q_place, meta, items))
        scores = [dot_last(nat[at, head_columns(n, 1)], nat[here, head_columns(n, 0)]) for n in range(pairs)]
        backs = [dot_last(nat[at, head_columns(n, 2)], nat_back[here, own[n]]) for n in range(pairs)]
        for n in range(pairs):
            p = jnp.exp2(scores[n] * SCALE_LOG2 - logs[n, 0, 0:1, :])
            if masked:
                p = jnp.where(live, p, 0.0)
            s = (p * (backs[n] - row_terms[n])).astype(BF16)
            dv[at, own[n]] += dot(p.astype(BF16), nat_back[here, own[n]])
            dk[at, own[n]] += dot(s, nat[here, head_columns(n, 0)])
            dq[:, own[n]] += dot_first(s, nat[at, head_columns(n, 1)])

    @pl.loop(low_start // block, index)
    def _(j):
        whole = high_start <= j * block

        @pl.when(whole)
        def _():
            tile(j, False)

        @pl.when(jnp.logical_not(whole))
        def _():
            tile(j, True)

    tile(index, True)
    per = block // step
    for n in range(pairs):
        out = (dq[:, own[n]] * SCALE).astype(BF16)
        for c in range(per):
            to = local_row(meta, items, index * per + c, rows, step)
            grads[pl.ds(to, step), head_columns(n, 0)] = out[c * step : (c + 1) * step, :]

    @pl.when(index == pl.num_programs(0) - 1)
    def _():
        for s in range(total // step):
            to = local_row(meta, items, s, rows, step)
            part = slice(s * step, (s + 1) * step)
            for n in range(pairs):
                grads[pl.ds(to, step), head_columns(n, 1)] = (dk[part, own[n]] * SCALE).astype(BF16)
                grads[pl.ds(to, step), head_columns(n, 2)] = dv[part, own[n]].astype(BF16)


def attend_back(meta, qkv, mixed, back, logs, items, rows, heads, pairs, call, after=()):
    total = qkv.shape[0]
    block = logs.shape[-1]
    step = math.gcd(rows, block)
    count = total // block
    wide = pl.BlockSpec((total, pairs * 3 * HEAD_DIM), lambda i, m: (0, call))
    narrow = pl.BlockSpec((total, pairs * HEAD_DIM), lambda i, m: (0, call))
    return run(
        functools.partial(attend_back_kernel, items, rows, step, block, pairs),
        "attend_back",
        (count,),
        meta,
        [
            (qkv, wide),
            (mixed, narrow),
            (back, narrow),
            (logs, pl.BlockSpec((pairs, 1, 8, block), lambda i, m: (call, i, 0, 0))),
        ],
        [((total, pairs * 3 * HEAD_DIM), BF16, pl.BlockSpec((total, pairs * 3 * HEAD_DIM), lambda i, m: (0, 0)))],
        [
            pltpu.VMEM((total, pairs * 3 * HEAD_DIM), BF16),
            pltpu.VMEM((total, pairs * HEAD_DIM), BF16),
            pltpu.VMEM((total, pairs * HEAD_DIM), BF16),
            pltpu.VMEM((block, pairs * HEAD_DIM), F32),
            pltpu.VMEM((total, pairs * HEAD_DIM), F32),
            pltpu.VMEM((total, pairs * HEAD_DIM), F32),
        ],
        after,
    )[0]


TILE = 512


def tile_of(size):
    return next(tile for tile in (min(TILE, size), 384, 256, 128) if size % tile == 0)


def part_of(array, row=lambda m: 0, column=0, source_row=0, rows=None, source_column=0, columns=None):
    rows, columns = rows or array.shape[0] - source_row, columns or array.shape[1] - source_column
    return array, (row, column, source_row, rows, source_column, columns)


class Pieces:
    def __init__(self, refs, places, dim, target, sems, meta):
        self.refs, self.places, self.dim, self.target, self.sems, self.meta = refs, places, dim, target, sems, meta
        self.tile = tile_of(target.shape[dim])

    def span(self, p):
        row, column, _, rows, _, columns = self.places[p]
        first, size = (column, columns) if self.dim else (row(None), rows)
        return first // self.tile, size // self.tile

    def copy(self, p, n):
        row, column, source_row, rows, source_column, columns = self.places[p]
        tile = self.tile
        at = (n - self.span(p)[0]) * tile + (source_column if self.dim else source_row)
        at = pl.ds(pl.multiple_of(at, math.gcd(tile, source_column if self.dim else source_row)), tile)
        to = pl.ds(pl.multiple_of(n * tile, tile), tile)
        if self.dim:
            source = self.refs[p].at[pl.ds(source_row, rows), at]
            target = self.target.at[pl.ds(pl.multiple_of(row(self.meta), math.gcd(rows, TILE)), rows), to]
        else:
            source = self.refs[p].at[at, pl.ds(source_column, columns)]
            target = self.target.at[to, pl.ds(column, columns)]
        return pltpu.make_async_copy(source, target, self.sems.at[p, n])

    def start(self):
        for n in range(self.target.shape[self.dim] // self.tile):
            for p in range(len(self.refs)):
                first, count = self.span(p)
                if first <= n < first + count:
                    self.copy(p, n).start()

    def wait(self, n):
        for p in range(len(self.refs)):
            first, count = self.span(p)
            if isinstance(n, int):
                if first <= n < first + count:
                    self.copy(p, n).wait()
            elif first == 0 and count == self.target.shape[self.dim] // self.tile:
                self.copy(p, n).wait()
            else:

                @pl.when((n >= first) & (n < first + count))
                def _(p=p):
                    self.copy(p, n).wait()


def tiles_of(size):
    return size // tile_of(size)


def rows_kernel(count, places, use, saved, finish, staged, filled, meta, *refs):
    parts = len(places)
    pieces, strips, refs = refs[:count], refs[count : count + parts], refs[count + parts :]
    stages = refs[len(refs) - staged :]
    refs = refs[: len(refs) - staged]
    blocks, (slots, weight, piece_sems, weight_sems) = refs[:-4], refs[-4:]
    i = pl.program_id(0)
    parts = Pieces(strips, places, 1, weight, weight_sems, meta)

    def fetch(n):
        return pltpu.make_async_copy(pieces[n], slots.at[n % 2], piece_sems.at[n % 2])

    @pl.when(i == 0)
    def _():
        fetch(0).start()
        parts.start()

    for n in range(1, count):

        @pl.when(i + 1 == n)
        def _(n=n):
            fetch(n).start()

    for n in range(count):

        @pl.when(i == n)
        def _(n=n):
            fetch(n).wait()

    wide = tile_of(use)
    many, loaded = use // wide, weight.shape[1] // parts.tile
    early = wide != parts.tile
    if early or staged:

        @pl.when(i == 0)
        def _():
            for n in range(loaded):
                parts.wait(n)

    if staged:
        blocks = blocks[: len(blocks) - 2 - saved - filled] + blocks[len(blocks) - 2 - saved :]
        x = slots[i % 2]
        for n in range(many + 1):
            if n < many:
                stages[n % 2][...] = dot(x, weight[:, n * wide : (n + 1) * wide])
            if n:
                finish(
                    stages[(n - 1) % 2][...], slice((n - 1) * wide, n * wide), *blocks[: len(blocks) - saved]
                )
    else:

        @pl.loop(0, many)
        def _(n):
            if not early:

                @pl.when(i == 0)
                def _():
                    parts.wait(n)

            at = pl.ds(pl.multiple_of(n * wide, wide), wide)
            finish(dot(slots[i % 2], weight[:, at]), at, *blocks[: len(blocks) - saved])

        if not early and loaded > many:

            @pl.when(i == 0)
            def _():
                for n in range(many, loaded):
                    parts.wait(n)

    if saved:
        kept = blocks[-1]
        kept[...] = weight[pl.ds(pl.multiple_of(i * kept.shape[0], kept.shape[0]), kept.shape[0]), :]


def rows_matmul(
    name, meta, pieces, weight, finish, extra, outs, use=None, rows=None, saved=False, staged=False, filled=(),
    after=()
):
    strips, places = zip(*weight)
    tall, depth = pieces[0].shape
    wide = max(place[1] + place[5] for place in places)
    use = use or wide
    count, parts = len(pieces), len(strips)
    block = lambda index: pl.BlockSpec((tall, use), lambda i, m: (index(i), 0))
    more = [((depth, wide), BF16, pl.BlockSpec((depth // count, wide), lambda i, m: (i, 0)))] if saved else []
    ins = [(p, ANYWHERE) for p in pieces] + [(p, ANYWHERE) for p in strips] + [(a, block(f)) for a, f in extra]
    return run(
        functools.partial(rows_kernel, count, places, use, saved, finish, 2 * staged, len(filled)),
        name,
        (count,),
        meta,
        ins + [(v, ANYWHERE) for v in filled],
        [((rows or count * tall, use), d, block(f)) for d, f in outs] + more,
        [
            pltpu.VMEM((2, tall, depth), BF16),
            pltpu.VMEM((depth, wide), BF16),
            pltpu.SemaphoreType.DMA((2,)),
            pltpu.SemaphoreType.DMA((parts, tiles_of(wide))),
        ]
        + [pltpu.VMEM((tall, tile_of(use)), F32)] * (2 * staged),
        after,
        {len(ins) + n: n for n in range(len(filled))},
    )


def store_rounded(value, at, out):
    out[:, at] = value.astype(BF16)


def store_gelu(value, at, back, hidden, back_before):
    below, density = gelu_parts(value)
    hidden[:, at] = (value * below).astype(BF16)
    back_before[:, at] = (back[:, at].astype(F32) * (below + value * density)).astype(BF16)


def same(i):
    return i


def term_kernel(count, places, offset, part, meta, *refs):
    x, strips, refs = refs[:count], refs[count : count + len(places)], refs[count + len(places) :]
    received = refs[0] if len(refs) == 11 else None
    out, held, extra, tiles, weight, x_sems, extra_sems, tile_sems, sems, _ = refs[-10:]
    i = pl.program_id(0)
    parts = Pieces(strips, places, 0, weight, sems, meta)
    wide = parts.tile
    many = weight.shape[0] // wide
    own_rows = pl.ds(pl.multiple_of((4 * i + offset) * part, part), part)
    out_rows = pl.ds(pl.multiple_of(i * part, part), part)

    def load_x(n):
        at = sum(v.shape[1] for v in x[:n])
        to = held.at[:, at : at + x[n].shape[1]]
        return pltpu.make_async_copy(x[n].at[own_rows, :], to, x_sems.at[n])

    def load_extra(n):
        at = pl.ds(pl.multiple_of(n * wide, wide), wide)
        return pltpu.make_async_copy(received.at[out_rows, at], extra.at[n], extra_sems.at[n])

    def put(n):
        at = pl.ds(pl.multiple_of(n * wide, wide), wide)
        return pltpu.make_async_copy(tiles.at[n % 2], out.at[out_rows, at], tile_sems.at[n % 2])

    for n in range(count):
        load_x(n).start()

    @pl.when(i == 0)
    def _():
        parts.start()

    if received is not None:
        for n in range(many):
            load_extra(n).start()
    for n in range(count):
        load_x(n).wait()

    @pl.loop(0, many)
    def _(n):
        @pl.when(i == 0)
        def _():
            parts.wait(n)

        if received is not None:
            load_extra(n).wait()

        @pl.when(n > 1)
        def _():
            put(n - 2).wait()

        at = pl.ds(pl.multiple_of(n * wide, wide), wide)
        value = dot_last(held[...], weight[at, :])
        if received is not None:
            value = value + extra[n].astype(F32)
        tiles[n % 2] = value.astype(BF16)
        put(n).start()

    for n in range(max(many - 2, 0), many):
        put(n).wait()


def term(name, meta, x, weight, part, ranks, offset, received=None, after=()):
    strips, places = zip(*weight)
    n = sum(v.shape[1] for v in x)
    width = max(place[0](None) + place[3] for place in places)
    many, wide = tiles_of(width), tile_of(width)
    rows = ranks // 4 * part
    return run(
        functools.partial(term_kernel, len(x), places, offset, part),
        name,
        (ranks // 4,),
        meta,
        [(v, ANYWHERE) for v in x]
        + [(s, ANYWHERE) for s in strips]
        + ([] if received is None else [(received, ANYWHERE)]),
        [((rows, width), BF16, ANYWHERE)],
        [
            pltpu.VMEM((part, n), BF16),
            pltpu.VMEM((many, part, wide), BF16),
            pltpu.VMEM((2, part, wide), BF16),
            pltpu.VMEM((width, n), BF16),
            pltpu.SemaphoreType.DMA((len(x),)),
            pltpu.SemaphoreType.DMA((many,)),
            pltpu.SemaphoreType.DMA((2,)),
            pltpu.SemaphoreType.DMA((len(strips), many)),
            pltpu.SMEM((1,), jnp.int32),
        ],
        after,
    )[0]


def finish_sum(send, keep, part, ranks):
    bit = 2
    while True:
        received = swap(send, "tensor", bit, ranks)
        if keep.shape[0] == part:
            return keep, received
        total = (keep.astype(F32) + received.astype(F32)).astype(BF16).reshape(-1, 2, part, keep.shape[1])
        keep, send = (total[:, n].reshape(-1, keep.shape[1]) for n in (0, 1))
        bit *= 2


def weight_grad_kernel(rows_a, first, meta, *refs):
    count = len(rows_a)
    left, (right, out, slots, held, left_sems, right_sems) = refs[:count], refs[count:]
    i = pl.program_id(0)
    steps = pl.num_programs(0)
    wide = slots.shape[2]
    parts = Pieces([right], [part_of(right)[1]], 1, held, right_sems, meta)
    tile = parts.tile

    def fetch(step, slot):
        at = pl.ds(pl.multiple_of(first + step * wide, wide), wide)
        return [
            pltpu.make_async_copy(ref.at[:, at], slots.at[slot, pl.ds(row, ref.shape[0])], left_sems.at[slot, n])
            for n, (ref, row) in enumerate(zip(left, rows_a))
        ]

    @pl.when(i == 0)
    def _():
        for copy in fetch(0, 0):
            copy.start()
        parts.start()

    @pl.when(i + 1 < steps)
    def _():
        for copy in fetch(i + 1, (i + 1) % 2):
            copy.start()

    for copy in fetch(i, i % 2):
        copy.wait()

    @pl.loop(0, held.shape[1] // tile)
    def _(n):
        @pl.when(i == 0)
        def _():
            parts.wait(n)

        at = pl.ds(pl.multiple_of(n * tile, tile), tile)
        out[:, at] = dot_first(slots[i % 2], held[:, at]).astype(BF16)


def weight_grad(name, meta, left, right, first, half, after=()):
    wide = min(512, half)
    total, n = right.shape
    return run(
        functools.partial(weight_grad_kernel, [r for _, r in left], first),
        name,
        (half // wide,),
        meta,
        [(a, ANYWHERE) for a, _ in left] + [(right, ANYWHERE)],
        [((half, n), BF16, pl.BlockSpec((wide, n), lambda i, m: (i, 0)))],
        [
            pltpu.VMEM((2, total, wide), BF16),
            pltpu.VMEM((total, n), BF16),
            pltpu.SemaphoreType.DMA((2, len(left))),
            pltpu.SemaphoreType.DMA((1, tiles_of(n))),
        ],
        after,
    )[0]


def strip_at(p, place, strip):
    return pl.ds(pl.multiple_of((p ^ place) * strip, strip), strip)


def turned(ref, place, strip):
    return jnp.concatenate([ref[:, strip_at(p, place, strip)] for p in range(ref.shape[1] // strip)], axis=1)


def store_turned(ref, value, place, strip):
    for p in range(value.shape[1] // strip):
        ref[:, strip_at(p, place, strip)] = value[:, p * strip : (p + 1) * strip].astype(ref.dtype)


def gains_kernel(items, strip, meta, *refs):
    pieces, (turned_out, plain, stack) = refs[:-3], refs[-3:]
    groups, short = len(pieces), pieces[0].shape[1]
    for k in range(groups):
        stack[k] = pieces[k][...]
    for j in range(groups):
        plain[:, j * short : (j + 1) * short] = stack[j ^ meta[items + 1]]
    turned_out[...] = turned(plain, meta[items + 2], strip)


def cast_heads_kernel(meta, weight, *outs):
    heads = weight.shape[1] // (4 * HEAD_DIM)
    for out in outs:
        for h in range(heads):
            at, near, far = 4 * h * HEAD_DIM, 3 * h * HEAD_DIM, (3 * heads + h) * HEAD_DIM
            out[:, near : near + 3 * HEAD_DIM] = weight[:, at : at + 3 * HEAD_DIM].astype(BF16)
            out[:, far : far + HEAD_DIM] = weight[:, at + 3 * HEAD_DIM : at + 4 * HEAD_DIM].astype(BF16)


def cast_hidden_kernel(meta, weight, *outs):
    for n, out in enumerate(outs):
        wide = out.shape[1]
        out[...] = weight[int(n < 2), :, n % 2 * wide : (n % 2 + 1) * wide].astype(BF16)


def first_norm_kernel(items, strip, meta, rows, gains, *outs):
    normed, _ = normalize(turned(rows, meta[items + 2], strip).astype(F32))
    for out in outs:
        out[...] = (normed * gains[0:1, :]).astype(BF16)


def turn_kernel(items, strip, meta, rows, *outs):
    for out in outs:
        out[...] = turned(rows, meta[items + 2], strip)


def add_kernel(meta, left, right, out):
    out[...] = left[...] + right[...]


def second_norm_kernel(items, strip, meta, rows, keep, received, gains, middle_out, *outs):
    middle = turned(rows, meta[items + 2], strip).astype(F32) + (
        keep[...].astype(F32) + received[...].astype(F32)
    )
    normed, _ = normalize(middle)
    middle_out[...] = middle
    for out in outs:
        out[...] = (normed * gains[1:2, :]).astype(BF16)


def second_back_kernel(middle, keep, received, back, gains, out, gain_out, *lows):
    normed, inverse = normalize(middle[...])
    given = keep[...].astype(F32) + received[...].astype(F32)
    grad, gain_part = normalize_back(given, normed, inverse, gains[1:2, :])
    grad = grad + back[...].astype(F32)
    out[...] = grad
    for low in lows:
        low[...] = grad.astype(BF16)

    @pl.when(pl.program_id(0) == 0)
    def _():
        gain_out[...] = jnp.zeros_like(gain_out)

    gain_out[...] += gain_part


def first_back_kernel(items, strip, meta, rows, gains, back, keep, received, out, gain_out):
    place = meta[items + 2]

    @pl.when(pl.program_id(0) == 0)
    def _():
        gain_out[...] = jnp.zeros_like(gain_out)

    normed, inverse = normalize(turned(rows, place, strip).astype(F32))
    given = keep[...].astype(F32) + received[...].astype(F32)
    grad, gain_part = normalize_back(given, normed, inverse, gains[0:1, :])
    gain_out[...] += gain_part
    store_turned(out, grad + back[...], place, strip)


def output_kernel(items, strip, meta, middle, keep, received, out):
    value = middle[...] + (keep[...].astype(F32) + received[...].astype(F32))
    store_turned(out, value, meta[items + 2], strip)


def gain_total_kernel(items, strip, meta, first, second, out):
    both = [jnp.sum(v, axis=0, keepdims=True) for v in (first[...], second[...])]
    store_turned(out, jnp.concatenate(both, axis=0), meta[items + 2], strip)


def adam_math(weight, grad, first, second, rate, decay):
    first = BETA_ONE * first + (1.0 - BETA_ONE) * grad
    second = BETA_TWO * second + (1.0 - BETA_TWO) * grad * grad
    scaled_first = first * (1.0 / (1.0 - BETA_ONE**STEP))
    scaled_second = second * (1.0 / (1.0 - BETA_TWO**STEP))
    update = scaled_first / (jnp.sqrt(scaled_second) + ADAM_EPS) + decay * weight
    return first, second, rate * update


def adam_kernel(join, counts, groups, per, items, meta, *refs):
    parts, at = [], 0
    for count in counts:
        parts.append(join([r[...].astype(F32) for r in refs[at : at + count]]))
        at += count
    own, far, weight = parts
    first, second = refs[at : at + 2]
    moment, square, *deltas = refs[-2 - groups :]
    moment[...], square[...], change = adam_math(
        weight, own + far, first[...], second[...], INNER_RATE, WEIGHT_DECAY
    )
    change = change.astype(BF16)
    if groups == 1:
        deltas[0][...] = change
    else:
        step = lax.rem(pl.program_id(0) // per + groups - meta[items + 1], groups)
        for k in range(groups):

            @pl.when(step == k)
            def _(k=k):
                deltas[k][...] = change


def side_by_side(parts):
    return parts[0] if len(parts) == 1 else jnp.concatenate(parts, axis=1)


def by_head(parts):
    *inward, outward = parts
    out, h = [], 0
    for part in inward:
        for n in range(part.shape[1] // (3 * HEAD_DIM)):
            out += [
                part[:, n * 3 * HEAD_DIM : (n + 1) * 3 * HEAD_DIM],
                outward[:, h * HEAD_DIM : (h + 1) * HEAD_DIM],
            ]
            h += 1
    return jnp.concatenate(out, axis=1)


def adam(name, meta, items, join, own, far, weight, first, second, part, groups=1, filled=(), after=()):
    rows, columns = first.shape[2:]
    tall = min(128, rows // groups)
    per = rows // groups // tall
    state = pl.BlockSpec((None, None, tall, columns), lambda i, m: (0, part, i, 0))

    def delta_block(k):
        def index(i, m):
            return (i if groups == 1 else jnp.clip(i - lax.rem(m[items + 1] + k, groups) * per, 0, per - 1), 0)

        return ((rows // groups, columns), BF16, pl.BlockSpec((tall, columns), index))

    ins = [
        (v, pl.BlockSpec((tall, wide), lambda i, m, at=at: (i, at))) for v, wide, at in own + far + weight
    ]
    ins += [(first, state), (second, state)]
    alias = {len(ins) + n: n for n in range(len(filled))}
    ins += [(v, ANYWHERE) for v in filled]
    return run(
        functools.partial(adam_kernel, join, [len(v) for v in (own, far, weight)], groups, per, items),
        name,
        (rows // tall,),
        meta,
        ins,
        [(first.shape, F32, state)] * 2 + [delta_block(k) for k in range(groups)],
        (),
        after,
        alias,
    )


def outer_math(weight, change, momentum, average):
    velocity = OUTER_MOMENTUM * momentum + change
    master = weight - OUTER_RATE * (change + OUTER_MOMENTUM * velocity)
    trail = EMA_KEEP * average + (1.0 - EMA_KEEP) * master
    return velocity, trail, master


def outer_kernel(groups, count, meta, *refs):
    totals, (weight, momentum, average) = refs[:count], refs[count : count + 3]
    change_out, velocity_out, trail_out, master_out, copy_out = refs[-5:]
    total = totals[0][...].astype(F32)
    for other in totals[1:]:
        total = total + other[...].astype(F32)
    change = total * (1.0 / groups)
    velocity, trail, master = outer_math(weight[...], change, momentum[...], average[...])
    change_out[...] = change
    velocity_out[...] = velocity
    trail_out[...] = trail
    master_out[...] = master
    copy_out[...] = master.astype(BF16)


def outer(name, meta, groups, totals, weight, momentum, average, part, filled=(), after=()):
    tall, wide = min(64, weight.shape[1]), weight.shape[2]
    spec = pl.BlockSpec((tall, wide), lambda i, m: (i, 0))
    state = pl.BlockSpec((None, tall, wide), lambda i, m: (part, i, 0))
    ins = [(v, spec) for v in totals] + [(v, state) for v in (weight, momentum, average)]
    alias = {len(ins) + n: n for n in range(len(filled))}
    return run(
        functools.partial(outer_kernel, groups, len(totals)),
        name,
        (weight.shape[1] // tall,),
        meta,
        ins + [(v, ANYWHERE) for v in filled],
        [(weight.shape, F32, state)] * 4 + [(weight.shape, BF16, state)],
        (),
        after,
        alias,
    )


def pause_kernel(meta, *refs):
    refs[-1][0] = 0


def pause(meta, *values, after=()):
    token = ((1,), jnp.int32, pl.BlockSpec(memory_space=pltpu.SMEM))
    out = run(
        pause_kernel, "pause", (1,), meta, [(v, ANYWHERE) for v in values],
        [(v.shape, v.dtype, ANYWHERE) for v in values] + [token], (), after, {n: n for n in range(len(values))},
    )
    line[:] = [out[-1]]
    return out[:-1]


def local(
    block_input,
    cotangent,
    lengths,
    weight_heads,
    weight_hidden,
    norm_gains,
    momentum_heads,
    momentum_hidden,
    momentum_gains,
    average_heads,
    average_hidden,
    average_gains,
    first_heads,
    first_hidden,
    first_gains,
    second_heads,
    second_hidden,
    second_gains,
):
    line.clear()
    groups, ranks = lax.axis_size("group"), lax.axis_size("tensor")
    group = lax.axis_index("group").astype(jnp.int32)
    shard = lax.axis_index("dp").astype(jnp.int32)
    rank = lax.axis_index("tensor").astype(jnp.int32)
    rows_here, width = block_input.shape
    total = rows_here * ranks
    strip = weight_heads.shape[0]
    half = width // 2
    heads = weight_heads.shape[1] // (4 * HEAD_DIM)
    units = weight_hidden.shape[2]
    items = lengths.shape[1]
    ends = jnp.cumsum(lengths[0]).astype(jnp.int32)
    meta = jnp.concatenate([ends, jnp.stack([rank, group, shard])])
    tall = math.gcd(rows_here, 160)
    steps = rows_here // tall
    wait = functools.partial(pause, meta)
    whole = lambda a: pl.BlockSpec(a.shape, lambda *i: (0,) * a.ndim)
    both = pl.BlockSpec((2, width), lambda *i: (0, 0))
    row_block = pl.BlockSpec((tall, width), lambda i, m: (i, 0))
    row_shape = (rows_here, width)
    gain_block = pl.BlockSpec((8, width), lambda i, m: (0, 0))

    def near(value):
        return swap(value, "tensor", 1, ranks)

    def across(value):
        return swap(value, "dp", 1, 2)

    def gather_far(value):
        pieces = {0: value}
        bit = ranks // 2
        while bit > 1:
            pieces |= {k | bit: swap(v, "tensor", bit, ranks) for k, v in pieces.items()}
            bit //= 2
        return [pieces[k] for k in range(0, ranks, 2)]

    def ordered(even, odd):
        return [v for pair in zip(even, odd) for v in pair]

    def gather_near(even, copy):
        return [near(copy)] + [near(v) for v in even[1:]]

    def scatter(name, x, weight):
        product = lambda n, received=None: term(
            f"{name}_{n}", meta, x, weight, rows_here, ranks, n, received
        )
        far_send = near(product(3))
        far_keep = near(product(1))
        send = product(2, far_send)
        keep = product(0, far_keep)
        return finish_sum(send, keep, rows_here, ranks)

    def along(value):
        return lax.ppermute(value, "group", [(i, (i + 1) % groups) for i in range(groups)])

    def row_parts(own, far):
        return [
            part_of(v, lambda m, k=k, at=at: lax.rem(m[items + 1] + groups - k, groups) * strip + at)
            for k, both_halves in enumerate(zip(own, far)) for at, v in zip((0, half), both_halves)
        ]

    gain_pieces = [norm_gains] + [swap(norm_gains, "group", k, groups) for k in range(1, groups)]
    tall_strip = pl.BlockSpec((strip // 2, heads * 4 * HEAD_DIM), lambda i, m: (i, 0))
    strips = list(run(
        cast_heads_kernel, "cast_heads", (2,), meta, [(weight_heads, tall_strip)],
        [((strip, heads * 4 * HEAD_DIM), BF16, tall_strip)],
    ))
    strips.append(along(strips[0]))
    crossed = [across(strips[0])]
    gains, plain_gains = run(
        functools.partial(gains_kernel, items, half), "gains", (1,), meta,
        [(v, whole(v)) for v in gain_pieces],
        [((2, width), F32, both)] * 2,
        [pltpu.VMEM((groups, 2, width // groups), F32)],
    )
    first_norm, copy = run(
        functools.partial(first_norm_kernel, items, half), "first_norm", (steps,), meta,
        [(block_input, row_block), (gains, both)],
        [(row_shape, BF16, row_block)] * 2,
    )
    even_one = gather_far(first_norm)
    quarter = units // 2
    strip_block = pl.BlockSpec((strip // 2, quarter), lambda i, m: (i, 0))
    shards = run(
        cast_hidden_kernel, "cast_hidden", (2,), meta,
        [(weight_hidden, pl.BlockSpec((2, strip // 2, units), lambda i, m: (0, i, 0)))],
        [((strip, quarter), BF16, strip_block)] * 4,
    )
    odd_first = near(wait(copy, after=crossed)[0])
    back_low, back_copy = run(
        functools.partial(turn_kernel, items, half), "turn", (steps,), meta,
        [(cotangent, row_block)], [(row_shape, BF16, row_block)] * 2,
    )
    strips[1] = wait(strips[1], after=[odd_first])[0]
    strips.append(along(strips[1]))
    crossed.append(across(strips[1]))
    wait()
    strips[2] = wait(strips[2], after=crossed[1:])[0]
    strips.append(along(strips[2]))
    crossed.append(across(strips[2]))
    wait()
    even_one[1:] = wait(*even_one[1:], after=crossed[2:])
    odd_one = [odd_first] + [near(v) for v in even_one[1:]]
    strips[3] = wait(strips[3])[0]
    crossed.append(across(strips[3]))
    def gathered(shard, after=()):
        return lax.all_gather(wait(shard, after=after)[0], "group", axis=0, tiled=True)

    def columns(own, far):
        return [
            part_of(v, lambda m, at=at: at, n * quarter)
            for n in range(2) for at, v in ((0, own[n]), (half, far[n]))
        ]

    lower_own = [gathered(shards[0], odd_one[1:])]
    back_low = wait(back_low)[0]
    even_back = gather_far(back_low)
    all_one = ordered(even_one, odd_one)
    triple, heads_all = rows_matmul(
        "qkv", meta, all_one, row_parts(strips, crossed), store_rounded, [], [(BF16, same)],
        use=heads * 3 * HEAD_DIM, saved=True,
    )
    inward_w = [part_of(heads_all, columns=heads * 3 * HEAD_DIM)]
    outward_w = [part_of(heads_all, source_column=heads * 3 * HEAD_DIM)]
    lower_own.append(gathered(shards[1]))
    lower_own[0] = wait(lower_own[0])[0]
    lower_far = [across(lower_own[0])]
    pairs = 2 if heads % 2 == 0 else 1
    calls = heads // pairs
    mixed, logs = attend(meta, triple, items, rows_here, heads, pairs, 0)
    raise_own = [gathered(shards[2])]
    for n in range(1, calls):
        mixed, logs = attend(meta, triple, items, rows_here, heads, pairs, n, (mixed, logs))
    lower_own[1] = wait(lower_own[1], after=lower_far)[0]
    lower_far.append(across(lower_own[1]))
    back_copy, *even_back[1:] = wait(back_copy, *even_back[1:])
    odd_back = gather_near(even_back, back_copy)
    raise_own.append(gathered(shards[3]))
    wait(after=odd_back)
    keep, received = scatter("project", [mixed], outward_w)
    raise_own[0] = wait(raise_own[0])[0]
    raise_far = [across(raise_own[0])]
    middle, second_norm = run(
        functools.partial(second_norm_kernel, items, half), "second_norm", (steps,), meta,
        [(block_input, row_block), (keep, row_block), (received, row_block), (gains, both)],
        [(row_shape, F32, row_block), (row_shape, BF16, row_block)],
    )
    even_two = gather_far(second_norm)
    odd_first = near(second_norm)
    raise_own[1] = wait(raise_own[1])[0]
    raise_far.append(across(raise_own[1]))
    raise_w = columns(raise_own, raise_far)
    all_back = ordered(even_back, odd_back)
    back_hidden, lower_all = rows_matmul(
        "back_hidden", meta, all_back, columns(lower_own, lower_far), store_rounded, [], [(BF16, same)], saved=True
    )
    lower_w = [part_of(lower_all)]
    wait(after=[odd_first])

    def feed(pieces, first, filled=()):
        return rows_matmul(
            "raise", meta, pieces, raise_w, store_gelu, [(back_hidden, lambda i: i + first)],
            [(BF16, lambda i: i + first)] * 2, rows=total, staged=True, filled=filled,
        )

    filled = feed([even_two[0], odd_first], 0)
    even_two[1:] = wait(*even_two[1:])
    odd_two = [odd_first] + [near(v) for v in even_two[1:]]
    wait()
    all_two = ordered(even_two, odd_two)
    hidden, back_before = feed(all_two[2:], 2, filled)
    pieces = lambda values: [(v, k * rows_here) for k, v in enumerate(values)]

    def grad(name, left, right, first):
        return weight_grad(name, meta, pieces(left), right, first, half)

    grad_lower_far = across(grad("lower_far", all_back, hidden, half))
    keep, received = scatter("back_second", [back_before], raise_w)
    grad_raise_far = across(grad("raise_far", all_two, back_before, half))
    grad_lower = grad("lower_own", all_back, hidden, 0)
    back_middle, gain_second, back_low_middle = run(
        lambda meta, *refs: second_back_kernel(*refs), "second_back", (steps,), meta,
        [(v, row_block) for v in (middle, keep, received, back_low)] + [(gains, both)],
        [(row_shape, F32, row_block), ((8, width), F32, gain_block), (row_shape, BF16, row_block)],
    )
    even_middle = gather_far(back_low_middle)
    odd_first = near(back_low_middle)
    grad_raise = grad("raise_own", all_two, back_before, 0)
    wait(after=[odd_first])
    out_keep, out_received = scatter("lower", [hidden], lower_w)

    def summed(delta):
        return lax.psum_scatter(delta, "group", scatter_dimension=0, tiled=True)

    def adam_hidden(name, own, far, weight, part, filled=()):
        moment, square, delta = adam(
            name, meta, items, side_by_side, [(own, units, 0)], [(far, units, 0)],
            [(v, v.shape[1], 0) for v in weight],
            first_hidden, second_hidden, part, filled=filled,
        )
        return moment, square, summed(delta)

    *states, lower_delta = adam_hidden("adam_lower", grad_lower, grad_lower_far, [lower_all], 1)
    even_middle[1:] = wait(*even_middle[1:])
    odd_middle = [odd_first] + [near(v) for v in even_middle[1:]]
    wait()

    all_middle = ordered(even_middle, odd_middle)
    back_mixed = rows_matmul("back_mixed", meta, all_middle, outward_w, store_rounded, [], [(BF16, same)])[0]
    grad_out_far = across(grad("out_far", all_middle, mixed, half))
    moment_hidden, square_hidden, raise_delta = adam_hidden(
        "adam_raise", grad_raise, grad_raise_far, raise_own, 0, tuple(states)
    )
    back_triples, grad_in_fars = [], []
    for n in range(calls):
        back_triples.append(
            attend_back(meta, triple, mixed, back_mixed, logs, items, rows_here, heads, pairs, n)
        )
        grad_in_fars.append(across(grad("in_far", all_one, back_triples[n], half)))
        if n == 0:
            grad_out = grad("out_own", all_middle, mixed, 0)
            block_output = run(
                functools.partial(output_kernel, items, half), "output", (steps,), meta,
                [(v, row_block) for v in (middle, out_keep, out_received)],
                [(row_shape, BF16, row_block)],
            )[0]
            hidden_out = outer(
                "outer_lower", meta, groups, [lower_delta], weight_hidden, momentum_hidden, average_hidden, 1
            )
    product = lambda n, received=None: term(
        f"back_first_{n}", meta, back_triples, inward_w, rows_here, ranks, n, received
    )
    far_send = near(product(3))
    far_keep = near(product(1))
    grad_ins = [grad("in_own", all_one, back_triples[0], 0)]
    send = product(2, far_send)
    grad_ins += [grad("in_own", all_one, v, 0) for v in back_triples[1:]]
    in_wide, out_wide = pairs * 3 * HEAD_DIM, heads * HEAD_DIM
    moment_heads, square_heads, *deltas = adam(
        "adam_heads", meta, items, by_head,
        [(v, in_wide, 0) for v in grad_ins] + [(grad_out, out_wide, 0)],
        [(v, in_wide, 0) for v in grad_in_fars] + [(grad_out_far, out_wide, 0)],
        [(heads_all, in_wide, n) for n in range(calls)] + [(heads_all, out_wide, 3)],
        first_heads[:, None], second_heads[:, None], 0, groups,
    )
    heads_deltas = [deltas[0]] + [
        lax.ppermute(deltas[k], "group", [(i, (i + k) % groups) for i in range(groups)])
        for k in range(1, groups)
    ]
    keep = product(0, far_keep)
    keep, received = finish_sum(send, keep, rows_here, ranks)
    input_grad, gain_first = run(
        functools.partial(first_back_kernel, items, half), "first_back", (steps,), meta,
        [(block_input, row_block), (gains, both)] + [(v, row_block) for v in (back_middle, keep, received)],
        [(row_shape, F32, row_block), ((8, width), F32, gain_block)],
    )
    gain_grad = run(
        functools.partial(gain_total_kernel, items, half), "gain_total", (1,), meta,
        [(v, whole(v)) for v in (gain_first, gain_second)],
        [((2, width), F32, both)],
    )[0]

    def added(value, other):
        return run(
            add_kernel, "add", (1,), meta, [(value, whole(value)), (other, whole(other))],
            [(value.shape, F32, whole(value))],
        )[0]

    far_gain = across(gain_grad)
    wait()
    gain_grad = added(gain_grad, far_gain)
    bit = 1
    while bit < ranks:
        far_gain = swap(gain_grad, "tensor", bit, ranks)
        wait()
        gain_grad = added(gain_grad, far_gain)
        bit *= 2
    moment_gains, square_gains, delta_gains = adam_math(
        plain_gains, gain_grad, first_gains[0], second_gains[0], GAIN_RATE, 0.0
    )
    short = width // groups

    def gain_part(k):
        return lax.dynamic_slice_in_dim(delta_gains, (group ^ k) * short, short, 1)

    change_gains = gain_part(0)
    for k in range(1, groups):
        change_gains = change_gains + swap(gain_part(k), "group", k, groups)
    change_gains = change_gains / groups
    velocity_gains, trail_gains, master_gains = outer_math(
        norm_gains, change_gains, momentum_gains, average_gains
    )
    change_hidden, velocity_hidden, trail_hidden, master_hidden, copy_hidden = outer(
        "outer_raise", meta, groups, [raise_delta], weight_hidden, momentum_hidden, average_hidden, 0,
        filled=hidden_out,
    )
    change_heads, velocity_heads, trail_heads, master_heads, copy_heads = (
        v[0]
        for v in outer(
            "outer_heads", meta, groups, heads_deltas, weight_heads[None], momentum_heads[None],
            average_heads[None], 0,
        )
    )
    return (
        block_output,
        input_grad,
        moment_heads[:, 0],
        moment_hidden,
        moment_gains[None],
        square_heads[:, 0],
        square_hidden,
        square_gains[None],
        change_heads,
        change_hidden,
        change_gains,
        velocity_heads,
        velocity_hidden,
        velocity_gains,
        trail_heads,
        trail_hidden,
        trail_gains,
        master_heads,
        master_hidden,
        master_gains,
        copy_heads,
        copy_hidden,
    )


def solution(mesh):
    rows = P(("group", "dp", "tensor"), None)
    heads, hidden, gains = P(("dp", "group"), "tensor"), P(None, ("dp", "group"), "tensor"), P(None, "group")
    states = (P("group", "dp", "tensor"), P("group", None, "dp", "tensor"), P("group", None, None))
    in_specs = (rows, rows, P(("group", "dp"), None)) + (heads, hidden, gains) * 3 + states * 2
    out_specs = (rows, rows) + states * 2 + (heads, hidden, gains) * 4 + (heads, hidden)
    return jax.shard_map(local, mesh=mesh, in_specs=in_specs, out_specs=out_specs, check_vma=False)
```

```python
import functools
import math

import jax
import jax.numpy as jnp
from jax import lax
from jax.experimental import pallas as pl
from jax.experimental.pallas import tpu as pltpu
from jax.sharding import PartitionSpec as P

HEAD_DIM = 128
STEP = 8

NORM_EPS = 1e-05
INNER_RATE = 0.02
GAIN_RATE = 0.5
BETA_ONE = 0.9
BETA_TWO = 0.95
ADAM_EPS = 1e-08
WEIGHT_DECAY = 0.1
OUTER_RATE = 0.7
OUTER_MOMENTUM = 0.9
EMA_KEEP = 0.5

BF16 = jnp.bfloat16
F32 = jnp.float32
SCALE = HEAD_DIM ** (-0.5)
LOG2E = math.log2(math.e)
SCALE_LOG2 = SCALE * LOG2E
NEGATIVE = -1e30


def swap(value, axis, bit, size):
    return lax.ppermute(value, axis, [(i, i ^ bit) for i in range(size)])


ANYWHERE = pl.BlockSpec(memory_space=pl.ANY)
LIMIT = 60 * 2**20
line = []


def run(kernel, name, grid, meta, ins, outs, scratch=(), after=(), alias=None):
    arrays = [a for a, _ in ins]
    extra = [a for a in line + list(after) if all(a is not b for b in arrays)]
    count, skip = len(ins), len(extra)

    def body(*refs):
        kernel(*refs[: 1 + count], *refs[1 + count + skip :])

    result = pl.pallas_call(
        body,
        grid_spec=pltpu.PrefetchScalarGridSpec(
            num_scalar_prefetch=1,
            grid=grid,
            in_specs=[s for _, s in ins] + [ANYWHERE] * skip,
            out_specs=[s for _, _, s in outs],
            scratch_shapes=list(scratch),
        ),
        out_shape=[jax.ShapeDtypeStruct(s, d) for s, d, _ in outs],
        input_output_aliases={1 + a: b for a, b in (alias or {}).items()},
        compiler_params=pltpu.CompilerParams(vmem_limit_bytes=LIMIT),
        cost_estimate=pl.CostEstimate(flops=10**12, bytes_accessed=1, transcendentals=0),
        name=name,
    )(meta, *arrays, *extra)
    line[:] = [result[0]]
    return result


def dot_last(left, right):
    return lax.dot_general(
        left, right, (((1,), (1,)), ((), ())), preferred_element_type=F32
    )


def dot_first(left, right):
    return lax.dot_general(
        left, right, (((0,), (0,)), ((), ())), preferred_element_type=F32
    )


def dot(left, right):
    return jnp.dot(left, right, preferred_element_type=F32)


def normalize(rows):
    mean = jnp.mean(rows, axis=-1, keepdims=True)
    centred = rows - mean
    var = jnp.mean(centred * centred, axis=-1, keepdims=True)
    inverse = lax.rsqrt(var + NORM_EPS)
    return centred * inverse, inverse


def normalize_back(back, normed, inverse, gain):
    scaled = back * gain
    first = jnp.mean(scaled, axis=-1, keepdims=True)
    second = jnp.mean(scaled * normed, axis=-1, keepdims=True)
    terms = (back * normed).reshape(-1, 8, back.shape[-1])
    return inverse * (scaled - first - normed * second), jnp.sum(terms, axis=0)


def gelu_parts(u):
    size = jnp.abs(u) * (0.5**0.5)
    t = 1.0 / (1.0 + 0.3275911 * size)
    poly = t * (
        0.254829592
        + t * (-0.284496736 + t * (1.421413741 + t * (-1.453152027 + t * 1.061405429)))
    )
    bell = jnp.exp(-0.5 * u * u)
    tail = 0.5 * poly * bell
    below = jnp.where(u >= 0.0, 1.0 - tail, tail)
    return below, bell * (1.0 / math.sqrt(2.0 * math.pi))


def item_start(places, meta, items):
    start = jnp.zeros_like(places)
    for k in range(items):
        start = jnp.where(places >= meta[k], meta[k], start)
    return start


def copy_in(meta, items, source, target, rows, step, total):
    for s in range(total // step):
        owner, offset = (s * step) // rows, (s * step) % rows
        local = pl.multiple_of((owner ^ meta[items]) * rows + offset, step)
        target[s * step : (s + 1) * step, :] = source[pl.ds(local, step), :]


def local_row(meta, items, chunk, rows, step):
    per = rows // step
    owner, offset = chunk // per, chunk % per
    return pl.multiple_of((owner ^ meta[items]) * rows + offset * step, step)


def head_columns(n, c):
    return slice((3 * n + c) * HEAD_DIM, (3 * n + c + 1) * HEAD_DIM)


def attend_kernel(items, rows, step, block, pairs, meta, qkv, *refs):
    mixed, logs, nat, values, acc, top = refs[-6:]
    total = qkv.shape[0]
    index = pl.program_id(0)

    @pl.when(index == 0)
    def _():
        copy_in(meta, items, qkv, nat, rows, step, total)
        for n in range(pairs):
            values[n, :, 0:HEAD_DIM] = nat[:, head_columns(n, 2)]
            values[n, :, HEAD_DIM:] = jnp.ones((total, HEAD_DIM), BF16)

    first_row = index * block
    acc[...] = jnp.zeros_like(acc)
    top[...] = jnp.full_like(top, NEGATIVE)
    low_start = item_start(first_row, meta, items)
    high_start = item_start(first_row + block - 1, meta, items)

    def tile(j, masked, keys=block, low=0, high=block):
        at = pl.ds(pl.multiple_of(j * block, block), keys)
        here = pl.ds(pl.multiple_of(first_row + low, math.gcd(block, low)), high - low)
        own = slice(low, high)
        if masked:
            q_place = first_row + low + lax.broadcasted_iota(jnp.int32, (high - low, 1), 0)
            k_place = j * block + lax.broadcasted_iota(jnp.int32, (1, keys), 1)
            live = (k_place <= q_place) & (k_place >= item_start(q_place, meta, items))
        scores = [dot_last(nat[here, head_columns(n, 0)], nat[at, head_columns(n, 1)]) for n in range(pairs)]
        for n in range(pairs):
            s = jnp.where(live, scores[n], NEGATIVE) if masked else scores[n]
            old = top[n, own, :]
            new = jnp.maximum(old, jnp.max(s, axis=1, keepdims=True))
            p = jnp.exp2((s - jnp.concatenate([new] * (keys // HEAD_DIM), axis=1)) * SCALE_LOG2)
            keep = jnp.exp2((old - new) * SCALE_LOG2)
            top[n, own, :] = new
            acc[n, own, :] = acc[n, own, :] * jnp.concatenate([keep, keep], axis=1) + dot(
                p.astype(BF16), values[n, at, :]
            )

    @pl.loop(low_start // block, index)
    def _(j):
        whole = high_start <= j * block

        @pl.when(whole)
        def _():
            tile(j, False)

        @pl.when(jnp.logical_not(whole))
        def _():
            tile(j, True)

    middle = block // 2
    tile(index, True, middle, 0, middle)
    tile(index, True, block, middle, block)
    per = block // step
    for n in range(pairs):
        weight = acc[n, :, HEAD_DIM:]
        out = (acc[n, :, 0:HEAD_DIM] / weight).astype(BF16)
        for c in range(per):
            at = local_row(meta, items, index * per + c, rows, step)
            mixed[pl.ds(at, step), n * HEAD_DIM : (n + 1) * HEAD_DIM] = out[c * step : (c + 1) * step, :]
        log = top[n] * SCALE_LOG2 + jnp.log(weight) * LOG2E
        logs[n, 0] = log.T[0:8, :]


def attend(meta, qkv, items, rows, heads, pairs, call, filled=(), after=()):
    total = qkv.shape[0]
    block = min(512, total)
    step = math.gcd(rows, block)
    count = total // block
    return run(
        functools.partial(attend_kernel, items, rows, step, block, pairs),
        "attend",
        (count,),
        meta,
        [(qkv, pl.BlockSpec((total, pairs * 3 * HEAD_DIM), lambda i, m: (0, call)))]
        + [(v, ANYWHERE) for v in filled],
        [
            ((total, heads * HEAD_DIM), BF16, pl.BlockSpec((total, pairs * HEAD_DIM), lambda i, m: (0, call))),
            ((heads, count, 8, block), F32, pl.BlockSpec((pairs, 1, 8, block), lambda i, m: (call, i, 0, 0))),
        ],
        [
            pltpu.VMEM((total, pairs * 3 * HEAD_DIM), BF16),
            pltpu.VMEM((pairs, total, 2 * HEAD_DIM), BF16),
            pltpu.VMEM((pairs, block, 2 * HEAD_DIM), F32),
            pltpu.VMEM((pairs, block, HEAD_DIM), F32),
        ],
        after,
        {1 + n: n for n in range(len(filled))},
    )


def attend_back_kernel(
    items, rows, step, block, pairs, meta, qkv, mixed, back, logs, grads, nat, nat_mixed, nat_back, dq, dk, dv
):
    total = qkv.shape[0]
    index = pl.program_id(0)
    own = [slice(n * HEAD_DIM, (n + 1) * HEAD_DIM) for n in range(pairs)]

    @pl.when(index == 0)
    def _():
        copy_in(meta, items, qkv, nat, rows, step, total)
        copy_in(meta, items, mixed, nat_mixed, rows, step, total)
        copy_in(meta, items, back, nat_back, rows, step, total)
        dk[...] = jnp.zeros_like(dk)
        dv[...] = jnp.zeros_like(dv)

    first_row = index * block
    here = pl.ds(pl.multiple_of(first_row, block), block)
    row_terms = []
    for n in range(pairs):
        product = nat_back[here, own[n]].astype(F32) * nat_mixed[here, own[n]].astype(F32)
        row_terms.append(jnp.sum(product.T, axis=0, keepdims=True))
    dq[...] = jnp.zeros_like(dq)
    low_start = item_start(first_row, meta, items)
    high_start = item_start(first_row + block - 1, meta, items)

    def tile(j, masked, low=0, high=block):
        at = pl.ds(pl.multiple_of(j * block + low, math.gcd(block, low)), high - low)
        here = pl.ds(pl.multiple_of(first_row + low, math.gcd(block, low)), block - low)
        mine = slice(low, block)
        if masked:
            k_place = j * block + low + lax.broadcasted_iota(jnp.int32, (high - low, 1), 0)
            q_place = first_row + mine.start + lax.broadcasted_iota(jnp.int32, (1, block - mine.start), 1)
            live = (k_place <= q_place) & (k_place >= item_start(q_place, meta, items))
        scores = [dot_last(nat[at, head_columns(n, 1)], nat[here, head_columns(n, 0)]) for n in range(pairs)]
        backs = [dot_last(nat[at, head_columns(n, 2)], nat_back[here, own[n]]) for n in range(pairs)]
        for n in range(pairs):
            p = jnp.exp2(scores[n] * SCALE_LOG2 - logs[n, 0, 0:1, mine])
            if masked:
                p = jnp.where(live, p, 0.0)
            s = (p * (backs[n] - row_terms[n][:, mine])).astype(BF16)
            dv[at, own[n]] += dot(p.astype(BF16), nat_back[here, own[n]])
            dk[at, own[n]] += dot(s, nat[here, head_columns(n, 0)])
            dq[mine, own[n]] += dot_first(s, nat[at, head_columns(n, 1)])

    @pl.loop(low_start // block, index)
    def _(j):
        whole = high_start <= j * block

        @pl.when(whole)
        def _():
            tile(j, False)

        @pl.when(jnp.logical_not(whole))
        def _():
            tile(j, True)

    middle = block // 2
    tile(index, True, 0, middle)
    tile(index, True, middle, block)
    per = block // step
    for n in range(pairs):
        out = (dq[:, own[n]] * SCALE).astype(BF16)
        for c in range(per):
            to = local_row(meta, items, index * per + c, rows, step)
            grads[pl.ds(to, step), head_columns(n, 0)] = out[c * step : (c + 1) * step, :]

    @pl.when(index == pl.num_programs(0) - 1)
    def _():
        for s in range(total // step):
            to = local_row(meta, items, s, rows, step)
            part = slice(s * step, (s + 1) * step)
            for n in range(pairs):
                grads[pl.ds(to, step), head_columns(n, 1)] = (dk[part, own[n]] * SCALE).astype(BF16)
                grads[pl.ds(to, step), head_columns(n, 2)] = dv[part, own[n]].astype(BF16)


def attend_back(meta, qkv, mixed, back, logs, items, rows, heads, pairs, call, after=()):
    total = qkv.shape[0]
    block = logs.shape[-1]
    step = math.gcd(rows, block)
    count = total // block
    wide = pl.BlockSpec((total, pairs * 3 * HEAD_DIM), lambda i, m: (0, call))
    narrow = pl.BlockSpec((total, pairs * HEAD_DIM), lambda i, m: (0, call))
    return run(
        functools.partial(attend_back_kernel, items, rows, step, block, pairs),
        "attend_back",
        (count,),
        meta,
        [
            (qkv, wide),
            (mixed, narrow),
            (back, narrow),
            (logs, pl.BlockSpec((pairs, 1, 8, block), lambda i, m: (call, i, 0, 0))),
        ],
        [((total, pairs * 3 * HEAD_DIM), BF16, pl.BlockSpec((total, pairs * 3 * HEAD_DIM), lambda i, m: (0, 0)))],
        [
            pltpu.VMEM((total, pairs * 3 * HEAD_DIM), BF16),
            pltpu.VMEM((total, pairs * HEAD_DIM), BF16),
            pltpu.VMEM((total, pairs * HEAD_DIM), BF16),
            pltpu.VMEM((block, pairs * HEAD_DIM), F32),
            pltpu.VMEM((total, pairs * HEAD_DIM), F32),
            pltpu.VMEM((total, pairs * HEAD_DIM), F32),
        ],
        after,
    )[0]


TILE = 512


def tile_of(size):
    return next(tile for tile in (min(TILE, size), 256, 128) if size % tile == 0)


def part_of(array, row=lambda m: 0, column=0, source_row=0, rows=None, source_column=0, columns=None):
    rows, columns = rows or array.shape[0] - source_row, columns or array.shape[1] - source_column
    return array, (row, column, source_row, rows, source_column, columns)


class Pieces:
    def __init__(self, refs, places, dim, target, sems, meta, tile=None):
        self.refs, self.places, self.dim, self.target, self.sems, self.meta = refs, places, dim, target, sems, meta
        self.tile = tile or tile_of(target.shape[dim])

    def span(self, p):
        row, column, _, rows, _, columns = self.places[p]
        first, size = (column, columns) if self.dim else (row(None), rows)
        return first // self.tile, size // self.tile

    def copy(self, p, n):
        row, column, source_row, rows, source_column, columns = self.places[p]
        tile = self.tile
        at = (n - self.span(p)[0]) * tile + (source_column if self.dim else source_row)
        at = pl.ds(pl.multiple_of(at, math.gcd(tile, source_column if self.dim else source_row)), tile)
        to = pl.ds(pl.multiple_of(n * tile, tile), tile)
        if self.dim:
            source = self.refs[p].at[pl.ds(source_row, rows), at]
            target = self.target.at[pl.ds(pl.multiple_of(row(self.meta), math.gcd(rows, TILE)), rows), to]
        else:
            source = self.refs[p].at[at, pl.ds(source_column, columns)]
            target = self.target.at[to, pl.ds(column, columns)]
        return pltpu.make_async_copy(source, target, self.sems.at[p, n])

    def start(self):
        for n in range(self.target.shape[self.dim] // self.tile):
            for p in range(len(self.refs)):
                first, count = self.span(p)
                if first <= n < first + count:
                    self.copy(p, n).start()

    def wait(self, n):
        for p in range(len(self.refs)):
            first, count = self.span(p)
            if isinstance(n, int):
                if first <= n < first + count:
                    self.copy(p, n).wait()
            elif first == 0 and count == self.target.shape[self.dim] // self.tile:
                self.copy(p, n).wait()
            else:

                @pl.when((n >= first) & (n < first + count))
                def _(p=p):
                    self.copy(p, n).wait()


def tiles_of(size):
    return size // tile_of(size)


def rows_kernel(count, places, use, saved, finish, staged, filled, meta, *refs):
    parts = len(places)
    pieces, strips, refs = refs[:count], refs[count : count + parts], refs[count + parts :]
    stages = refs[len(refs) - staged :]
    refs = refs[: len(refs) - staged]
    blocks, (slots, weight, piece_sems, weight_sems) = refs[:-4], refs[-4:]
    i = pl.program_id(0)
    parts = Pieces(strips, places, 1, weight, weight_sems, meta)

    def fetch(n):
        return pltpu.make_async_copy(pieces[n], slots.at[n % 2], piece_sems.at[n % 2])

    @pl.when(i == 0)
    def _():
        fetch(0).start()
        parts.start()

    for n in range(1, count):

        @pl.when(i + 1 == n)
        def _(n=n):
            fetch(n).start()

    for n in range(count):

        @pl.when(i == n)
        def _(n=n):
            fetch(n).wait()

    wide = tile_of(use)
    many, loaded = use // wide, weight.shape[1] // parts.tile
    early = wide != parts.tile
    if early or staged:

        @pl.when(i == 0)
        def _():
            for n in range(loaded):
                parts.wait(n)

    if staged:
        blocks = blocks[: len(blocks) - 2 - saved - filled] + blocks[len(blocks) - 2 - saved :]
        x = slots[i % 2]
        for n in range(many + 1):
            if n < many:
                stages[n % 2][...] = dot(x, weight[:, n * wide : (n + 1) * wide])
            if n:
                finish(
                    stages[(n - 1) % 2][...], slice((n - 1) * wide, n * wide), *blocks[: len(blocks) - saved]
                )
    else:

        @pl.loop(0, many)
        def _(n):
            if not early:

                @pl.when(i == 0)
                def _():
                    parts.wait(n)

            at = pl.ds(pl.multiple_of(n * wide, wide), wide)
            finish(dot(slots[i % 2], weight[:, at]), at, *blocks[: len(blocks) - saved])

        if not early and loaded > many:

            @pl.when(i == 0)
            def _():
                for n in range(many, loaded):
                    parts.wait(n)

    if saved:
        kept = blocks[-1]
        kept[...] = weight[pl.ds(pl.multiple_of(i * kept.shape[0], kept.shape[0]), kept.shape[0]), :]


def rows_matmul(
    name, meta, pieces, weight, finish, extra, outs, use=None, rows=None, saved=False, staged=False, filled=(),
    after=()
):
    strips, places = zip(*weight)
    tall, depth = pieces[0].shape
    wide = max(place[1] + place[5] for place in places)
    use = use or wide
    count, parts = len(pieces), len(strips)
    block = lambda index: pl.BlockSpec((tall, use), lambda i, m: (index(i), 0))
    more = [((depth, wide), BF16, pl.BlockSpec((depth // count, wide), lambda i, m: (i, 0)))] if saved else []
    ins = [(p, ANYWHERE) for p in pieces] + [(p, ANYWHERE) for p in strips] + [(a, block(f)) for a, f in extra]
    return run(
        functools.partial(rows_kernel, count, places, use, saved, finish, 2 * staged, len(filled)),
        name,
        (count,),
        meta,
        ins + [(v, ANYWHERE) for v in filled],
        [((rows or count * tall, use), d, block(f)) for d, f in outs] + more,
        [
            pltpu.VMEM((2, tall, depth), BF16),
            pltpu.VMEM((depth, wide), BF16),
            pltpu.SemaphoreType.DMA((2,)),
            pltpu.SemaphoreType.DMA((parts, tiles_of(wide))),
        ]
        + [pltpu.VMEM((tall, tile_of(use)), F32)] * (2 * staged),
        after,
        {len(ins) + n: n for n in range(len(filled))},
    )


def store_rounded(value, at, out):
    out[:, at] = value.astype(BF16)


def store_gelu(value, at, back, hidden, back_before):
    below, density = gelu_parts(value)
    hidden[:, at] = (value * below).astype(BF16)
    back_before[:, at] = (back[:, at].astype(F32) * (below + value * density)).astype(BF16)


def same(i):
    return i


def term_kernel(count, places, offset, part, meta, *refs):
    x, strips, refs = refs[:count], refs[count : count + len(places)], refs[count + len(places) :]
    received = refs[0] if len(refs) == 11 else None
    out, held, extra, tiles, weight, x_sems, extra_sems, tile_sems, sems, _ = refs[-10:]
    i = pl.program_id(0)
    parts = Pieces(strips, places, 0, weight, sems, meta)
    wide = parts.tile
    many = weight.shape[0] // wide
    own_rows = pl.ds(pl.multiple_of((4 * i + offset) * part, part), part)
    out_rows = pl.ds(pl.multiple_of(i * part, part), part)

    def load_x(n):
        at = sum(v.shape[1] for v in x[:n])
        to = held.at[:, at : at + x[n].shape[1]]
        return pltpu.make_async_copy(x[n].at[own_rows, :], to, x_sems.at[n])

    def load_extra(n):
        at = pl.ds(pl.multiple_of(n * wide, wide), wide)
        return pltpu.make_async_copy(received.at[out_rows, at], extra.at[n], extra_sems.at[n])

    def put(n):
        at = pl.ds(pl.multiple_of(n * wide, wide), wide)
        return pltpu.make_async_copy(tiles.at[n % 2], out.at[out_rows, at], tile_sems.at[n % 2])

    for n in range(count):
        load_x(n).start()

    @pl.when(i == 0)
    def _():
        parts.start()

    if received is not None:
        for n in range(many):
            load_extra(n).start()
    for n in range(count):
        load_x(n).wait()

    @pl.loop(0, many)
    def _(n):
        @pl.when(i == 0)
        def _():
            parts.wait(n)

        if received is not None:
            load_extra(n).wait()

        @pl.when(n > 1)
        def _():
            put(n - 2).wait()

        at = pl.ds(pl.multiple_of(n * wide, wide), wide)
        value = dot_last(held[...], weight[at, :])
        if received is not None:
            value = value + extra[n].astype(F32)
        tiles[n % 2] = value.astype(BF16)
        put(n).start()

    for n in range(max(many - 2, 0), many):
        put(n).wait()


def term(name, meta, x, weight, part, ranks, offset, received=None, after=()):
    strips, places = zip(*weight)
    n = sum(v.shape[1] for v in x)
    width = max(place[0](None) + place[3] for place in places)
    many, wide = tiles_of(width), tile_of(width)
    rows = ranks // 4 * part
    return run(
        functools.partial(term_kernel, len(x), places, offset, part),
        name,
        (ranks // 4,),
        meta,
        [(v, ANYWHERE) for v in x]
        + [(s, ANYWHERE) for s in strips]
        + ([] if received is None else [(received, ANYWHERE)]),
        [((rows, width), BF16, ANYWHERE)],
        [
            pltpu.VMEM((part, n), BF16),
            pltpu.VMEM((many, part, wide), BF16),
            pltpu.VMEM((2, part, wide), BF16),
            pltpu.VMEM((width, n), BF16),
            pltpu.SemaphoreType.DMA((len(x),)),
            pltpu.SemaphoreType.DMA((many,)),
            pltpu.SemaphoreType.DMA((2,)),
            pltpu.SemaphoreType.DMA((len(strips), many)),
            pltpu.SMEM((1,), jnp.int32),
        ],
        after,
    )[0]


def finish_sum(send, keep, part, ranks):
    bit = 2
    while True:
        received = swap(send, "tensor", bit, ranks)
        if keep.shape[0] == part:
            return keep, received
        total = (keep.astype(F32) + received.astype(F32)).astype(BF16).reshape(-1, 2, part, keep.shape[1])
        keep, send = (total[:, n].reshape(-1, keep.shape[1]) for n in (0, 1))
        bit *= 2


def weight_grad_kernel(rows_a, columns, first, meta, *refs):
    count, many = len(rows_a), len(columns)
    left, right, (out, slots, held, left_sems, right_sems) = (
        refs[:count], refs[count : count + many], refs[count + many :]
    )
    i = pl.program_id(0)
    steps = pl.num_programs(0)
    wide = slots.shape[2]
    places = [part_of(v, column=at)[1] for v, at in zip(right, columns)]
    loads = tile_of(right[0].shape[1])
    parts = Pieces(right, places, 1, held, right_sems, meta, loads)
    tile = tile_of(held.shape[1])

    def fetch(step, slot):
        at = pl.ds(pl.multiple_of(first + step * wide, wide), wide)
        return [
            pltpu.make_async_copy(ref.at[:, at], slots.at[slot, pl.ds(row, ref.shape[0])], left_sems.at[slot, n])
            for n, (ref, row) in enumerate(zip(left, rows_a))
        ]

    @pl.when(i == 0)
    def _():
        for copy in fetch(0, 0):
            copy.start()
        parts.start()

    @pl.when(i + 1 < steps)
    def _():
        for copy in fetch(i + 1, (i + 1) % 2):
            copy.start()

    for copy in fetch(i, i % 2):
        copy.wait()

    @pl.loop(0, held.shape[1] // tile)
    def _(n):
        @pl.when(i == 0)
        def _():
            for m in range(tile // loads):
                parts.wait(n * (tile // loads) + m)

        at = pl.ds(pl.multiple_of(n * tile, tile), tile)
        out[:, at] = dot_first(slots[i % 2], held[:, at]).astype(BF16)


def weight_grad(name, meta, left, right, first, half, after=()):
    wide = min(512, half)
    columns, n = [], 0
    for v in right:
        columns.append(n)
        n += v.shape[1]
    total = right[0].shape[0]
    return run(
        functools.partial(weight_grad_kernel, [r for _, r in left], columns, first),
        name,
        (half // wide,),
        meta,
        [(a, ANYWHERE) for a, _ in left] + [(v, ANYWHERE) for v in right],
        [((half, n), BF16, pl.BlockSpec((wide, n), lambda i, m: (i, 0)))],
        [
            pltpu.VMEM((2, total, wide), BF16),
            pltpu.VMEM((total, n), BF16),
            pltpu.SemaphoreType.DMA((2, len(left))),
            pltpu.SemaphoreType.DMA((len(right), n // tile_of(right[0].shape[1]))),
        ],
        after,
    )[0]


def strip_at(p, place, strip):
    return pl.ds(pl.multiple_of((p ^ place) * strip, strip), strip)


def turned(ref, place, strip):
    return jnp.concatenate([ref[:, strip_at(p, place, strip)] for p in range(ref.shape[1] // strip)], axis=1)


def store_turned(ref, value, place, strip):
    for p in range(value.shape[1] // strip):
        ref[:, strip_at(p, place, strip)] = value[:, p * strip : (p + 1) * strip].astype(ref.dtype)


def gains_kernel(items, strip, meta, *refs):
    pieces, (turned_out, plain, stack) = refs[:-3], refs[-3:]
    groups, short = len(pieces), pieces[0].shape[1]
    for k in range(groups):
        stack[k] = pieces[k][...]
    for j in range(groups):
        plain[:, j * short : (j + 1) * short] = stack[j ^ meta[items + 1]]
    turned_out[...] = turned(plain, meta[items + 2], strip)


def cast_heads_kernel(meta, weight, *outs):
    heads = weight.shape[1] // (4 * HEAD_DIM)
    for out in outs:
        for h in range(heads):
            at, near, far = 4 * h * HEAD_DIM, 3 * h * HEAD_DIM, (3 * heads + h) * HEAD_DIM
            out[:, near : near + 3 * HEAD_DIM] = weight[:, at : at + 3 * HEAD_DIM].astype(BF16)
            out[:, far : far + HEAD_DIM] = weight[:, at + 3 * HEAD_DIM : at + 4 * HEAD_DIM].astype(BF16)


def cast_hidden_kernel(meta, weight, *outs):
    for n, out in enumerate(outs):
        wide = out.shape[1]
        out[...] = weight[int(n < 2), :, n % 2 * wide : (n % 2 + 1) * wide].astype(BF16)


def first_norm_kernel(items, strip, meta, rows, gains, *outs):
    normed, _ = normalize(turned(rows, meta[items + 2], strip).astype(F32))
    for out in outs:
        out[...] = (normed * gains[0:1, :]).astype(BF16)


def turn_kernel(items, strip, meta, rows, *outs):
    for out in outs:
        out[...] = turned(rows, meta[items + 2], strip)


def add_kernel(meta, left, right, out):
    out[...] = left[...] + right[...]


def second_norm_kernel(items, strip, meta, rows, keep, received, gains, middle_out, *outs):
    middle = turned(rows, meta[items + 2], strip).astype(F32) + (
        keep[...].astype(F32) + received[...].astype(F32)
    )
    normed, _ = normalize(middle)
    middle_out[...] = middle
    for out in outs:
        out[...] = (normed * gains[1:2, :]).astype(BF16)


def second_back_kernel(middle, keep, received, back, gains, out, gain_out, *lows):
    normed, inverse = normalize(middle[...])
    given = keep[...].astype(F32) + received[...].astype(F32)
    grad, gain_part = normalize_back(given, normed, inverse, gains[1:2, :])
    grad = grad + back[...].astype(F32)
    out[...] = grad
    for low in lows:
        low[...] = grad.astype(BF16)

    @pl.when(pl.program_id(0) == 0)
    def _():
        gain_out[...] = jnp.zeros_like(gain_out)

    gain_out[...] += gain_part


def first_back_kernel(items, strip, meta, rows, gains, back, keep, received, out, gain_out):
    place = meta[items + 2]

    @pl.when(pl.program_id(0) == 0)
    def _():
        gain_out[...] = jnp.zeros_like(gain_out)

    normed, inverse = normalize(turned(rows, place, strip).astype(F32))
    given = keep[...].astype(F32) + received[...].astype(F32)
    grad, gain_part = normalize_back(given, normed, inverse, gains[0:1, :])
    gain_out[...] += gain_part
    store_turned(out, grad + back[...], place, strip)


def output_kernel(items, strip, meta, middle, keep, received, out):
    value = middle[...] + (keep[...].astype(F32) + received[...].astype(F32))
    store_turned(out, value, meta[items + 2], strip)


def gain_total_kernel(items, strip, meta, first, second, out):
    both = [jnp.sum(v, axis=0, keepdims=True) for v in (first[...], second[...])]
    store_turned(out, jnp.concatenate(both, axis=0), meta[items + 2], strip)


def adam_math(weight, grad, first, second, rate, decay):
    first = BETA_ONE * first + (1.0 - BETA_ONE) * grad
    second = BETA_TWO * second + (1.0 - BETA_TWO) * grad * grad
    scaled_first = first * (1.0 / (1.0 - BETA_ONE**STEP))
    scaled_second = second * (1.0 / (1.0 - BETA_TWO**STEP))
    update = scaled_first / (jnp.sqrt(scaled_second) + ADAM_EPS) + decay * weight
    return first, second, rate * update


def adam_kernel(join, counts, groups, per, items, meta, *refs):
    parts, at = [], 0
    for count in counts:
        parts.append(join([r[...].astype(F32) for r in refs[at : at + count]]))
        at += count
    own, far, weight = parts
    first, second = refs[at : at + 2]
    moment, square, *deltas = refs[-2 - groups :]
    moment[...], square[...], change = adam_math(
        weight, own + far, first[...], second[...], INNER_RATE, WEIGHT_DECAY
    )
    change = change.astype(BF16)
    if groups == 1:
        deltas[0][...] = change
    else:
        step = lax.rem(pl.program_id(0) // per + groups - meta[items + 1], groups)
        for k in range(groups):

            @pl.when(step == k)
            def _(k=k):
                deltas[k][...] = change


def side_by_side(parts):
    return parts[0] if len(parts) == 1 else jnp.concatenate(parts, axis=1)


def by_head(parts):
    *inward, outward = parts
    out, h = [], 0
    for part in inward:
        for n in range(part.shape[1] // (3 * HEAD_DIM)):
            out += [
                part[:, n * 3 * HEAD_DIM : (n + 1) * 3 * HEAD_DIM],
                outward[:, h * HEAD_DIM : (h + 1) * HEAD_DIM],
            ]
            h += 1
    return jnp.concatenate(out, axis=1)


def adam(name, meta, items, join, own, far, weight, first, second, part, groups=1, filled=(), after=()):
    rows, columns = first.shape[2:]
    tall = min(128, rows // groups)
    per = rows // groups // tall
    state = pl.BlockSpec((None, None, tall, columns), lambda i, m: (0, part, i, 0))

    def delta_block(k):
        def index(i, m):
            return (i if groups == 1 else jnp.clip(i - lax.rem(m[items + 1] + k, groups) * per, 0, per - 1), 0)

        return ((rows // groups, columns), BF16, pl.BlockSpec((tall, columns), index))

    ins = [
        (v, pl.BlockSpec((tall, wide), lambda i, m, at=at: (i, at))) for v, wide, at in own + far + weight
    ]
    ins += [(first, state), (second, state)]
    alias = {len(ins) + n: n for n in range(len(filled))}
    ins += [(v, ANYWHERE) for v in filled]
    return run(
        functools.partial(adam_kernel, join, [len(v) for v in (own, far, weight)], groups, per, items),
        name,
        (rows // tall,),
        meta,
        ins,
        [(first.shape, F32, state)] * 2 + [delta_block(k) for k in range(groups)],
        (),
        after,
        alias,
    )


def outer_math(weight, change, momentum, average):
    velocity = OUTER_MOMENTUM * momentum + change
    master = weight - OUTER_RATE * (change + OUTER_MOMENTUM * velocity)
    trail = EMA_KEEP * average + (1.0 - EMA_KEEP) * master
    return velocity, trail, master


def outer_kernel(groups, count, meta, *refs):
    totals, (weight, momentum, average) = refs[:count], refs[count : count + 3]
    change_out, velocity_out, trail_out, master_out, copy_out = refs[-5:]
    total = totals[0][...].astype(F32)
    for other in totals[1:]:
        total = total + other[...].astype(F32)
    change = total * (1.0 / groups)
    velocity, trail, master = outer_math(weight[...], change, momentum[...], average[...])
    change_out[...] = change
    velocity_out[...] = velocity
    trail_out[...] = trail
    master_out[...] = master
    copy_out[...] = master.astype(BF16)


def outer(name, meta, groups, totals, weight, momentum, average, part, filled=(), after=()):
    tall, wide = min(64, weight.shape[1]), weight.shape[2]
    spec = pl.BlockSpec((tall, wide), lambda i, m: (i, 0))
    state = pl.BlockSpec((None, tall, wide), lambda i, m: (part, i, 0))
    ins = [(v, spec) for v in totals] + [(v, state) for v in (weight, momentum, average)]
    alias = {len(ins) + n: n for n in range(len(filled))}
    return run(
        functools.partial(outer_kernel, groups, len(totals)),
        name,
        (weight.shape[1] // tall,),
        meta,
        ins + [(v, ANYWHERE) for v in filled],
        [(weight.shape, F32, state)] * 4 + [(weight.shape, BF16, state)],
        (),
        after,
        alias,
    )


def pause_kernel(meta, *refs):
    refs[-1][0] = 0


def pause(meta, *values, after=()):
    token = ((1,), jnp.int32, pl.BlockSpec(memory_space=pltpu.SMEM))
    out = run(
        pause_kernel, "pause", (1,), meta, [(v, ANYWHERE) for v in values],
        [(v.shape, v.dtype, ANYWHERE) for v in values] + [token], (), after, {n: n for n in range(len(values))},
    )
    line[:] = [out[-1]]
    return out[:-1]


def local(
    block_input,
    cotangent,
    lengths,
    weight_heads,
    weight_hidden,
    norm_gains,
    momentum_heads,
    momentum_hidden,
    momentum_gains,
    average_heads,
    average_hidden,
    average_gains,
    first_heads,
    first_hidden,
    first_gains,
    second_heads,
    second_hidden,
    second_gains,
):
    line.clear()
    groups, ranks = lax.axis_size("group"), lax.axis_size("tensor")
    group = lax.axis_index("group").astype(jnp.int32)
    shard = lax.axis_index("dp").astype(jnp.int32)
    rank = lax.axis_index("tensor").astype(jnp.int32)
    rows_here, width = block_input.shape
    total = rows_here * ranks
    strip = weight_heads.shape[0]
    half = width // 2
    heads = weight_heads.shape[1] // (4 * HEAD_DIM)
    units = weight_hidden.shape[2]
    items = lengths.shape[1]
    ends = jnp.cumsum(lengths[0]).astype(jnp.int32)
    meta = jnp.concatenate([ends, jnp.stack([rank, group, shard])])
    tall = math.gcd(rows_here, 160)
    steps = rows_here // tall
    wait = functools.partial(pause, meta)
    whole = lambda a: pl.BlockSpec(a.shape, lambda *i: (0,) * a.ndim)
    both = pl.BlockSpec((2, width), lambda *i: (0, 0))
    row_block = pl.BlockSpec((tall, width), lambda i, m: (i, 0))
    row_shape = (rows_here, width)
    gain_block = pl.BlockSpec((8, width), lambda i, m: (0, 0))

    def near(value):
        return swap(value, "tensor", 1, ranks)

    def across(value):
        return swap(value, "dp", 1, 2)

    def gather_far(value):
        pieces = {0: value}
        bit = ranks // 2
        while bit > 1:
            pieces |= {k | bit: swap(v, "tensor", bit, ranks) for k, v in pieces.items()}
            bit //= 2
        return [pieces[k] for k in range(0, ranks, 2)]

    def ordered(even, odd):
        return [v for pair in zip(even, odd) for v in pair]

    def gather_near(even, copy):
        return [near(copy)] + [near(v) for v in even[1:]]

    def scatter(name, x, weight):
        product = lambda n, received=None: term(
            f"{name}_{n}", meta, x, weight, rows_here, ranks, n, received
        )
        far_send = near(product(3))
        far_keep = near(product(1))
        send = product(2, far_send)
        keep = product(0, far_keep)
        return finish_sum(send, keep, rows_here, ranks)

    def along(value):
        return lax.ppermute(value, "group", [(i, (i + 1) % groups) for i in range(groups)])

    def row_parts(own, far):
        return [
            part_of(v, lambda m, k=k, at=at: lax.rem(m[items + 1] + groups - k, groups) * strip + at)
            for k, both_halves in enumerate(zip(own, far)) for at, v in zip((0, half), both_halves)
        ]

    gain_pieces = [norm_gains] + [swap(norm_gains, "group", k, groups) for k in range(1, groups)]
    tall_strip = pl.BlockSpec((strip // 2, heads * 4 * HEAD_DIM), lambda i, m: (i, 0))
    strips = list(run(
        cast_heads_kernel, "cast_heads", (2,), meta, [(weight_heads, tall_strip)],
        [((strip, heads * 4 * HEAD_DIM), BF16, tall_strip)],
    ))
    strips.append(along(strips[0]))
    crossed = [across(strips[0])]
    gains, plain_gains = run(
        functools.partial(gains_kernel, items, half), "gains", (1,), meta,
        [(v, whole(v)) for v in gain_pieces],
        [((2, width), F32, both)] * 2,
        [pltpu.VMEM((groups, 2, width // groups), F32)],
    )
    first_norm, copy = run(
        functools.partial(first_norm_kernel, items, half), "first_norm", (steps,), meta,
        [(block_input, row_block), (gains, both)],
        [(row_shape, BF16, row_block)] * 2,
    )
    even_one = gather_far(first_norm)
    quarter = units // 2
    strip_block = pl.BlockSpec((strip // 2, quarter), lambda i, m: (i, 0))
    shards = run(
        cast_hidden_kernel, "cast_hidden", (2,), meta,
        [(weight_hidden, pl.BlockSpec((2, strip // 2, units), lambda i, m: (0, i, 0)))],
        [((strip, quarter), BF16, strip_block)] * 4,
    )
    odd_first = near(wait(copy, after=crossed)[0])
    back_low, back_copy = run(
        functools.partial(turn_kernel, items, half), "turn", (steps,), meta,
        [(cotangent, row_block)], [(row_shape, BF16, row_block)] * 2,
    )
    strips[1] = wait(strips[1], after=[odd_first])[0]
    strips.append(along(strips[1]))
    crossed.append(across(strips[1]))
    wait()
    strips[2] = wait(strips[2], after=crossed[1:])[0]
    strips.append(along(strips[2]))
    crossed.append(across(strips[2]))
    wait()
    even_one[1:] = wait(*even_one[1:], after=crossed[2:])
    odd_one = [odd_first] + [near(v) for v in even_one[1:]]
    strips[3] = wait(strips[3])[0]
    crossed.append(across(strips[3]))
    def gathered(shard, after=()):
        return lax.all_gather(wait(shard, after=after)[0], "group", axis=0, tiled=True)

    def columns(own, far):
        return [
            part_of(v, lambda m, at=at: at, n * quarter)
            for n in range(2) for at, v in ((0, own[n]), (half, far[n]))
        ]

    lower_own = [gathered(shards[0], odd_one[1:])]
    back_low = wait(back_low)[0]
    even_back = gather_far(back_low)
    all_one = ordered(even_one, odd_one)
    triple, heads_all = rows_matmul(
        "qkv", meta, all_one, row_parts(strips, crossed), store_rounded, [], [(BF16, same)],
        use=heads * 3 * HEAD_DIM, saved=True,
    )
    inward_w = [part_of(heads_all, columns=heads * 3 * HEAD_DIM)]
    outward_w = [part_of(heads_all, source_column=heads * 3 * HEAD_DIM)]
    lower_own.append(gathered(shards[1]))
    lower_own[0] = wait(lower_own[0])[0]
    lower_far = [across(lower_own[0])]
    pairs = 2 if heads % 2 == 0 else 1
    calls = heads // pairs
    mixed, logs = attend(meta, triple, items, rows_here, heads, pairs, 0)
    raise_own = [gathered(shards[2])]
    for n in range(1, calls):
        mixed, logs = attend(meta, triple, items, rows_here, heads, pairs, n, (mixed, logs))
    lower_own[1] = wait(lower_own[1], after=lower_far)[0]
    lower_far.append(across(lower_own[1]))
    back_copy, *even_back[1:] = wait(back_copy, *even_back[1:])
    odd_back = gather_near(even_back, back_copy)
    raise_own.append(gathered(shards[3]))
    wait(after=odd_back)
    keep, received = scatter("project", [mixed], outward_w)
    raise_own[0] = wait(raise_own[0])[0]
    raise_far = [across(raise_own[0])]
    middle, second_norm = run(
        functools.partial(second_norm_kernel, items, half), "second_norm", (steps,), meta,
        [(block_input, row_block), (keep, row_block), (received, row_block), (gains, both)],
        [(row_shape, F32, row_block), (row_shape, BF16, row_block)],
    )
    even_two = gather_far(second_norm)
    odd_first = near(second_norm)
    raise_own[1] = wait(raise_own[1])[0]
    raise_far.append(across(raise_own[1]))
    raise_w = columns(raise_own, raise_far)
    all_back = ordered(even_back, odd_back)
    back_hidden, lower_all = rows_matmul(
        "back_hidden", meta, all_back, columns(lower_own, lower_far), store_rounded, [], [(BF16, same)], saved=True
    )
    lower_w = [part_of(lower_all)]
    wait(after=[odd_first])

    def feed(pieces, first, filled=()):
        return rows_matmul(
            "raise", meta, pieces, raise_w, store_gelu, [(back_hidden, lambda i: i + first)],
            [(BF16, lambda i: i + first)] * 2, rows=total, staged=True, filled=filled,
        )

    filled = feed([even_two[0], odd_first], 0)
    even_two[1:] = wait(*even_two[1:])
    odd_two = [odd_first] + [near(v) for v in even_two[1:]]
    wait()
    all_two = ordered(even_two, odd_two)
    hidden, back_before = feed(all_two[2:], 2, filled)
    pieces = lambda values: [(v, k * rows_here) for k, v in enumerate(values)]

    def grad(name, left, right, first):
        return weight_grad(name, meta, pieces(left), right if type(right) is list else [right], first, half)

    grad_lower_far = across(grad("lower_far", all_back, hidden, half))
    keep, received = scatter("back_second", [back_before], raise_w)
    grad_raise_far = across(grad("raise_far", all_two, back_before, half))
    grad_lower = grad("lower_own", all_back, hidden, 0)
    back_middle, gain_second, back_low_middle = run(
        lambda meta, *refs: second_back_kernel(*refs), "second_back", (steps,), meta,
        [(v, row_block) for v in (middle, keep, received, back_low)] + [(gains, both)],
        [(row_shape, F32, row_block), ((8, width), F32, gain_block), (row_shape, BF16, row_block)],
    )
    even_middle = gather_far(back_low_middle)
    odd_first = near(back_low_middle)
    grad_raise = grad("raise_own", all_two, back_before, 0)
    wait(after=[odd_first])
    out_keep, out_received = scatter("lower", [hidden], lower_w)

    def summed(delta):
        return lax.psum_scatter(delta, "group", scatter_dimension=0, tiled=True)

    def adam_hidden(name, own, far, weight, part, filled=()):
        moment, square, delta = adam(
            name, meta, items, side_by_side, [(own, units, 0)], [(far, units, 0)],
            [(v, v.shape[1], 0) for v in weight],
            first_hidden, second_hidden, part, filled=filled,
        )
        return moment, square, summed(delta)

    *states, lower_delta = adam_hidden("adam_lower", grad_lower, grad_lower_far, [lower_all], 1)
    even_middle[1:] = wait(*even_middle[1:])
    odd_middle = [odd_first] + [near(v) for v in even_middle[1:]]
    wait()

    all_middle = ordered(even_middle, odd_middle)
    back_mixed = rows_matmul("back_mixed", meta, all_middle, outward_w, store_rounded, [], [(BF16, same)])[0]
    grad_out_far = across(grad("out_far", all_middle, mixed, half))
    moment_hidden, square_hidden, raise_delta = adam_hidden(
        "adam_raise", grad_raise, grad_raise_far, raise_own, 0, tuple(states)
    )
    back_triples, grad_in_fars = [], []
    for n in range(calls):
        back_triples.append(
            attend_back(meta, triple, mixed, back_mixed, logs, items, rows_here, heads, pairs, n)
        )
        grad_in_fars.append(across(grad("in_far", all_one, back_triples[n], half)))
        if n == 0:
            grad_out = grad("out_own", all_middle, mixed, 0)
            block_output = run(
                functools.partial(output_kernel, items, half), "output", (steps,), meta,
                [(v, row_block) for v in (middle, out_keep, out_received)],
                [(row_shape, BF16, row_block)],
            )[0]
            hidden_out = outer(
                "outer_lower", meta, groups, [lower_delta], weight_hidden, momentum_hidden, average_hidden, 1
            )
    product = lambda n, received=None: term(
        f"back_first_{n}", meta, back_triples, inward_w, rows_here, ranks, n, received
    )
    far_send = near(product(3))
    far_keep = near(product(1))
    send = product(2, far_send)
    grad_in = grad("in_own", all_one, back_triples, 0)
    in_wide, out_wide = pairs * 3 * HEAD_DIM, heads * HEAD_DIM
    moment_heads, square_heads, *deltas = adam(
        "adam_heads", meta, items, by_head,
        [(grad_in, calls * in_wide, 0), (grad_out, out_wide, 0)],
        [(v, in_wide, 0) for v in grad_in_fars] + [(grad_out_far, out_wide, 0)],
        [(heads_all, calls * in_wide, 0), (heads_all, out_wide, 3)],
        first_heads[:, None], second_heads[:, None], 0, groups,
    )
    heads_deltas = [deltas[0]] + [
        lax.ppermute(deltas[k], "group", [(i, (i + k) % groups) for i in range(groups)])
        for k in range(1, groups)
    ]
    keep = product(0, far_keep)
    keep, received = finish_sum(send, keep, rows_here, ranks)
    input_grad, gain_first = run(
        functools.partial(first_back_kernel, items, half), "first_back", (steps,), meta,
        [(block_input, row_block), (gains, both)] + [(v, row_block) for v in (back_middle, keep, received)],
        [(row_shape, F32, row_block), ((8, width), F32, gain_block)],
    )
    gain_grad = run(
        functools.partial(gain_total_kernel, items, half), "gain_total", (1,), meta,
        [(v, whole(v)) for v in (gain_first, gain_second)],
        [((2, width), F32, both)],
    )[0]

    def added(value, other):
        return run(
            add_kernel, "add", (1,), meta, [(value, whole(value)), (other, whole(other))],
            [(value.shape, F32, whole(value))],
        )[0]

    far_gain = across(gain_grad)
    wait()
    gain_grad = added(gain_grad, far_gain)
    bit = 1
    while bit < ranks:
        far_gain = swap(gain_grad, "tensor", bit, ranks)
        wait()
        gain_grad = added(gain_grad, far_gain)
        bit *= 2
    moment_gains, square_gains, delta_gains = adam_math(
        plain_gains, gain_grad, first_gains[0], second_gains[0], GAIN_RATE, 0.0
    )
    short = width // groups

    def gain_part(k):
        return lax.dynamic_slice_in_dim(delta_gains, (group ^ k) * short, short, 1)

    change_gains = gain_part(0)
    for k in range(1, groups):
        change_gains = change_gains + swap(gain_part(k), "group", k, groups)
    change_gains = change_gains / groups
    velocity_gains, trail_gains, master_gains = outer_math(
        norm_gains, change_gains, momentum_gains, average_gains
    )
    change_hidden, velocity_hidden, trail_hidden, master_hidden, copy_hidden = outer(
        "outer_raise", meta, groups, [raise_delta], weight_hidden, momentum_hidden, average_hidden, 0,
        filled=hidden_out,
    )
    change_heads, velocity_heads, trail_heads, master_heads, copy_heads = (
        v[0]
        for v in outer(
            "outer_heads", meta, groups, heads_deltas, weight_heads[None], momentum_heads[None],
            average_heads[None], 0,
        )
    )
    return (
        block_output,
        input_grad,
        moment_heads[:, 0],
        moment_hidden,
        moment_gains[None],
        square_heads[:, 0],
        square_hidden,
        square_gains[None],
        change_heads,
        change_hidden,
        change_gains,
        velocity_heads,
        velocity_hidden,
        velocity_gains,
        trail_heads,
        trail_hidden,
        trail_gains,
        master_heads,
        master_hidden,
        master_gains,
        copy_heads,
        copy_hidden,
    )


def solution(mesh):
    rows = P(("group", "dp", "tensor"), None)
    heads, hidden, gains = P(("dp", "group"), "tensor"), P(None, ("dp", "group"), "tensor"), P(None, "group")
    states = (P("group", "dp", "tensor"), P("group", None, "dp", "tensor"), P("group", None, None))
    in_specs = (rows, rows, P(("group", "dp"), None)) + (heads, hidden, gains) * 3 + states * 2
    out_specs = (rows, rows) + states * 2 + (heads, hidden, gains) * 4 + (heads, hidden)
    return jax.shard_map(local, mesh=mesh, in_specs=in_specs, out_specs=out_specs, check_vma=False)
```

```python
import functools
import math

import jax
import jax.numpy as jnp
from jax import lax
from jax.experimental import pallas as pl
from jax.experimental.pallas import tpu as pltpu
from jax.sharding import PartitionSpec as P

HEAD_DIM = 128
STEP = 8

NORM_EPS = 1e-05
INNER_RATE = 0.02
GAIN_RATE = 0.5
BETA_ONE = 0.9
BETA_TWO = 0.95
ADAM_EPS = 1e-08
WEIGHT_DECAY = 0.1
OUTER_RATE = 0.7
OUTER_MOMENTUM = 0.9
EMA_KEEP = 0.5

BF16 = jnp.bfloat16
F32 = jnp.float32
SCALE = HEAD_DIM ** (-0.5)
LOG2E = math.log2(math.e)
SCALE_LOG2 = SCALE * LOG2E
NEGATIVE = -1e30


def swap(value, axis, bit, size):
    return lax.ppermute(value, axis, [(i, i ^ bit) for i in range(size)])


ANYWHERE = pl.BlockSpec(memory_space=pl.ANY)
LIMIT = 60 * 2**20
line = []


def run(kernel, name, grid, meta, ins, outs, scratch=(), after=(), alias=None):
    arrays = [a for a, _ in ins]
    extra = [a for a in line + list(after) if all(a is not b for b in arrays)]
    count, skip = len(ins), len(extra)

    def body(*refs):
        kernel(*refs[: 1 + count], *refs[1 + count + skip :])

    result = pl.pallas_call(
        body,
        grid_spec=pltpu.PrefetchScalarGridSpec(
            num_scalar_prefetch=1,
            grid=grid,
            in_specs=[s for _, s in ins] + [ANYWHERE] * skip,
            out_specs=[s for _, _, s in outs],
            scratch_shapes=list(scratch),
        ),
        out_shape=[jax.ShapeDtypeStruct(s, d) for s, d, _ in outs],
        input_output_aliases={1 + a: b for a, b in (alias or {}).items()},
        compiler_params=pltpu.CompilerParams(vmem_limit_bytes=LIMIT),
        cost_estimate=pl.CostEstimate(flops=10**12, bytes_accessed=1, transcendentals=0),
        name=name,
    )(meta, *arrays, *extra)
    line[:] = [result[0]]
    return result


def dot_last(left, right):
    return lax.dot_general(
        left, right, (((1,), (1,)), ((), ())), preferred_element_type=F32
    )


def dot_first(left, right):
    return lax.dot_general(
        left, right, (((0,), (0,)), ((), ())), preferred_element_type=F32
    )


def dot(left, right):
    return jnp.dot(left, right, preferred_element_type=F32)


def normalize(rows):
    mean = jnp.mean(rows, axis=-1, keepdims=True)
    centred = rows - mean
    var = jnp.mean(centred * centred, axis=-1, keepdims=True)
    inverse = lax.rsqrt(var + NORM_EPS)
    return centred * inverse, inverse


def normalize_back(back, normed, inverse, gain):
    scaled = back * gain
    first = jnp.mean(scaled, axis=-1, keepdims=True)
    second = jnp.mean(scaled * normed, axis=-1, keepdims=True)
    terms = (back * normed).reshape(-1, 8, back.shape[-1])
    return inverse * (scaled - first - normed * second), jnp.sum(terms, axis=0)


def gelu_parts(u):
    size = jnp.abs(u) * (0.5**0.5)
    t = 1.0 / (1.0 + 0.3275911 * size)
    poly = t * (
        0.254829592
        + t * (-0.284496736 + t * (1.421413741 + t * (-1.453152027 + t * 1.061405429)))
    )
    bell = jnp.exp(-0.5 * u * u)
    tail = 0.5 * poly * bell
    below = jnp.where(u >= 0.0, 1.0 - tail, tail)
    return below, bell * (1.0 / math.sqrt(2.0 * math.pi))


def item_start(places, meta, items):
    start = jnp.zeros_like(places)
    for k in range(items):
        start = jnp.where(places >= meta[k], meta[k], start)
    return start


def copy_in(meta, items, source, target, rows, step, total):
    for s in range(total // step):
        owner, offset = (s * step) // rows, (s * step) % rows
        local = pl.multiple_of((owner ^ meta[items]) * rows + offset, step)
        target[s * step : (s + 1) * step, :] = source[pl.ds(local, step), :]


def local_row(meta, items, chunk, rows, step):
    per = rows // step
    owner, offset = chunk // per, chunk % per
    return pl.multiple_of((owner ^ meta[items]) * rows + offset * step, step)


def head_columns(n, c):
    return slice((3 * n + c) * HEAD_DIM, (3 * n + c + 1) * HEAD_DIM)


def attend_kernel(items, rows, step, block, pairs, meta, qkv, *refs):
    mixed, logs, nat, values, acc, top = refs[-6:]
    total = qkv.shape[0]
    index = pl.program_id(0)

    @pl.when(index == 0)
    def _():
        copy_in(meta, items, qkv, nat, rows, step, total)
        for n in range(pairs):
            values[n, :, 0:HEAD_DIM] = nat[:, head_columns(n, 2)]
            values[n, :, HEAD_DIM:] = jnp.ones((total, HEAD_DIM), BF16)

    first_row = index * block
    acc[...] = jnp.zeros_like(acc)
    top[...] = jnp.full_like(top, NEGATIVE)
    low_start = item_start(first_row, meta, items)
    high_start = item_start(first_row + block - 1, meta, items)

    def tile(j, masked, keys=block, low=0, high=block):
        at = pl.ds(pl.multiple_of(j * block, block), keys)
        here = pl.ds(pl.multiple_of(first_row + low, math.gcd(block, low)), high - low)
        own = slice(low, high)
        if masked:
            q_place = first_row + low + lax.broadcasted_iota(jnp.int32, (high - low, 1), 0)
            k_place = j * block + lax.broadcasted_iota(jnp.int32, (1, keys), 1)
            live = (k_place <= q_place) & (k_place >= item_start(q_place, meta, items))
        scores = [dot_last(nat[here, head_columns(n, 0)], nat[at, head_columns(n, 1)]) for n in range(pairs)]
        for n in range(pairs):
            s = jnp.where(live, scores[n], NEGATIVE) if masked else scores[n]
            old = top[n, own, :]
            new = jnp.maximum(old, jnp.max(s, axis=1, keepdims=True))
            p = jnp.exp2((s - jnp.concatenate([new] * (keys // HEAD_DIM), axis=1)) * SCALE_LOG2)
            keep = jnp.exp2((old - new) * SCALE_LOG2)
            top[n, own, :] = new
            acc[n, own, :] = acc[n, own, :] * jnp.concatenate([keep, keep], axis=1) + dot(
                p.astype(BF16), values[n, at, :]
            )

    @pl.loop(low_start // block, index)
    def _(j):
        whole = high_start <= j * block

        @pl.when(whole)
        def _():
            tile(j, False)

        @pl.when(jnp.logical_not(whole))
        def _():
            tile(j, True)

    middle = block // 2
    tile(index, True, middle, 0, middle)
    tile(index, True, block, middle, block)
    per = block // step
    for n in range(pairs):
        weight = acc[n, :, HEAD_DIM:]
        out = (acc[n, :, 0:HEAD_DIM] / weight).astype(BF16)
        for c in range(per):
            at = local_row(meta, items, index * per + c, rows, step)
            mixed[pl.ds(at, step), n * HEAD_DIM : (n + 1) * HEAD_DIM] = out[c * step : (c + 1) * step, :]
        log = top[n] * SCALE_LOG2 + jnp.log(weight) * LOG2E
        logs[n, 0] = log.T[0:8, :]


def attend(meta, qkv, items, rows, heads, pairs, call, filled=(), after=()):
    total = qkv.shape[0]
    block = min(512, total)
    step = math.gcd(rows, block)
    count = total // block
    return run(
        functools.partial(attend_kernel, items, rows, step, block, pairs),
        "attend",
        (count,),
        meta,
        [(qkv, pl.BlockSpec((total, pairs * 3 * HEAD_DIM), lambda i, m: (0, call)))]
        + [(v, ANYWHERE) for v in filled],
        [
            ((total, heads * HEAD_DIM), BF16, pl.BlockSpec((total, pairs * HEAD_DIM), lambda i, m: (0, call))),
            ((heads, count, 8, block), F32, pl.BlockSpec((pairs, 1, 8, block), lambda i, m: (call, i, 0, 0))),
        ],
        [
            pltpu.VMEM((total, pairs * 3 * HEAD_DIM), BF16),
            pltpu.VMEM((pairs, total, 2 * HEAD_DIM), BF16),
            pltpu.VMEM((pairs, block, 2 * HEAD_DIM), F32),
            pltpu.VMEM((pairs, block, HEAD_DIM), F32),
        ],
        after,
        {1 + n: n for n in range(len(filled))},
    )


def attend_back_kernel(
    items, rows, step, block, pairs, meta, qkv, mixed, back, logs, grads, nat, nat_mixed, nat_back, dq, dk, dv
):
    total = qkv.shape[0]
    index = pl.program_id(0)
    own = [slice(n * HEAD_DIM, (n + 1) * HEAD_DIM) for n in range(pairs)]

    @pl.when(index == 0)
    def _():
        copy_in(meta, items, qkv, nat, rows, step, total)
        copy_in(meta, items, mixed, nat_mixed, rows, step, total)
        copy_in(meta, items, back, nat_back, rows, step, total)
        dk[...] = jnp.zeros_like(dk)
        dv[...] = jnp.zeros_like(dv)

    first_row = index * block
    here = pl.ds(pl.multiple_of(first_row, block), block)
    row_terms = []
    for n in range(pairs):
        product = nat_back[here, own[n]].astype(F32) * nat_mixed[here, own[n]].astype(F32)
        row_terms.append(jnp.sum(product.T, axis=0, keepdims=True))
    dq[...] = jnp.zeros_like(dq)
    low_start = item_start(first_row, meta, items)
    high_start = item_start(first_row + block - 1, meta, items)

    def tile(j, masked, low=0, high=block):
        at = pl.ds(pl.multiple_of(j * block + low, math.gcd(block, low)), high - low)
        here = pl.ds(pl.multiple_of(first_row + low, math.gcd(block, low)), block - low)
        mine = slice(low, block)
        if masked:
            k_place = j * block + low + lax.broadcasted_iota(jnp.int32, (high - low, 1), 0)
            q_place = first_row + mine.start + lax.broadcasted_iota(jnp.int32, (1, block - mine.start), 1)
            live = (k_place <= q_place) & (k_place >= item_start(q_place, meta, items))
        scores = [dot_last(nat[at, head_columns(n, 1)], nat[here, head_columns(n, 0)]) for n in range(pairs)]
        backs = [dot_last(nat[at, head_columns(n, 2)], nat_back[here, own[n]]) for n in range(pairs)]
        for n in range(pairs):
            p = jnp.exp2(scores[n] * SCALE_LOG2 - logs[n, 0, 0:1, mine])
            if masked:
                p = jnp.where(live, p, 0.0)
            s = (p * (backs[n] - row_terms[n][:, mine])).astype(BF16)
            dv[at, own[n]] += dot(p.astype(BF16), nat_back[here, own[n]])
            dk[at, own[n]] += dot(s, nat[here, head_columns(n, 0)])
            dq[mine, own[n]] += dot_first(s, nat[at, head_columns(n, 1)])

    @pl.loop(low_start // block, index)
    def _(j):
        whole = high_start <= j * block

        @pl.when(whole)
        def _():
            tile(j, False)

        @pl.when(jnp.logical_not(whole))
        def _():
            tile(j, True)

    middle = block // 2
    tile(index, True, 0, middle)
    tile(index, True, middle, block)
    per = block // step
    for n in range(pairs):
        out = (dq[:, own[n]] * SCALE).astype(BF16)
        for c in range(per):
            to = local_row(meta, items, index * per + c, rows, step)
            grads[pl.ds(to, step), head_columns(n, 0)] = out[c * step : (c + 1) * step, :]

    @pl.when(index == pl.num_programs(0) - 1)
    def _():
        for s in range(total // step):
            to = local_row(meta, items, s, rows, step)
            part = slice(s * step, (s + 1) * step)
            for n in range(pairs):
                grads[pl.ds(to, step), head_columns(n, 1)] = (dk[part, own[n]] * SCALE).astype(BF16)
                grads[pl.ds(to, step), head_columns(n, 2)] = dv[part, own[n]].astype(BF16)


def attend_back(meta, qkv, mixed, back, logs, items, rows, heads, pairs, call, after=()):
    total = qkv.shape[0]
    block = logs.shape[-1]
    step = math.gcd(rows, block)
    count = total // block
    wide = pl.BlockSpec((total, pairs * 3 * HEAD_DIM), lambda i, m: (0, call))
    narrow = pl.BlockSpec((total, pairs * HEAD_DIM), lambda i, m: (0, call))
    return run(
        functools.partial(attend_back_kernel, items, rows, step, block, pairs),
        "attend_back",
        (count,),
        meta,
        [
            (qkv, wide),
            (mixed, narrow),
            (back, narrow),
            (logs, pl.BlockSpec((pairs, 1, 8, block), lambda i, m: (call, i, 0, 0))),
        ],
        [((total, pairs * 3 * HEAD_DIM), BF16, pl.BlockSpec((total, pairs * 3 * HEAD_DIM), lambda i, m: (0, 0)))],
        [
            pltpu.VMEM((total, pairs * 3 * HEAD_DIM), BF16),
            pltpu.VMEM((total, pairs * HEAD_DIM), BF16),
            pltpu.VMEM((total, pairs * HEAD_DIM), BF16),
            pltpu.VMEM((block, pairs * HEAD_DIM), F32),
            pltpu.VMEM((total, pairs * HEAD_DIM), F32),
            pltpu.VMEM((total, pairs * HEAD_DIM), F32),
        ],
        after,
    )[0]


TILE = 512


def tile_of(size):
    return next(tile for tile in (min(TILE, size), 256, 128) if size % tile == 0)


def part_of(array, row=lambda m: 0, column=0, source_row=0, rows=None, source_column=0, columns=None):
    rows, columns = rows or array.shape[0] - source_row, columns or array.shape[1] - source_column
    return array, (row, column, source_row, rows, source_column, columns)


class Pieces:
    def __init__(self, refs, places, dim, target, sems, meta, tile=None):
        self.refs, self.places, self.dim, self.target, self.sems, self.meta = refs, places, dim, target, sems, meta
        self.tile = tile or tile_of(target.shape[dim])

    def span(self, p):
        row, column, _, rows, _, columns = self.places[p]
        first, size = (column, columns) if self.dim else (row(None), rows)
        return first // self.tile, size // self.tile

    def copy(self, p, n):
        row, column, source_row, rows, source_column, columns = self.places[p]
        tile = self.tile
        at = (n - self.span(p)[0]) * tile + (source_column if self.dim else source_row)
        at = pl.ds(pl.multiple_of(at, math.gcd(tile, source_column if self.dim else source_row)), tile)
        to = pl.ds(pl.multiple_of(n * tile, tile), tile)
        if self.dim:
            source = self.refs[p].at[pl.ds(source_row, rows), at]
            target = self.target.at[pl.ds(pl.multiple_of(row(self.meta), math.gcd(rows, TILE)), rows), to]
        else:
            source = self.refs[p].at[at, pl.ds(source_column, columns)]
            target = self.target.at[to, pl.ds(column, columns)]
        return pltpu.make_async_copy(source, target, self.sems.at[p, n])

    def start(self):
        for n in range(self.target.shape[self.dim] // self.tile):
            for p in range(len(self.refs)):
                first, count = self.span(p)
                if first <= n < first + count:
                    self.copy(p, n).start()

    def wait(self, n):
        for p in range(len(self.refs)):
            first, count = self.span(p)
            if isinstance(n, int):
                if first <= n < first + count:
                    self.copy(p, n).wait()
            elif first == 0 and count == self.target.shape[self.dim] // self.tile:
                self.copy(p, n).wait()
            else:

                @pl.when((n >= first) & (n < first + count))
                def _(p=p):
                    self.copy(p, n).wait()


def tiles_of(size):
    return size // tile_of(size)


def rows_kernel(count, places, use, saved, finish, staged, filled, meta, *refs):
    parts = len(places)
    pieces, strips, refs = refs[:count], refs[count : count + parts], refs[count + parts :]
    stages = refs[len(refs) - staged :]
    refs = refs[: len(refs) - staged]
    blocks, (slots, weight, piece_sems, weight_sems) = refs[:-4], refs[-4:]
    i = pl.program_id(0)
    parts = Pieces(strips, places, 1, weight, weight_sems, meta)

    def fetch(n):
        return pltpu.make_async_copy(pieces[n], slots.at[n % 2], piece_sems.at[n % 2])

    @pl.when(i == 0)
    def _():
        fetch(0).start()
        parts.start()

    for n in range(1, count):

        @pl.when(i + 1 == n)
        def _(n=n):
            fetch(n).start()

    for n in range(count):

        @pl.when(i == n)
        def _(n=n):
            fetch(n).wait()

    wide = tile_of(use)
    many, loaded = use // wide, weight.shape[1] // parts.tile
    early = wide != parts.tile
    if early or staged:

        @pl.when(i == 0)
        def _():
            for n in range(loaded):
                parts.wait(n)

    if staged:
        blocks = blocks[: len(blocks) - 2 - saved - filled] + blocks[len(blocks) - 2 - saved :]
        x = slots[i % 2]
        for n in range(many + 1):
            if n < many:
                stages[n % 2][...] = dot(x, weight[:, n * wide : (n + 1) * wide])
            if n:
                finish(
                    stages[(n - 1) % 2][...], slice((n - 1) * wide, n * wide), *blocks[: len(blocks) - saved]
                )
    else:

        @pl.loop(0, many)
        def _(n):
            if not early:

                @pl.when(i == 0)
                def _():
                    parts.wait(n)

            at = pl.ds(pl.multiple_of(n * wide, wide), wide)
            finish(dot(slots[i % 2], weight[:, at]), at, *blocks[: len(blocks) - saved])

        if not early and loaded > many:

            @pl.when(i == 0)
            def _():
                for n in range(many, loaded):
                    parts.wait(n)

    if saved:
        kept = blocks[-1]
        kept[...] = weight[pl.ds(pl.multiple_of(i * kept.shape[0], kept.shape[0]), kept.shape[0]), :]


def rows_matmul(
    name, meta, pieces, weight, finish, extra, outs, use=None, rows=None, saved=False, staged=False, filled=(),
    block_column=0, columns=None, after=()
):
    strips, places = zip(*weight)
    tall, depth = pieces[0].shape
    wide = max(place[1] + place[5] for place in places)
    use = use or wide
    count, parts = len(pieces), len(strips)
    block = lambda index: pl.BlockSpec((tall, use), lambda i, m: (index(i), block_column))
    more = [((depth, wide), BF16, pl.BlockSpec((depth // count, wide), lambda i, m: (i, 0)))] if saved else []
    ins = [(p, ANYWHERE) for p in pieces] + [(p, ANYWHERE) for p in strips] + [(a, block(f)) for a, f in extra]
    return run(
        functools.partial(rows_kernel, count, places, use, saved, finish, 2 * staged, len(filled)),
        name,
        (count,),
        meta,
        ins + [(v, ANYWHERE) for v in filled],
        [((rows or count * tall, columns or use), d, block(f)) for d, f in outs] + more,
        [
            pltpu.VMEM((2, tall, depth), BF16),
            pltpu.VMEM((depth, wide), BF16),
            pltpu.SemaphoreType.DMA((2,)),
            pltpu.SemaphoreType.DMA((parts, tiles_of(wide))),
        ]
        + [pltpu.VMEM((tall, tile_of(use)), F32)] * (2 * staged),
        after,
        {len(ins) + n: n for n in range(len(filled))},
    )


def store_rounded(value, at, out):
    out[:, at] = value.astype(BF16)


def store_gelu(value, at, back, hidden, back_before):
    below, density = gelu_parts(value)
    hidden[:, at] = (value * below).astype(BF16)
    back_before[:, at] = (back[:, at].astype(F32) * (below + value * density)).astype(BF16)


def same(i):
    return i


def term_kernel(count, places, offset, part, meta, *refs):
    x, strips, refs = refs[:count], refs[count : count + len(places)], refs[count + len(places) :]
    received = refs[0] if len(refs) == 11 else None
    out, held, extra, tiles, weight, x_sems, extra_sems, tile_sems, sems, _ = refs[-10:]
    i = pl.program_id(0)
    parts = Pieces(strips, places, 0, weight, sems, meta)
    wide = parts.tile
    many = weight.shape[0] // wide
    own_rows = pl.ds(pl.multiple_of((4 * i + offset) * part, part), part)
    out_rows = pl.ds(pl.multiple_of(i * part, part), part)

    def load_x(n):
        at = sum(v.shape[1] for v in x[:n])
        to = held.at[:, at : at + x[n].shape[1]]
        return pltpu.make_async_copy(x[n].at[own_rows, :], to, x_sems.at[n])

    def load_extra(n):
        at = pl.ds(pl.multiple_of(n * wide, wide), wide)
        return pltpu.make_async_copy(received.at[out_rows, at], extra.at[n], extra_sems.at[n])

    def put(n):
        at = pl.ds(pl.multiple_of(n * wide, wide), wide)
        return pltpu.make_async_copy(tiles.at[n % 2], out.at[out_rows, at], tile_sems.at[n % 2])

    for n in range(count):
        load_x(n).start()

    @pl.when(i == 0)
    def _():
        parts.start()

    if received is not None:
        for n in range(many):
            load_extra(n).start()
    for n in range(count):
        load_x(n).wait()

    @pl.loop(0, many)
    def _(n):
        @pl.when(i == 0)
        def _():
            parts.wait(n)

        if received is not None:
            load_extra(n).wait()

        @pl.when(n > 1)
        def _():
            put(n - 2).wait()

        at = pl.ds(pl.multiple_of(n * wide, wide), wide)
        value = dot_last(held[...], weight[at, :])
        if received is not None:
            value = value + extra[n].astype(F32)
        tiles[n % 2] = value.astype(BF16)
        put(n).start()

    for n in range(max(many - 2, 0), many):
        put(n).wait()


def term(name, meta, x, weight, part, ranks, offset, received=None, after=()):
    strips, places = zip(*weight)
    n = sum(v.shape[1] for v in x)
    width = max(place[0](None) + place[3] for place in places)
    many, wide = tiles_of(width), tile_of(width)
    rows = ranks // 4 * part
    return run(
        functools.partial(term_kernel, len(x), places, offset, part),
        name,
        (ranks // 4,),
        meta,
        [(v, ANYWHERE) for v in x]
        + [(s, ANYWHERE) for s in strips]
        + ([] if received is None else [(received, ANYWHERE)]),
        [((rows, width), BF16, ANYWHERE)],
        [
            pltpu.VMEM((part, n), BF16),
            pltpu.VMEM((many, part, wide), BF16),
            pltpu.VMEM((2, part, wide), BF16),
            pltpu.VMEM((width, n), BF16),
            pltpu.SemaphoreType.DMA((len(x),)),
            pltpu.SemaphoreType.DMA((many,)),
            pltpu.SemaphoreType.DMA((2,)),
            pltpu.SemaphoreType.DMA((len(strips), many)),
            pltpu.SMEM((1,), jnp.int32),
        ],
        after,
    )[0]


def finish_sum(send, keep, part, ranks):
    bit = 2
    while True:
        received = swap(send, "tensor", bit, ranks)
        if keep.shape[0] == part:
            return keep, received
        total = (keep.astype(F32) + received.astype(F32)).astype(BF16).reshape(-1, 2, part, keep.shape[1])
        keep, send = (total[:, n].reshape(-1, keep.shape[1]) for n in (0, 1))
        bit *= 2


def weight_grad_kernel(rows_a, columns, first, meta, *refs):
    count, many = len(rows_a), len(columns)
    left, right, (out, slots, held, left_sems, right_sems) = (
        refs[:count], refs[count : count + many], refs[count + many :]
    )
    i = pl.program_id(0)
    steps = pl.num_programs(0)
    wide = slots.shape[2]
    places = [part_of(v, column=at)[1] for v, at in zip(right, columns)]
    loads = tile_of(right[0].shape[1])
    parts = Pieces(right, places, 1, held, right_sems, meta, loads)
    tile = tile_of(held.shape[1])

    def fetch(step, slot):
        at = pl.ds(pl.multiple_of(first + step * wide, wide), wide)
        return [
            pltpu.make_async_copy(ref.at[:, at], slots.at[slot, pl.ds(row, ref.shape[0])], left_sems.at[slot, n])
            for n, (ref, row) in enumerate(zip(left, rows_a))
        ]

    @pl.when(i == 0)
    def _():
        for copy in fetch(0, 0):
            copy.start()
        parts.start()

    @pl.when(i + 1 < steps)
    def _():
        for copy in fetch(i + 1, (i + 1) % 2):
            copy.start()

    for copy in fetch(i, i % 2):
        copy.wait()

    @pl.loop(0, held.shape[1] // tile)
    def _(n):
        @pl.when(i == 0)
        def _():
            for m in range(tile // loads):
                parts.wait(n * (tile // loads) + m)

        at = pl.ds(pl.multiple_of(n * tile, tile), tile)
        out[:, at] = dot_first(slots[i % 2], held[:, at]).astype(BF16)


def weight_grad(name, meta, left, right, first, half, after=()):
    wide = min(512, half)
    columns, n = [], 0
    for v in right:
        columns.append(n)
        n += v.shape[1]
    total = right[0].shape[0]
    return run(
        functools.partial(weight_grad_kernel, [r for _, r in left], columns, first),
        name,
        (half // wide,),
        meta,
        [(a, ANYWHERE) for a, _ in left] + [(v, ANYWHERE) for v in right],
        [((half, n), BF16, pl.BlockSpec((wide, n), lambda i, m: (i, 0)))],
        [
            pltpu.VMEM((2, total, wide), BF16),
            pltpu.VMEM((total, n), BF16),
            pltpu.SemaphoreType.DMA((2, len(left))),
            pltpu.SemaphoreType.DMA((len(right), n // tile_of(right[0].shape[1]))),
        ],
        after,
    )[0]


def strip_at(p, place, strip):
    return pl.ds(pl.multiple_of((p ^ place) * strip, strip), strip)


def turned(ref, place, strip):
    return jnp.concatenate([ref[:, strip_at(p, place, strip)] for p in range(ref.shape[1] // strip)], axis=1)


def store_turned(ref, value, place, strip):
    for p in range(value.shape[1] // strip):
        ref[:, strip_at(p, place, strip)] = value[:, p * strip : (p + 1) * strip].astype(ref.dtype)


def gains_kernel(items, strip, meta, *refs):
    pieces, (turned_out, plain, stack) = refs[:-3], refs[-3:]
    groups, short = len(pieces), pieces[0].shape[1]
    for k in range(groups):
        stack[k] = pieces[k][...]
    for j in range(groups):
        plain[:, j * short : (j + 1) * short] = stack[j ^ meta[items + 1]]
    turned_out[...] = turned(plain, meta[items + 2], strip)


def cast_heads_kernel(meta, weight, *outs):
    heads = weight.shape[1] // (4 * HEAD_DIM)
    for out in outs:
        for h in range(heads):
            at, near, far = 4 * h * HEAD_DIM, 3 * h * HEAD_DIM, (3 * heads + h) * HEAD_DIM
            out[:, near : near + 3 * HEAD_DIM] = weight[:, at : at + 3 * HEAD_DIM].astype(BF16)
            out[:, far : far + HEAD_DIM] = weight[:, at + 3 * HEAD_DIM : at + 4 * HEAD_DIM].astype(BF16)


def cast_hidden_kernel(meta, weight, *outs):
    for n, out in enumerate(outs):
        wide = out.shape[1]
        out[...] = weight[int(n < 2), :, n % 2 * wide : (n % 2 + 1) * wide].astype(BF16)


def first_norm_kernel(items, strip, meta, rows, gains, *outs):
    normed, _ = normalize(turned(rows, meta[items + 2], strip).astype(F32))
    for out in outs:
        out[...] = (normed * gains[0:1, :]).astype(BF16)


def turn_kernel(items, strip, meta, rows, *outs):
    for out in outs:
        out[...] = turned(rows, meta[items + 2], strip)


def add_kernel(meta, left, right, out):
    out[...] = left[...] + right[...]


def second_norm_kernel(items, strip, meta, rows, keep, received, gains, middle_out, *outs):
    middle = turned(rows, meta[items + 2], strip).astype(F32) + (
        keep[...].astype(F32) + received[...].astype(F32)
    )
    normed, _ = normalize(middle)
    middle_out[...] = middle
    for out in outs:
        out[...] = (normed * gains[1:2, :]).astype(BF16)


def second_back_kernel(middle, keep, received, back, gains, out, gain_out, *lows):
    normed, inverse = normalize(middle[...])
    given = keep[...].astype(F32) + received[...].astype(F32)
    grad, gain_part = normalize_back(given, normed, inverse, gains[1:2, :])
    grad = grad + back[...].astype(F32)
    out[...] = grad
    for low in lows:
        low[...] = grad.astype(BF16)

    @pl.when(pl.program_id(0) == 0)
    def _():
        gain_out[...] = jnp.zeros_like(gain_out)

    gain_out[...] += gain_part


def first_back_kernel(items, strip, meta, rows, gains, back, keep, received, out, gain_out):
    place = meta[items + 2]

    @pl.when(pl.program_id(0) == 0)
    def _():
        gain_out[...] = jnp.zeros_like(gain_out)

    normed, inverse = normalize(turned(rows, place, strip).astype(F32))
    given = keep[...].astype(F32) + received[...].astype(F32)
    grad, gain_part = normalize_back(given, normed, inverse, gains[0:1, :])
    gain_out[...] += gain_part
    store_turned(out, grad + back[...], place, strip)


def output_kernel(items, strip, meta, middle, keep, received, out):
    value = middle[...] + (keep[...].astype(F32) + received[...].astype(F32))
    store_turned(out, value, meta[items + 2], strip)


def gain_total_kernel(items, strip, meta, first, second, out):
    both = [jnp.sum(v, axis=0, keepdims=True) for v in (first[...], second[...])]
    store_turned(out, jnp.concatenate(both, axis=0), meta[items + 2], strip)


def adam_math(weight, grad, first, second, rate, decay):
    first = BETA_ONE * first + (1.0 - BETA_ONE) * grad
    second = BETA_TWO * second + (1.0 - BETA_TWO) * grad * grad
    scaled_first = first * (1.0 / (1.0 - BETA_ONE**STEP))
    scaled_second = second * (1.0 / (1.0 - BETA_TWO**STEP))
    update = scaled_first / (jnp.sqrt(scaled_second) + ADAM_EPS) + decay * weight
    return first, second, rate * update


def adam_kernel(join, counts, groups, per, items, meta, *refs):
    parts, at = [], 0
    for count in counts:
        parts.append(join([r[...].astype(F32) for r in refs[at : at + count]]))
        at += count
    own, far, weight = parts
    first, second = refs[at : at + 2]
    moment, square, *deltas = refs[-2 - groups :]
    moment[...], square[...], change = adam_math(
        weight, own + far, first[...], second[...], INNER_RATE, WEIGHT_DECAY
    )
    change = change.astype(BF16)
    if groups == 1:
        deltas[0][...] = change
    else:
        step = lax.rem(pl.program_id(0) // per + groups - meta[items + 1], groups)
        for k in range(groups):

            @pl.when(step == k)
            def _(k=k):
                deltas[k][...] = change


def side_by_side(parts):
    return parts[0] if len(parts) == 1 else jnp.concatenate(parts, axis=1)


def by_head(parts):
    *inward, outward = parts
    out, h = [], 0
    for part in inward:
        for n in range(part.shape[1] // (3 * HEAD_DIM)):
            out += [
                part[:, n * 3 * HEAD_DIM : (n + 1) * 3 * HEAD_DIM],
                outward[:, h * HEAD_DIM : (h + 1) * HEAD_DIM],
            ]
            h += 1
    return jnp.concatenate(out, axis=1)


def adam(name, meta, items, join, own, far, weight, first, second, part, groups=1, filled=(), after=()):
    rows, columns = first.shape[2:]
    tall = min(128, rows // groups)
    per = rows // groups // tall
    state = pl.BlockSpec((None, None, tall, columns), lambda i, m: (0, part, i, 0))

    def delta_block(k):
        def index(i, m):
            return (i if groups == 1 else jnp.clip(i - lax.rem(m[items + 1] + k, groups) * per, 0, per - 1), 0)

        return ((rows // groups, columns), BF16, pl.BlockSpec((tall, columns), index))

    ins = [
        (v, pl.BlockSpec((tall, wide), lambda i, m, at=at: (i, at))) for v, wide, at in own + far + weight
    ]
    ins += [(first, state), (second, state)]
    alias = {len(ins) + n: n for n in range(len(filled))}
    ins += [(v, ANYWHERE) for v in filled]
    return run(
        functools.partial(adam_kernel, join, [len(v) for v in (own, far, weight)], groups, per, items),
        name,
        (rows // tall,),
        meta,
        ins,
        [(first.shape, F32, state)] * 2 + [delta_block(k) for k in range(groups)],
        (),
        after,
        alias,
    )


def outer_math(weight, change, momentum, average):
    velocity = OUTER_MOMENTUM * momentum + change
    master = weight - OUTER_RATE * (change + OUTER_MOMENTUM * velocity)
    trail = EMA_KEEP * average + (1.0 - EMA_KEEP) * master
    return velocity, trail, master


def outer_kernel(groups, count, meta, *refs):
    totals, (weight, momentum, average) = refs[:count], refs[count : count + 3]
    change_out, velocity_out, trail_out, master_out, copy_out = refs[-5:]
    total = totals[0][...].astype(F32)
    for other in totals[1:]:
        total = total + other[...].astype(F32)
    change = total * (1.0 / groups)
    velocity, trail, master = outer_math(weight[...], change, momentum[...], average[...])
    change_out[...] = change
    velocity_out[...] = velocity
    trail_out[...] = trail
    master_out[...] = master
    copy_out[...] = master.astype(BF16)


def outer(name, meta, groups, totals, weight, momentum, average, part, filled=(), after=()):
    tall, wide = min(64, weight.shape[1]), weight.shape[2]
    spec = pl.BlockSpec((tall, wide), lambda i, m: (i, 0))
    state = pl.BlockSpec((None, tall, wide), lambda i, m: (part, i, 0))
    ins = [(v, spec) for v in totals] + [(v, state) for v in (weight, momentum, average)]
    alias = {len(ins) + n: n for n in range(len(filled))}
    return run(
        functools.partial(outer_kernel, groups, len(totals)),
        name,
        (weight.shape[1] // tall,),
        meta,
        ins + [(v, ANYWHERE) for v in filled],
        [(weight.shape, F32, state)] * 4 + [(weight.shape, BF16, state)],
        (),
        after,
        alias,
    )


def pause_kernel(meta, *refs):
    refs[-1][0] = 0


def pause(meta, *values, after=()):
    token = ((1,), jnp.int32, pl.BlockSpec(memory_space=pltpu.SMEM))
    out = run(
        pause_kernel, "pause", (1,), meta, [(v, ANYWHERE) for v in values],
        [(v.shape, v.dtype, ANYWHERE) for v in values] + [token], (), after, {n: n for n in range(len(values))},
    )
    line[:] = [out[-1]]
    return out[:-1]


def local(
    block_input,
    cotangent,
    lengths,
    weight_heads,
    weight_hidden,
    norm_gains,
    momentum_heads,
    momentum_hidden,
    momentum_gains,
    average_heads,
    average_hidden,
    average_gains,
    first_heads,
    first_hidden,
    first_gains,
    second_heads,
    second_hidden,
    second_gains,
):
    line.clear()
    groups, ranks = lax.axis_size("group"), lax.axis_size("tensor")
    group = lax.axis_index("group").astype(jnp.int32)
    shard = lax.axis_index("dp").astype(jnp.int32)
    rank = lax.axis_index("tensor").astype(jnp.int32)
    rows_here, width = block_input.shape
    total = rows_here * ranks
    strip = weight_heads.shape[0]
    half = width // 2
    heads = weight_heads.shape[1] // (4 * HEAD_DIM)
    units = weight_hidden.shape[2]
    items = lengths.shape[1]
    ends = jnp.cumsum(lengths[0]).astype(jnp.int32)
    meta = jnp.concatenate([ends, jnp.stack([rank, group, shard])])
    tall = math.gcd(rows_here, 160)
    steps = rows_here // tall
    wait = functools.partial(pause, meta)
    whole = lambda a: pl.BlockSpec(a.shape, lambda *i: (0,) * a.ndim)
    both = pl.BlockSpec((2, width), lambda *i: (0, 0))
    row_block = pl.BlockSpec((tall, width), lambda i, m: (i, 0))
    row_shape = (rows_here, width)
    gain_block = pl.BlockSpec((8, width), lambda i, m: (0, 0))

    def near(value):
        return swap(value, "tensor", 1, ranks)

    def across(value):
        return swap(value, "dp", 1, 2)

    def gather_far(value):
        pieces = {0: value}
        bit = ranks // 2
        while bit > 1:
            pieces |= {k | bit: swap(v, "tensor", bit, ranks) for k, v in pieces.items()}
            bit //= 2
        return [pieces[k] for k in range(0, ranks, 2)]

    def ordered(even, odd):
        return [v for pair in zip(even, odd) for v in pair]

    def gather_near(even, copy):
        return [near(copy)] + [near(v) for v in even[1:]]

    def scatter(name, x, weight, between=None):
        product = lambda n, received=None: term(
            f"{name}_{n}", meta, x, weight, rows_here, ranks, n, received
        )
        far_send = near(product(3))
        if between:
            between()
        far_keep = near(product(1))
        send = product(2, far_send)
        keep = product(0, far_keep)
        return finish_sum(send, keep, rows_here, ranks)

    def along(value):
        return lax.ppermute(value, "group", [(i, (i + 1) % groups) for i in range(groups)])

    def row_parts(own, far):
        return [
            part_of(v, lambda m, k=k, at=at: lax.rem(m[items + 1] + groups - k, groups) * strip + at)
            for k, both_halves in enumerate(zip(own, far)) for at, v in zip((0, half), both_halves)
        ]

    gain_pieces = [norm_gains] + [swap(norm_gains, "group", k, groups) for k in range(1, groups)]
    tall_strip = pl.BlockSpec((strip // 2, heads * 4 * HEAD_DIM), lambda i, m: (i, 0))
    strips = list(run(
        cast_heads_kernel, "cast_heads", (2,), meta, [(weight_heads, tall_strip)],
        [((strip, heads * 4 * HEAD_DIM), BF16, tall_strip)],
    ))
    strips.append(along(strips[0]))
    crossed = [across(strips[0])]
    gains, plain_gains = run(
        functools.partial(gains_kernel, items, half), "gains", (1,), meta,
        [(v, whole(v)) for v in gain_pieces],
        [((2, width), F32, both)] * 2,
        [pltpu.VMEM((groups, 2, width // groups), F32)],
    )
    first_norm, copy = run(
        functools.partial(first_norm_kernel, items, half), "first_norm", (steps,), meta,
        [(block_input, row_block), (gains, both)],
        [(row_shape, BF16, row_block)] * 2,
    )
    even_one = gather_far(first_norm)
    quarter = units // 2
    strip_block = pl.BlockSpec((strip // 2, quarter), lambda i, m: (i, 0))
    shards = run(
        cast_hidden_kernel, "cast_hidden", (2,), meta,
        [(weight_hidden, pl.BlockSpec((2, strip // 2, units), lambda i, m: (0, i, 0)))],
        [((strip, quarter), BF16, strip_block)] * 4,
    )
    odd_first = near(wait(copy, after=crossed)[0])
    back_low, back_copy = run(
        functools.partial(turn_kernel, items, half), "turn", (steps,), meta,
        [(cotangent, row_block)], [(row_shape, BF16, row_block)] * 2,
    )
    strips[1] = wait(strips[1], after=[odd_first])[0]
    strips.append(along(strips[1]))
    crossed.append(across(strips[1]))
    wait()
    strips[2] = wait(strips[2], after=crossed[1:])[0]
    strips.append(along(strips[2]))
    crossed.append(across(strips[2]))
    wait()
    even_one[1:] = wait(*even_one[1:], after=crossed[2:])
    odd_one = [odd_first] + [near(v) for v in even_one[1:]]
    strips[3] = wait(strips[3])[0]
    crossed.append(across(strips[3]))
    def gathered(shard, after=()):
        return lax.all_gather(wait(shard, after=after)[0], "group", axis=0, tiled=True)

    def columns(own, far):
        return [
            part_of(v, lambda m, at=at: at, n * quarter)
            for n in range(2) for at, v in ((0, own[n]), (half, far[n]))
        ]

    lower_own = [gathered(shards[0], odd_one[1:])]
    back_low = wait(back_low)[0]
    even_back = gather_far(back_low)
    all_one = ordered(even_one, odd_one)
    triple, heads_all = rows_matmul(
        "qkv", meta, all_one, row_parts(strips, crossed), store_rounded, [], [(BF16, same)],
        use=heads * 3 * HEAD_DIM, saved=True,
    )
    inward_w = [part_of(heads_all, columns=heads * 3 * HEAD_DIM)]
    outward_w = [part_of(heads_all, source_column=heads * 3 * HEAD_DIM)]
    lower_own.append(gathered(shards[1]))
    lower_own[0] = wait(lower_own[0])[0]
    lower_far = [across(lower_own[0])]
    pairs = 2 if heads % 2 == 0 else 1
    calls = heads // pairs
    mixed, logs = attend(meta, triple, items, rows_here, heads, pairs, 0)
    raise_own = [gathered(shards[2])]
    for n in range(1, calls):
        mixed, logs = attend(meta, triple, items, rows_here, heads, pairs, n, (mixed, logs))
    lower_own[1] = wait(lower_own[1], after=lower_far)[0]
    lower_far.append(across(lower_own[1]))
    back_copy, *even_back[1:] = wait(back_copy, *even_back[1:])
    odd_back = gather_near(even_back, back_copy)
    raise_own.append(gathered(shards[3]))
    wait(after=odd_back)
    keep, received = scatter("project", [mixed], outward_w)
    raise_own[0] = wait(raise_own[0])[0]
    raise_far = [across(raise_own[0])]
    middle, second_norm = run(
        functools.partial(second_norm_kernel, items, half), "second_norm", (steps,), meta,
        [(block_input, row_block), (keep, row_block), (received, row_block), (gains, both)],
        [(row_shape, F32, row_block), (row_shape, BF16, row_block)],
    )
    even_two = gather_far(second_norm)
    odd_first = near(second_norm)
    raise_own[1] = wait(raise_own[1])[0]
    raise_far.append(across(raise_own[1]))
    raise_w = columns(raise_own, raise_far)
    all_back = ordered(even_back, odd_back)
    back_hidden, lower_all = rows_matmul(
        "back_hidden", meta, all_back, columns(lower_own, lower_far), store_rounded, [], [(BF16, same)], saved=True
    )
    lower_w = [part_of(lower_all)]
    wait(after=[odd_first])

    def feed(pieces, first, weight, filled=(), column=0):
        return rows_matmul(
            "raise", meta, pieces, weight, store_gelu, [(back_hidden, lambda i: i + first)],
            [(BF16, lambda i: i + first)] * 2, rows=total, staged=True, filled=filled,
            block_column=column, columns=units,
        )

    filled = ()
    for n in range(2):
        unit_half = [part_of(raise_own[n]), part_of(raise_far[n], lambda m: half)]
        filled = feed([even_two[0], odd_first], 0, unit_half, filled, n)
    even_two[1:] = wait(*even_two[1:])
    odd_two = [odd_first] + [near(v) for v in even_two[1:]]
    wait()
    all_two = ordered(even_two, odd_two)
    hidden, back_before = feed(all_two[2:], 2, raise_w, filled)
    pieces = lambda values: [(v, k * rows_here) for k, v in enumerate(values)]

    def grad(name, left, right, first):
        return weight_grad(name, meta, pieces(left), right if type(right) is list else [right], first, half)

    grad_lower_far = across(grad("lower_far", all_back, hidden, half))
    keep, received = scatter("back_second", [back_before], raise_w)
    grad_raise_far = across(grad("raise_far", all_two, back_before, half))
    grad_lower = grad("lower_own", all_back, hidden, 0)
    middle_back = []

    def second_back():
        middle_back.extend(run(
            lambda meta, *refs: second_back_kernel(*refs), "second_back", (steps,), meta,
            [(v, row_block) for v in (middle, keep, received, back_low)] + [(gains, both)],
            [(row_shape, F32, row_block), ((8, width), F32, gain_block), (row_shape, BF16, row_block)],
        ))
        middle_back.append(gather_far(middle_back[2]))
        middle_back.append(near(middle_back[2]))
        middle_back.append(grad("raise_own", all_two, back_before, 0))
        wait(after=middle_back[4:5])

    out_keep, out_received = scatter("lower", [hidden], lower_w, second_back)
    back_middle, gain_second, back_low_middle, even_middle, odd_first, grad_raise = middle_back

    def summed(delta):
        return lax.psum_scatter(delta, "group", scatter_dimension=0, tiled=True)

    def adam_hidden(name, own, far, weight, part, filled=()):
        moment, square, delta = adam(
            name, meta, items, side_by_side, [(own, units, 0)], [(far, units, 0)],
            [(v, v.shape[1], 0) for v in weight],
            first_hidden, second_hidden, part, filled=filled,
        )
        return moment, square, summed(delta)

    *states, lower_delta = adam_hidden("adam_lower", grad_lower, grad_lower_far, [lower_all], 1)
    even_middle[1:] = wait(*even_middle[1:])
    odd_middle = [odd_first] + [near(v) for v in even_middle[1:]]
    wait()

    all_middle = ordered(even_middle, odd_middle)
    back_mixed = rows_matmul("back_mixed", meta, all_middle, outward_w, store_rounded, [], [(BF16, same)])[0]
    grad_out_far = across(grad("out_far", all_middle, mixed, half))
    moment_hidden, square_hidden, raise_delta = adam_hidden(
        "adam_raise", grad_raise, grad_raise_far, raise_own, 0, tuple(states)
    )
    back_triples, grad_in_fars = [], []
    for n in range(calls):
        back_triples.append(
            attend_back(meta, triple, mixed, back_mixed, logs, items, rows_here, heads, pairs, n)
        )
        grad_in_fars.append(across(grad("in_far", all_one, back_triples[n], half)))
        if n == 0:
            grad_out = grad("out_own", all_middle, mixed, 0)
            block_output = run(
                functools.partial(output_kernel, items, half), "output", (steps,), meta,
                [(v, row_block) for v in (middle, out_keep, out_received)],
                [(row_shape, BF16, row_block)],
            )[0]
            hidden_out = outer(
                "outer_lower", meta, groups, [lower_delta], weight_hidden, momentum_hidden, average_hidden, 1
            )
    product = lambda n, received=None: term(
        f"back_first_{n}", meta, back_triples, inward_w, rows_here, ranks, n, received
    )
    far_send = near(product(3))
    far_keep = near(product(1))
    send = product(2, far_send)
    grad_in = grad("in_own", all_one, back_triples, 0)
    in_wide, out_wide = pairs * 3 * HEAD_DIM, heads * HEAD_DIM
    moment_heads, square_heads, *deltas = adam(
        "adam_heads", meta, items, by_head,
        [(grad_in, calls * in_wide, 0), (grad_out, out_wide, 0)],
        [(v, in_wide, 0) for v in grad_in_fars] + [(grad_out_far, out_wide, 0)],
        [(heads_all, calls * in_wide, 0), (heads_all, out_wide, 3)],
        first_heads[:, None], second_heads[:, None], 0, groups,
    )
    heads_deltas = [deltas[0]] + [
        lax.ppermute(deltas[k], "group", [(i, (i + k) % groups) for i in range(groups)])
        for k in range(1, groups)
    ]
    keep = product(0, far_keep)
    keep, received = finish_sum(send, keep, rows_here, ranks)
    input_grad, gain_first = run(
        functools.partial(first_back_kernel, items, half), "first_back", (steps,), meta,
        [(block_input, row_block), (gains, both)] + [(v, row_block) for v in (back_middle, keep, received)],
        [(row_shape, F32, row_block), ((8, width), F32, gain_block)],
    )
    gain_grad = run(
        functools.partial(gain_total_kernel, items, half), "gain_total", (1,), meta,
        [(v, whole(v)) for v in (gain_first, gain_second)],
        [((2, width), F32, both)],
    )[0]

    def added(value, other):
        return run(
            add_kernel, "add", (1,), meta, [(value, whole(value)), (other, whole(other))],
            [(value.shape, F32, whole(value))],
        )[0]

    far_gain = across(gain_grad)
    wait()
    gain_grad = added(gain_grad, far_gain)
    bit = 1
    while bit < ranks:
        far_gain = swap(gain_grad, "tensor", bit, ranks)
        wait()
        gain_grad = added(gain_grad, far_gain)
        bit *= 2
    moment_gains, square_gains, delta_gains = adam_math(
        plain_gains, gain_grad, first_gains[0], second_gains[0], GAIN_RATE, 0.0
    )
    short = width // groups

    def gain_part(k):
        return lax.dynamic_slice_in_dim(delta_gains, (group ^ k) * short, short, 1)

    change_gains = gain_part(0)
    for k in range(1, groups):
        change_gains = change_gains + swap(gain_part(k), "group", k, groups)
    change_gains = change_gains / groups
    velocity_gains, trail_gains, master_gains = outer_math(
        norm_gains, change_gains, momentum_gains, average_gains
    )
    change_hidden, velocity_hidden, trail_hidden, master_hidden, copy_hidden = outer(
        "outer_raise", meta, groups, [raise_delta], weight_hidden, momentum_hidden, average_hidden, 0,
        filled=hidden_out,
    )
    change_heads, velocity_heads, trail_heads, master_heads, copy_heads = (
        v[0]
        for v in outer(
            "outer_heads", meta, groups, heads_deltas, weight_heads[None], momentum_heads[None],
            average_heads[None], 0,
        )
    )
    return (
        block_output,
        input_grad,
        moment_heads[:, 0],
        moment_hidden,
        moment_gains[None],
        square_heads[:, 0],
        square_hidden,
        square_gains[None],
        change_heads,
        change_hidden,
        change_gains,
        velocity_heads,
        velocity_hidden,
        velocity_gains,
        trail_heads,
        trail_hidden,
        trail_gains,
        master_heads,
        master_hidden,
        master_gains,
        copy_heads,
        copy_hidden,
    )


def solution(mesh):
    rows = P(("group", "dp", "tensor"), None)
    heads, hidden, gains = P(("dp", "group"), "tensor"), P(None, ("dp", "group"), "tensor"), P(None, "group")
    states = (P("group", "dp", "tensor"), P("group", None, "dp", "tensor"), P("group", None, None))
    in_specs = (rows, rows, P(("group", "dp"), None)) + (heads, hidden, gains) * 3 + states * 2
    out_specs = (rows, rows) + states * 2 + (heads, hidden, gains) * 4 + (heads, hidden)
    return jax.shard_map(local, mesh=mesh, in_specs=in_specs, out_specs=out_specs, check_vma=False)
```

```python
import functools
import math

import jax
import jax.numpy as jnp
from jax import lax
from jax.experimental import pallas as pl
from jax.experimental.pallas import tpu as pltpu
from jax.sharding import PartitionSpec as P

HEAD_DIM = 128
STEP = 8

NORM_EPS = 1e-05
INNER_RATE = 0.02
GAIN_RATE = 0.5
BETA_ONE = 0.9
BETA_TWO = 0.95
ADAM_EPS = 1e-08
WEIGHT_DECAY = 0.1
OUTER_RATE = 0.7
OUTER_MOMENTUM = 0.9
EMA_KEEP = 0.5

BF16 = jnp.bfloat16
F32 = jnp.float32
SCALE = HEAD_DIM ** (-0.5)
LOG2E = math.log2(math.e)
SCALE_LOG2 = SCALE * LOG2E
NEGATIVE = -1e30


def swap(value, axis, bit, size):
    return lax.ppermute(value, axis, [(i, i ^ bit) for i in range(size)])


ANYWHERE = pl.BlockSpec(memory_space=pl.ANY)
LIMIT = 60 * 2**20
line = []


def run(kernel, name, grid, meta, ins, outs, scratch=(), after=(), alias=None):
    arrays = [a for a, _ in ins]
    extra = [a for a in line + list(after) if all(a is not b for b in arrays)]
    count, skip = len(ins), len(extra)

    def body(*refs):
        kernel(*refs[: 1 + count], *refs[1 + count + skip :])

    result = pl.pallas_call(
        body,
        grid_spec=pltpu.PrefetchScalarGridSpec(
            num_scalar_prefetch=1,
            grid=grid,
            in_specs=[s for _, s in ins] + [ANYWHERE] * skip,
            out_specs=[s for _, _, s in outs],
            scratch_shapes=list(scratch),
        ),
        out_shape=[jax.ShapeDtypeStruct(s, d) for s, d, _ in outs],
        input_output_aliases={1 + a: b for a, b in (alias or {}).items()},
        compiler_params=pltpu.CompilerParams(vmem_limit_bytes=LIMIT),
        cost_estimate=pl.CostEstimate(flops=10**12, bytes_accessed=1, transcendentals=0),
        name=name,
    )(meta, *arrays, *extra)
    line[:] = [result[0]]
    return result


def dot_last(left, right):
    return lax.dot_general(
        left, right, (((1,), (1,)), ((), ())), preferred_element_type=F32
    )


def dot_first(left, right):
    return lax.dot_general(
        left, right, (((0,), (0,)), ((), ())), preferred_element_type=F32
    )


def dot(left, right):
    return jnp.dot(left, right, preferred_element_type=F32)


def normalize(rows):
    mean = jnp.mean(rows, axis=-1, keepdims=True)
    centred = rows - mean
    var = jnp.mean(centred * centred, axis=-1, keepdims=True)
    inverse = lax.rsqrt(var + NORM_EPS)
    return centred * inverse, inverse


def normalize_back(back, normed, inverse, gain):
    scaled = back * gain
    first = jnp.mean(scaled, axis=-1, keepdims=True)
    second = jnp.mean(scaled * normed, axis=-1, keepdims=True)
    terms = (back * normed).reshape(-1, 8, back.shape[-1])
    return inverse * (scaled - first - normed * second), jnp.sum(terms, axis=0)


def gelu_parts(u):
    size = jnp.abs(u) * (0.5**0.5)
    t = 1.0 / (1.0 + 0.3275911 * size)
    poly = t * (
        0.254829592
        + t * (-0.284496736 + t * (1.421413741 + t * (-1.453152027 + t * 1.061405429)))
    )
    bell = jnp.exp(-0.5 * u * u)
    tail = 0.5 * poly * bell
    below = jnp.where(u >= 0.0, 1.0 - tail, tail)
    return below, bell * (1.0 / math.sqrt(2.0 * math.pi))


def item_start(places, meta, items):
    start = jnp.zeros_like(places)
    for k in range(items):
        start = jnp.where(places >= meta[k], meta[k], start)
    return start


def copy_in(meta, items, source, target, rows, step, total):
    for s in range(total // step):
        owner, offset = (s * step) // rows, (s * step) % rows
        local = pl.multiple_of((owner ^ meta[items]) * rows + offset, step)
        target[s * step : (s + 1) * step, :] = source[pl.ds(local, step), :]


def local_row(meta, items, chunk, rows, step):
    per = rows // step
    owner, offset = chunk // per, chunk % per
    return pl.multiple_of((owner ^ meta[items]) * rows + offset * step, step)


def head_columns(n, c):
    return slice((3 * n + c) * HEAD_DIM, (3 * n + c + 1) * HEAD_DIM)


def attend_kernel(items, rows, step, block, pairs, meta, qkv, *refs):
    mixed, logs, nat, values, acc, top = refs[-6:]
    total = qkv.shape[0]
    index = pl.program_id(0)

    @pl.when(index == 0)
    def _():
        copy_in(meta, items, qkv, nat, rows, step, total)
        for n in range(pairs):
            values[n, :, 0:HEAD_DIM] = nat[:, head_columns(n, 2)]
            values[n, :, HEAD_DIM:] = jnp.ones((total, HEAD_DIM), BF16)

    first_row = index * block
    acc[...] = jnp.zeros_like(acc)
    top[...] = jnp.full_like(top, NEGATIVE)
    low_start = item_start(first_row, meta, items)
    high_start = item_start(first_row + block - 1, meta, items)

    def tile(j, masked, keys=block, low=0, high=block):
        at = pl.ds(pl.multiple_of(j * block, block), keys)
        here = pl.ds(pl.multiple_of(first_row + low, math.gcd(block, low)), high - low)
        own = slice(low, high)
        if masked:
            q_place = first_row + low + lax.broadcasted_iota(jnp.int32, (high - low, 1), 0)
            k_place = j * block + lax.broadcasted_iota(jnp.int32, (1, keys), 1)
            live = (k_place <= q_place) & (k_place >= item_start(q_place, meta, items))
        scores = [dot_last(nat[here, head_columns(n, 0)], nat[at, head_columns(n, 1)]) for n in range(pairs)]
        for n in range(pairs):
            s = jnp.where(live, scores[n], NEGATIVE) if masked else scores[n]
            old = top[n, own, :]
            new = jnp.maximum(old, jnp.max(s, axis=1, keepdims=True))
            p = jnp.exp2((s - jnp.concatenate([new] * (keys // HEAD_DIM), axis=1)) * SCALE_LOG2)
            keep = jnp.exp2((old - new) * SCALE_LOG2)
            top[n, own, :] = new
            acc[n, own, :] = acc[n, own, :] * jnp.concatenate([keep, keep], axis=1) + dot(
                p.astype(BF16), values[n, at, :]
            )

    @pl.loop(low_start // block, index)
    def _(j):
        whole = high_start <= j * block

        @pl.when(whole)
        def _():
            tile(j, False)

        @pl.when(jnp.logical_not(whole))
        def _():
            tile(j, True)

    middle = block // 2
    tile(index, True, middle, 0, middle)
    tile(index, True, block, middle, block)
    per = block // step
    for n in range(pairs):
        weight = acc[n, :, HEAD_DIM:]
        out = (acc[n, :, 0:HEAD_DIM] / weight).astype(BF16)
        for c in range(per):
            at = local_row(meta, items, index * per + c, rows, step)
            mixed[pl.ds(at, step), n * HEAD_DIM : (n + 1) * HEAD_DIM] = out[c * step : (c + 1) * step, :]
        log = top[n] * SCALE_LOG2 + jnp.log(weight) * LOG2E
        logs[n, 0] = log.T[0:8, :]


def attend(meta, qkv, items, rows, heads, pairs, call, filled=(), after=()):
    total = qkv.shape[0]
    block = min(512, total)
    step = math.gcd(rows, block)
    count = total // block
    return run(
        functools.partial(attend_kernel, items, rows, step, block, pairs),
        "attend",
        (count,),
        meta,
        [(qkv, pl.BlockSpec((total, pairs * 3 * HEAD_DIM), lambda i, m: (0, call)))]
        + [(v, ANYWHERE) for v in filled],
        [
            ((total, heads * HEAD_DIM), BF16, pl.BlockSpec((total, pairs * HEAD_DIM), lambda i, m: (0, call))),
            ((heads, count, 8, block), F32, pl.BlockSpec((pairs, 1, 8, block), lambda i, m: (call, i, 0, 0))),
        ],
        [
            pltpu.VMEM((total, pairs * 3 * HEAD_DIM), BF16),
            pltpu.VMEM((pairs, total, 2 * HEAD_DIM), BF16),
            pltpu.VMEM((pairs, block, 2 * HEAD_DIM), F32),
            pltpu.VMEM((pairs, block, HEAD_DIM), F32),
        ],
        after,
        {1 + n: n for n in range(len(filled))},
    )


def attend_back_kernel(
    items, rows, step, block, pairs, meta, qkv, mixed, back, logs, grads, nat, nat_mixed, nat_back, dq, dk, dv
):
    total = qkv.shape[0]
    index = pl.program_id(0)
    own = [slice(n * HEAD_DIM, (n + 1) * HEAD_DIM) for n in range(pairs)]

    @pl.when(index == 0)
    def _():
        copy_in(meta, items, qkv, nat, rows, step, total)
        copy_in(meta, items, mixed, nat_mixed, rows, step, total)
        copy_in(meta, items, back, nat_back, rows, step, total)
        dk[...] = jnp.zeros_like(dk)
        dv[...] = jnp.zeros_like(dv)

    first_row = index * block
    here = pl.ds(pl.multiple_of(first_row, block), block)
    row_terms = []
    for n in range(pairs):
        product = nat_back[here, own[n]].astype(F32) * nat_mixed[here, own[n]].astype(F32)
        row_terms.append(jnp.sum(product.T, axis=0, keepdims=True))
    dq[...] = jnp.zeros_like(dq)
    low_start = item_start(first_row, meta, items)
    high_start = item_start(first_row + block - 1, meta, items)

    def tile(j, masked, low=0, high=block):
        at = pl.ds(pl.multiple_of(j * block + low, math.gcd(block, low)), high - low)
        here = pl.ds(pl.multiple_of(first_row + low, math.gcd(block, low)), block - low)
        mine = slice(low, block)
        if masked:
            k_place = j * block + low + lax.broadcasted_iota(jnp.int32, (high - low, 1), 0)
            q_place = first_row + mine.start + lax.broadcasted_iota(jnp.int32, (1, block - mine.start), 1)
            live = (k_place <= q_place) & (k_place >= item_start(q_place, meta, items))
        scores = [dot_last(nat[at, head_columns(n, 1)], nat[here, head_columns(n, 0)]) for n in range(pairs)]
        backs = [dot_last(nat[at, head_columns(n, 2)], nat_back[here, own[n]]) for n in range(pairs)]
        for n in range(pairs):
            p = jnp.exp2(scores[n] * SCALE_LOG2 - logs[n, 0, 0:1, mine])
            if masked:
                p = jnp.where(live, p, 0.0)
            s = (p * (backs[n] - row_terms[n][:, mine])).astype(BF16)
            dv[at, own[n]] += dot(p.astype(BF16), nat_back[here, own[n]])
            dk[at, own[n]] += dot(s, nat[here, head_columns(n, 0)])
            dq[mine, own[n]] += dot_first(s, nat[at, head_columns(n, 1)])

    @pl.loop(low_start // block, index)
    def _(j):
        whole = high_start <= j * block

        @pl.when(whole)
        def _():
            tile(j, False)

        @pl.when(jnp.logical_not(whole))
        def _():
            tile(j, True)

    middle = block // 2
    tile(index, True, 0, middle)
    tile(index, True, middle, block)
    per = block // step
    for n in range(pairs):
        out = (dq[:, own[n]] * SCALE).astype(BF16)
        for c in range(per):
            to = local_row(meta, items, index * per + c, rows, step)
            grads[pl.ds(to, step), head_columns(n, 0)] = out[c * step : (c + 1) * step, :]

    @pl.when(index == pl.num_programs(0) - 1)
    def _():
        for s in range(total // step):
            to = local_row(meta, items, s, rows, step)
            part = slice(s * step, (s + 1) * step)
            for n in range(pairs):
                grads[pl.ds(to, step), head_columns(n, 1)] = (dk[part, own[n]] * SCALE).astype(BF16)
                grads[pl.ds(to, step), head_columns(n, 2)] = dv[part, own[n]].astype(BF16)


def attend_back(meta, qkv, mixed, back, logs, items, rows, heads, pairs, call, after=()):
    total = qkv.shape[0]
    block = logs.shape[-1]
    step = math.gcd(rows, block)
    count = total // block
    wide = pl.BlockSpec((total, pairs * 3 * HEAD_DIM), lambda i, m: (0, call))
    narrow = pl.BlockSpec((total, pairs * HEAD_DIM), lambda i, m: (0, call))
    return run(
        functools.partial(attend_back_kernel, items, rows, step, block, pairs),
        "attend_back",
        (count,),
        meta,
        [
            (qkv, wide),
            (mixed, narrow),
            (back, narrow),
            (logs, pl.BlockSpec((pairs, 1, 8, block), lambda i, m: (call, i, 0, 0))),
        ],
        [((total, pairs * 3 * HEAD_DIM), BF16, pl.BlockSpec((total, pairs * 3 * HEAD_DIM), lambda i, m: (0, 0)))],
        [
            pltpu.VMEM((total, pairs * 3 * HEAD_DIM), BF16),
            pltpu.VMEM((total, pairs * HEAD_DIM), BF16),
            pltpu.VMEM((total, pairs * HEAD_DIM), BF16),
            pltpu.VMEM((block, pairs * HEAD_DIM), F32),
            pltpu.VMEM((total, pairs * HEAD_DIM), F32),
            pltpu.VMEM((total, pairs * HEAD_DIM), F32),
        ],
        after,
    )[0]


TILE = 512


def tile_of(size):
    return next(tile for tile in (min(TILE, size), 256, 128) if size % tile == 0)


def part_of(array, row=lambda m: 0, column=0, source_row=0, rows=None, source_column=0, columns=None):
    rows, columns = rows or array.shape[0] - source_row, columns or array.shape[1] - source_column
    return array, (row, column, source_row, rows, source_column, columns)


class Pieces:
    def __init__(self, refs, places, dim, target, sems, meta, tile=None):
        self.refs, self.places, self.dim, self.target, self.sems, self.meta = refs, places, dim, target, sems, meta
        self.tile = tile or tile_of(target.shape[dim])

    def span(self, p):
        row, column, _, rows, _, columns = self.places[p]
        first, size = (column, columns) if self.dim else (row(None), rows)
        return first // self.tile, size // self.tile

    def copy(self, p, n):
        row, column, source_row, rows, source_column, columns = self.places[p]
        tile = self.tile
        at = (n - self.span(p)[0]) * tile + (source_column if self.dim else source_row)
        at = pl.ds(pl.multiple_of(at, math.gcd(tile, source_column if self.dim else source_row)), tile)
        to = pl.ds(pl.multiple_of(n * tile, tile), tile)
        if self.dim:
            source = self.refs[p].at[pl.ds(source_row, rows), at]
            target = self.target.at[pl.ds(pl.multiple_of(row(self.meta), math.gcd(rows, TILE)), rows), to]
        else:
            source = self.refs[p].at[at, pl.ds(source_column, columns)]
            target = self.target.at[to, pl.ds(column, columns)]
        return pltpu.make_async_copy(source, target, self.sems.at[p, n])

    def start(self):
        for n in range(self.target.shape[self.dim] // self.tile):
            for p in range(len(self.refs)):
                first, count = self.span(p)
                if first <= n < first + count:
                    self.copy(p, n).start()

    def wait(self, n):
        for p in range(len(self.refs)):
            first, count = self.span(p)
            if isinstance(n, int):
                if first <= n < first + count:
                    self.copy(p, n).wait()
            elif first == 0 and count == self.target.shape[self.dim] // self.tile:
                self.copy(p, n).wait()
            else:

                @pl.when((n >= first) & (n < first + count))
                def _(p=p):
                    self.copy(p, n).wait()


def tiles_of(size):
    return size // tile_of(size)


def rows_kernel(count, places, use, saved, finish, staged, filled, meta, *refs):
    parts = len(places)
    pieces, strips, refs = refs[:count], refs[count : count + parts], refs[count + parts :]
    stages = refs[len(refs) - staged :]
    refs = refs[: len(refs) - staged]
    blocks, (slots, weight, piece_sems, weight_sems) = refs[:-4], refs[-4:]
    i = pl.program_id(0)
    parts = Pieces(strips, places, 1, weight, weight_sems, meta)

    def fetch(n):
        return pltpu.make_async_copy(pieces[n], slots.at[n % 2], piece_sems.at[n % 2])

    @pl.when(i == 0)
    def _():
        fetch(0).start()
        parts.start()

    for n in range(1, count):

        @pl.when(i + 1 == n)
        def _(n=n):
            fetch(n).start()

    for n in range(count):

        @pl.when(i == n)
        def _(n=n):
            fetch(n).wait()

    wide = tile_of(use)
    many, loaded = use // wide, weight.shape[1] // parts.tile
    early = wide != parts.tile
    if early or staged:

        @pl.when(i == 0)
        def _():
            for n in range(loaded):
                parts.wait(n)

    if staged:
        blocks = blocks[: len(blocks) - 2 - saved - filled] + blocks[len(blocks) - 2 - saved :]
        x = slots[i % 2]
        for n in range(many + 1):
            if n < many:
                stages[n % 2][...] = dot(x, weight[:, n * wide : (n + 1) * wide])
            if n:
                finish(
                    stages[(n - 1) % 2][...], slice((n - 1) * wide, n * wide), *blocks[: len(blocks) - saved]
                )
    else:

        @pl.loop(0, many)
        def _(n):
            if not early:

                @pl.when(i == 0)
                def _():
                    parts.wait(n)

            at = pl.ds(pl.multiple_of(n * wide, wide), wide)
            finish(dot(slots[i % 2], weight[:, at]), at, *blocks[: len(blocks) - saved])

        if not early and loaded > many:

            @pl.when(i == 0)
            def _():
                for n in range(many, loaded):
                    parts.wait(n)

    if saved:
        kept = blocks[-1]
        kept[...] = weight[pl.ds(pl.multiple_of(i * kept.shape[0], kept.shape[0]), kept.shape[0]), :]


def rows_matmul(
    name, meta, pieces, weight, finish, extra, outs, use=None, rows=None, saved=False, staged=False, filled=(),
    block_column=0, columns=None, after=()
):
    strips, places = zip(*weight)
    tall, depth = pieces[0].shape
    wide = max(place[1] + place[5] for place in places)
    use = use or wide
    count, parts = len(pieces), len(strips)
    block = lambda index: pl.BlockSpec((tall, use), lambda i, m: (index(i), block_column))
    more = [((depth, wide), BF16, pl.BlockSpec((depth // count, wide), lambda i, m: (i, 0)))] if saved else []
    ins = [(p, ANYWHERE) for p in pieces] + [(p, ANYWHERE) for p in strips] + [(a, block(f)) for a, f in extra]
    return run(
        functools.partial(rows_kernel, count, places, use, saved, finish, 2 * staged, len(filled)),
        name,
        (count,),
        meta,
        ins + [(v, ANYWHERE) for v in filled],
        [((rows or count * tall, columns or use), d, block(f)) for d, f in outs] + more,
        [
            pltpu.VMEM((2, tall, depth), BF16),
            pltpu.VMEM((depth, wide), BF16),
            pltpu.SemaphoreType.DMA((2,)),
            pltpu.SemaphoreType.DMA((parts, tiles_of(wide))),
        ]
        + [pltpu.VMEM((tall, tile_of(use)), F32)] * (2 * staged),
        after,
        {len(ins) + n: n for n in range(len(filled))},
    )


def store_rounded(value, at, out):
    out[:, at] = value.astype(BF16)


def store_gelu(value, at, back, hidden, back_before):
    below, density = gelu_parts(value)
    hidden[:, at] = (value * below).astype(BF16)
    back_before[:, at] = (back[:, at].astype(F32) * (below + value * density)).astype(BF16)


def same(i):
    return i


def term_kernel(count, places, offset, part, meta, *refs):
    x, strips, refs = refs[:count], refs[count : count + len(places)], refs[count + len(places) :]
    received = refs[0] if len(refs) == 11 else None
    out, held, extra, tiles, weight, x_sems, extra_sems, tile_sems, sems, _ = refs[-10:]
    i = pl.program_id(0)
    parts = Pieces(strips, places, 0, weight, sems, meta)
    wide = parts.tile
    many = weight.shape[0] // wide
    own_rows = pl.ds(pl.multiple_of((4 * i + offset) * part, part), part)
    out_rows = pl.ds(pl.multiple_of(i * part, part), part)

    def load_x(n):
        at = sum(v.shape[1] for v in x[:n])
        to = held.at[:, at : at + x[n].shape[1]]
        return pltpu.make_async_copy(x[n].at[own_rows, :], to, x_sems.at[n])

    def load_extra(n):
        at = pl.ds(pl.multiple_of(n * wide, wide), wide)
        return pltpu.make_async_copy(received.at[out_rows, at], extra.at[n], extra_sems.at[n])

    def put(n):
        at = pl.ds(pl.multiple_of(n * wide, wide), wide)
        return pltpu.make_async_copy(tiles.at[n % 2], out.at[out_rows, at], tile_sems.at[n % 2])

    for n in range(count):
        load_x(n).start()

    @pl.when(i == 0)
    def _():
        parts.start()

    if received is not None:
        for n in range(many):
            load_extra(n).start()
    for n in range(count):
        load_x(n).wait()

    @pl.loop(0, many)
    def _(n):
        @pl.when(i == 0)
        def _():
            parts.wait(n)

        if received is not None:
            load_extra(n).wait()

        @pl.when(n > 1)
        def _():
            put(n - 2).wait()

        at = pl.ds(pl.multiple_of(n * wide, wide), wide)
        value = dot_last(held[...], weight[at, :])
        if received is not None:
            value = value + extra[n].astype(F32)
        tiles[n % 2] = value.astype(BF16)
        put(n).start()

    for n in range(max(many - 2, 0), many):
        put(n).wait()


def term(name, meta, x, weight, part, ranks, offset, received=None, after=()):
    strips, places = zip(*weight)
    n = sum(v.shape[1] for v in x)
    width = max(place[0](None) + place[3] for place in places)
    many, wide = tiles_of(width), tile_of(width)
    rows = ranks // 4 * part
    return run(
        functools.partial(term_kernel, len(x), places, offset, part),
        name,
        (ranks // 4,),
        meta,
        [(v, ANYWHERE) for v in x]
        + [(s, ANYWHERE) for s in strips]
        + ([] if received is None else [(received, ANYWHERE)]),
        [((rows, width), BF16, ANYWHERE)],
        [
            pltpu.VMEM((part, n), BF16),
            pltpu.VMEM((many, part, wide), BF16),
            pltpu.VMEM((2, part, wide), BF16),
            pltpu.VMEM((width, n), BF16),
            pltpu.SemaphoreType.DMA((len(x),)),
            pltpu.SemaphoreType.DMA((many,)),
            pltpu.SemaphoreType.DMA((2,)),
            pltpu.SemaphoreType.DMA((len(strips), many)),
            pltpu.SMEM((1,), jnp.int32),
        ],
        after,
    )[0]


def finish_sum(send, keep, part, ranks):
    bit = 2
    while True:
        received = swap(send, "tensor", bit, ranks)
        if keep.shape[0] == part:
            return keep, received
        total = (keep.astype(F32) + received.astype(F32)).astype(BF16).reshape(-1, 2, part, keep.shape[1])
        keep, send = (total[:, n].reshape(-1, keep.shape[1]) for n in (0, 1))
        bit *= 2


def weight_grad_kernel(rows_a, columns, first, meta, *refs):
    count, many = len(rows_a), len(columns)
    left, right, (out, slots, held, left_sems, right_sems) = (
        refs[:count], refs[count : count + many], refs[count + many :]
    )
    i = pl.program_id(0)
    steps = pl.num_programs(0)
    wide = slots.shape[2]
    places = [part_of(v, column=at)[1] for v, at in zip(right, columns)]
    loads = tile_of(right[0].shape[1])
    parts = Pieces(right, places, 1, held, right_sems, meta, loads)
    tile = tile_of(held.shape[1])

    def fetch(step, slot):
        at = pl.ds(pl.multiple_of(first + step * wide, wide), wide)
        return [
            pltpu.make_async_copy(ref.at[:, at], slots.at[slot, pl.ds(row, ref.shape[0])], left_sems.at[slot, n])
            for n, (ref, row) in enumerate(zip(left, rows_a))
        ]

    @pl.when(i == 0)
    def _():
        for copy in fetch(0, 0):
            copy.start()
        parts.start()

    @pl.when(i + 1 < steps)
    def _():
        for copy in fetch(i + 1, (i + 1) % 2):
            copy.start()

    for copy in fetch(i, i % 2):
        copy.wait()

    @pl.loop(0, held.shape[1] // tile)
    def _(n):
        @pl.when(i == 0)
        def _():
            for m in range(tile // loads):
                parts.wait(n * (tile // loads) + m)

        at = pl.ds(pl.multiple_of(n * tile, tile), tile)
        out[:, at] = dot_first(slots[i % 2], held[:, at]).astype(BF16)


def weight_grad(name, meta, left, right, first, half, after=()):
    wide = min(512, half)
    columns, n = [], 0
    for v in right:
        columns.append(n)
        n += v.shape[1]
    total = right[0].shape[0]
    return run(
        functools.partial(weight_grad_kernel, [r for _, r in left], columns, first),
        name,
        (half // wide,),
        meta,
        [(a, ANYWHERE) for a, _ in left] + [(v, ANYWHERE) for v in right],
        [((half, n), BF16, pl.BlockSpec((wide, n), lambda i, m: (i, 0)))],
        [
            pltpu.VMEM((2, total, wide), BF16),
            pltpu.VMEM((total, n), BF16),
            pltpu.SemaphoreType.DMA((2, len(left))),
            pltpu.SemaphoreType.DMA((len(right), n // tile_of(right[0].shape[1]))),
        ],
        after,
    )[0]


def strip_at(p, place, strip):
    return pl.ds(pl.multiple_of((p ^ place) * strip, strip), strip)


def turned(ref, place, strip):
    return jnp.concatenate([ref[:, strip_at(p, place, strip)] for p in range(ref.shape[1] // strip)], axis=1)


def store_turned(ref, value, place, strip):
    for p in range(value.shape[1] // strip):
        ref[:, strip_at(p, place, strip)] = value[:, p * strip : (p + 1) * strip].astype(ref.dtype)


def gains_kernel(items, strip, meta, *refs):
    pieces, (turned_out, plain, stack) = refs[:-3], refs[-3:]
    groups, short = len(pieces), pieces[0].shape[1]
    for k in range(groups):
        stack[k] = pieces[k][...]
    for j in range(groups):
        plain[:, j * short : (j + 1) * short] = stack[j ^ meta[items + 1]]
    turned_out[...] = turned(plain, meta[items + 2], strip)


def cast_heads_kernel(meta, weight, *outs):
    heads = weight.shape[1] // (4 * HEAD_DIM)
    for out in outs:
        for h in range(heads):
            at, near, far = 4 * h * HEAD_DIM, 3 * h * HEAD_DIM, (3 * heads + h) * HEAD_DIM
            out[:, near : near + 3 * HEAD_DIM] = weight[:, at : at + 3 * HEAD_DIM].astype(BF16)
            out[:, far : far + HEAD_DIM] = weight[:, at + 3 * HEAD_DIM : at + 4 * HEAD_DIM].astype(BF16)


def cast_hidden_kernel(meta, weight, *outs):
    for n, out in enumerate(outs):
        wide = out.shape[1]
        out[...] = weight[int(n < 2), :, n % 2 * wide : (n % 2 + 1) * wide].astype(BF16)


def first_norm_kernel(items, strip, meta, rows, gains, *outs):
    normed, _ = normalize(turned(rows, meta[items + 2], strip).astype(F32))
    for out in outs:
        out[...] = (normed * gains[0:1, :]).astype(BF16)


def turn_kernel(items, strip, meta, rows, *outs):
    for out in outs:
        out[...] = turned(rows, meta[items + 2], strip)


def add_kernel(meta, left, right, out):
    out[...] = left[...] + right[...]


def second_norm_kernel(items, strip, meta, rows, keep, received, gains, middle_out, *outs):
    middle = turned(rows, meta[items + 2], strip).astype(F32) + (
        keep[...].astype(F32) + received[...].astype(F32)
    )
    normed, _ = normalize(middle)
    middle_out[...] = middle
    for out in outs:
        out[...] = (normed * gains[1:2, :]).astype(BF16)


def second_back_kernel(middle, keep, received, back, gains, out, gain_out, *lows):
    normed, inverse = normalize(middle[...])
    given = keep[...].astype(F32) + received[...].astype(F32)
    grad, gain_part = normalize_back(given, normed, inverse, gains[1:2, :])
    grad = grad + back[...].astype(F32)
    out[...] = grad
    for low in lows:
        low[...] = grad.astype(BF16)

    @pl.when(pl.program_id(0) == 0)
    def _():
        gain_out[...] = jnp.zeros_like(gain_out)

    gain_out[...] += gain_part


def first_back_kernel(items, strip, meta, rows, gains, back, keep, received, out, gain_out):
    place = meta[items + 2]

    @pl.when(pl.program_id(0) == 0)
    def _():
        gain_out[...] = jnp.zeros_like(gain_out)

    normed, inverse = normalize(turned(rows, place, strip).astype(F32))
    given = keep[...].astype(F32) + received[...].astype(F32)
    grad, gain_part = normalize_back(given, normed, inverse, gains[0:1, :])
    gain_out[...] += gain_part
    store_turned(out, grad + back[...], place, strip)


def output_kernel(items, strip, meta, middle, keep, received, out):
    value = middle[...] + (keep[...].astype(F32) + received[...].astype(F32))
    store_turned(out, value, meta[items + 2], strip)


def gain_total_kernel(items, strip, meta, first, second, out):
    both = [jnp.sum(v, axis=0, keepdims=True) for v in (first[...], second[...])]
    store_turned(out, jnp.concatenate(both, axis=0), meta[items + 2], strip)


def adam_math(weight, grad, first, second, rate, decay):
    first = BETA_ONE * first + (1.0 - BETA_ONE) * grad
    second = BETA_TWO * second + (1.0 - BETA_TWO) * grad * grad
    scaled_first = first * (1.0 / (1.0 - BETA_ONE**STEP))
    scaled_second = second * (1.0 / (1.0 - BETA_TWO**STEP))
    update = scaled_first / (jnp.sqrt(scaled_second) + ADAM_EPS) + decay * weight
    return first, second, rate * update


def adam_kernel(join, counts, groups, per, items, meta, *refs):
    parts, at = [], 0
    for count in counts:
        parts.append(join([r[...].astype(F32) for r in refs[at : at + count]]))
        at += count
    own, far, weight = parts
    first, second = refs[at : at + 2]
    moment, square, *deltas = refs[-2 - groups :]
    moment[...], square[...], change = adam_math(
        weight, own + far, first[...], second[...], INNER_RATE, WEIGHT_DECAY
    )
    change = change.astype(BF16)
    if groups == 1:
        deltas[0][...] = change
    else:
        step = lax.rem(pl.program_id(0) // per + groups - meta[items + 1], groups)
        for k in range(groups):

            @pl.when(step == k)
            def _(k=k):
                deltas[k][...] = change


def side_by_side(parts):
    return parts[0] if len(parts) == 1 else jnp.concatenate(parts, axis=1)


def by_head(parts):
    *inward, outward = parts
    out, h = [], 0
    for part in inward:
        for n in range(part.shape[1] // (3 * HEAD_DIM)):
            out += [
                part[:, n * 3 * HEAD_DIM : (n + 1) * 3 * HEAD_DIM],
                outward[:, h * HEAD_DIM : (h + 1) * HEAD_DIM],
            ]
            h += 1
    return jnp.concatenate(out, axis=1)


def adam(name, meta, items, join, own, far, weight, first, second, part, groups=1, filled=(), after=()):
    rows, columns = first.shape[2:]
    tall = min(128, rows // groups)
    per = rows // groups // tall
    state = pl.BlockSpec((None, None, tall, columns), lambda i, m: (0, part, i, 0))

    def delta_block(k):
        def index(i, m):
            return (i if groups == 1 else jnp.clip(i - lax.rem(m[items + 1] + k, groups) * per, 0, per - 1), 0)

        return ((rows // groups, columns), BF16, pl.BlockSpec((tall, columns), index))

    ins = [
        (v, pl.BlockSpec((tall, wide), lambda i, m, at=at: (i, at))) for v, wide, at in own + far + weight
    ]
    ins += [(first, state), (second, state)]
    alias = {len(ins) + n: n for n in range(len(filled))}
    ins += [(v, ANYWHERE) for v in filled]
    return run(
        functools.partial(adam_kernel, join, [len(v) for v in (own, far, weight)], groups, per, items),
        name,
        (rows // tall,),
        meta,
        ins,
        [(first.shape, F32, state)] * 2 + [delta_block(k) for k in range(groups)],
        (),
        after,
        alias,
    )


def outer_math(weight, change, momentum, average):
    velocity = OUTER_MOMENTUM * momentum + change
    master = weight - OUTER_RATE * (change + OUTER_MOMENTUM * velocity)
    trail = EMA_KEEP * average + (1.0 - EMA_KEEP) * master
    return velocity, trail, master


def outer_kernel(groups, count, meta, *refs):
    totals, (weight, momentum, average) = refs[:count], refs[count : count + 3]
    change_out, velocity_out, trail_out, master_out, copy_out = refs[-5:]
    total = totals[0][...].astype(F32)
    for other in totals[1:]:
        total = total + other[...].astype(F32)
    change = total * (1.0 / groups)
    velocity, trail, master = outer_math(weight[...], change, momentum[...], average[...])
    change_out[...] = change
    velocity_out[...] = velocity
    trail_out[...] = trail
    master_out[...] = master
    copy_out[...] = master.astype(BF16)


def outer(name, meta, groups, totals, weight, momentum, average, part, filled=(), after=()):
    tall, wide = min(64, weight.shape[1]), weight.shape[2]
    spec = pl.BlockSpec((tall, wide), lambda i, m: (i, 0))
    state = pl.BlockSpec((None, tall, wide), lambda i, m: (part, i, 0))
    ins = [(v, spec) for v in totals] + [(v, state) for v in (weight, momentum, average)]
    alias = {len(ins) + n: n for n in range(len(filled))}
    return run(
        functools.partial(outer_kernel, groups, len(totals)),
        name,
        (weight.shape[1] // tall,),
        meta,
        ins + [(v, ANYWHERE) for v in filled],
        [(weight.shape, F32, state)] * 4 + [(weight.shape, BF16, state)],
        (),
        after,
        alias,
    )


def pause_kernel(meta, *refs):
    refs[-1][0] = 0


def pause(meta, *values, after=()):
    token = ((1,), jnp.int32, pl.BlockSpec(memory_space=pltpu.SMEM))
    out = run(
        pause_kernel, "pause", (1,), meta, [(v, ANYWHERE) for v in values],
        [(v.shape, v.dtype, ANYWHERE) for v in values] + [token], (), after, {n: n for n in range(len(values))},
    )
    line[:] = [out[-1]]
    return out[:-1]


def local(
    block_input,
    cotangent,
    lengths,
    weight_heads,
    weight_hidden,
    norm_gains,
    momentum_heads,
    momentum_hidden,
    momentum_gains,
    average_heads,
    average_hidden,
    average_gains,
    first_heads,
    first_hidden,
    first_gains,
    second_heads,
    second_hidden,
    second_gains,
):
    line.clear()
    groups, ranks = lax.axis_size("group"), lax.axis_size("tensor")
    group = lax.axis_index("group").astype(jnp.int32)
    shard = lax.axis_index("dp").astype(jnp.int32)
    rank = lax.axis_index("tensor").astype(jnp.int32)
    rows_here, width = block_input.shape
    total = rows_here * ranks
    strip = weight_heads.shape[0]
    half = width // 2
    heads = weight_heads.shape[1] // (4 * HEAD_DIM)
    units = weight_hidden.shape[2]
    items = lengths.shape[1]
    ends = jnp.cumsum(lengths[0]).astype(jnp.int32)
    meta = jnp.concatenate([ends, jnp.stack([rank, group, shard])])
    tall = math.gcd(rows_here, 160)
    steps = rows_here // tall
    wait = functools.partial(pause, meta)
    whole = lambda a: pl.BlockSpec(a.shape, lambda *i: (0,) * a.ndim)
    both = pl.BlockSpec((2, width), lambda *i: (0, 0))
    row_block = pl.BlockSpec((tall, width), lambda i, m: (i, 0))
    row_shape = (rows_here, width)
    gain_block = pl.BlockSpec((8, width), lambda i, m: (0, 0))

    def near(value):
        return swap(value, "tensor", 1, ranks)

    def across(value):
        return swap(value, "dp", 1, 2)

    def gather_far(value):
        pieces = {0: value}
        bit = ranks // 2
        while bit > 1:
            pieces |= {k | bit: swap(v, "tensor", bit, ranks) for k, v in pieces.items()}
            bit //= 2
        return [pieces[k] for k in range(0, ranks, 2)]

    def ordered(even, odd):
        return [v for pair in zip(even, odd) for v in pair]

    def gather_near(even, copy):
        return [near(copy)] + [near(v) for v in even[1:]]

    def scatter(name, x, weight, between=None):
        product = lambda n, received=None: term(
            f"{name}_{n}", meta, x, weight, rows_here, ranks, n, received
        )
        far_send = near(product(3))
        if between:
            between()
        far_keep = near(product(1))
        send = product(2, far_send)
        keep = product(0, far_keep)
        return finish_sum(send, keep, rows_here, ranks)

    def along(value):
        return lax.ppermute(value, "group", [(i, (i + 1) % groups) for i in range(groups)])

    def row_parts(own, far):
        return [
            part_of(v, lambda m, k=k, at=at: lax.rem(m[items + 1] + groups - k, groups) * strip + at)
            for k, both_halves in enumerate(zip(own, far)) for at, v in zip((0, half), both_halves)
        ]

    gain_pieces = [norm_gains] + [swap(norm_gains, "group", k, groups) for k in range(1, groups)]
    tall_strip = pl.BlockSpec((strip // 2, heads * 4 * HEAD_DIM), lambda i, m: (i, 0))
    strips = list(run(
        cast_heads_kernel, "cast_heads", (2,), meta, [(weight_heads, tall_strip)],
        [((strip, heads * 4 * HEAD_DIM), BF16, tall_strip)],
    ))
    strips.append(along(strips[0]))
    crossed = [across(strips[0])]
    gains, plain_gains = run(
        functools.partial(gains_kernel, items, half), "gains", (1,), meta,
        [(v, whole(v)) for v in gain_pieces],
        [((2, width), F32, both)] * 2,
        [pltpu.VMEM((groups, 2, width // groups), F32)],
    )
    first_norm, copy = run(
        functools.partial(first_norm_kernel, items, half), "first_norm", (steps,), meta,
        [(block_input, row_block), (gains, both)],
        [(row_shape, BF16, row_block)] * 2,
    )
    even_one = gather_far(first_norm)
    quarter = units // 2
    strip_block = pl.BlockSpec((strip // 2, quarter), lambda i, m: (i, 0))
    shards = run(
        cast_hidden_kernel, "cast_hidden", (2,), meta,
        [(weight_hidden, pl.BlockSpec((2, strip // 2, units), lambda i, m: (0, i, 0)))],
        [((strip, quarter), BF16, strip_block)] * 4,
    )
    odd_first = near(wait(copy, after=crossed)[0])
    back_low, back_copy = run(
        functools.partial(turn_kernel, items, half), "turn", (steps,), meta,
        [(cotangent, row_block)], [(row_shape, BF16, row_block)] * 2,
    )
    strips[1] = wait(strips[1], after=[odd_first])[0]
    strips.append(along(strips[1]))
    crossed.append(across(strips[1]))
    wait()
    strips[2] = wait(strips[2], after=crossed[1:])[0]
    strips.append(along(strips[2]))
    crossed.append(across(strips[2]))
    wait()
    even_one[1:] = wait(*even_one[1:], after=crossed[2:])
    odd_one = [odd_first] + [near(v) for v in even_one[1:]]
    strips[3] = wait(strips[3])[0]
    crossed.append(across(strips[3]))
    def gathered(shard, after=()):
        return lax.all_gather(wait(shard, after=after)[0], "group", axis=0, tiled=True)

    def columns(own, far):
        return [
            part_of(v, lambda m, at=at: at, n * quarter)
            for n in range(2) for at, v in ((0, own[n]), (half, far[n]))
        ]

    lower_own = [gathered(shards[0], odd_one[1:])]
    back_low = wait(back_low)[0]
    even_back = gather_far(back_low)
    all_one = ordered(even_one, odd_one)
    triple, heads_all = rows_matmul(
        "qkv", meta, all_one, row_parts(strips, crossed), store_rounded, [], [(BF16, same)],
        use=heads * 3 * HEAD_DIM, saved=True,
    )
    inward_w = [part_of(heads_all, columns=heads * 3 * HEAD_DIM)]
    outward_w = [part_of(heads_all, source_column=heads * 3 * HEAD_DIM)]
    lower_own.append(gathered(shards[1]))
    lower_own[0] = wait(lower_own[0])[0]
    lower_far = [across(lower_own[0])]
    pairs = 2 if heads % 2 == 0 else 1
    calls = heads // pairs
    mixed, logs = attend(meta, triple, items, rows_here, heads, pairs, 0)
    raise_own = [gathered(shards[2])]
    for n in range(1, calls):
        mixed, logs = attend(meta, triple, items, rows_here, heads, pairs, n, (mixed, logs))
    lower_own[1] = wait(lower_own[1], after=lower_far)[0]
    lower_far.append(across(lower_own[1]))
    back_copy, *even_back[1:] = wait(back_copy, *even_back[1:])
    odd_back = gather_near(even_back, back_copy)
    raise_own.append(gathered(shards[3]))
    wait(after=odd_back)
    keep, received = scatter("project", [mixed], outward_w)
    raise_own[0] = wait(raise_own[0])[0]
    raise_far = [across(raise_own[0])]
    middle, second_norm = run(
        functools.partial(second_norm_kernel, items, half), "second_norm", (steps,), meta,
        [(block_input, row_block), (keep, row_block), (received, row_block), (gains, both)],
        [(row_shape, F32, row_block), (row_shape, BF16, row_block)],
    )
    even_two = gather_far(second_norm)
    odd_first = near(second_norm)
    raise_own[1] = wait(raise_own[1])[0]
    raise_far.append(across(raise_own[1]))
    raise_w = columns(raise_own, raise_far)
    all_back = ordered(even_back, odd_back)
    back_hidden, lower_all = rows_matmul(
        "back_hidden", meta, all_back, columns(lower_own, lower_far), store_rounded, [], [(BF16, same)], saved=True
    )
    lower_w = [part_of(lower_all)]
    wait(after=[odd_first])

    def feed(pieces, first, weight, filled=(), column=0):
        return rows_matmul(
            "raise", meta, pieces, weight, store_gelu, [(back_hidden, lambda i: i + first)],
            [(BF16, lambda i: i + first)] * 2, rows=total, staged=True, filled=filled,
            block_column=column, columns=units,
        )

    filled = ()
    for n in range(2):
        unit_half = [part_of(raise_own[n]), part_of(raise_far[n], lambda m: half)]
        filled = feed([even_two[0], odd_first], 0, unit_half, filled, n)
    even_two[1:] = wait(*even_two[1:])
    odd_two = [odd_first] + [near(v) for v in even_two[1:]]
    wait()
    all_two = ordered(even_two, odd_two)
    hidden, back_before = feed(all_two[2:], 2, raise_w, filled)
    pieces = lambda values: [(v, k * rows_here) for k, v in enumerate(values)]

    def grad(name, left, right, first):
        return weight_grad(name, meta, pieces(left), right if type(right) is list else [right], first, half)

    grad_lower_far = across(grad("lower_far", all_back, hidden, half))
    keep, received = scatter("back_second", [back_before], raise_w)
    grad_raise_far = across(grad("raise_far", all_two, back_before, half))
    grad_lower = grad("lower_own", all_back, hidden, 0)
    middle_back = []

    def second_back():
        middle_back.extend(run(
            lambda meta, *refs: second_back_kernel(*refs), "second_back", (steps,), meta,
            [(v, row_block) for v in (middle, keep, received, back_low)] + [(gains, both)],
            [(row_shape, F32, row_block), ((8, width), F32, gain_block), (row_shape, BF16, row_block)],
        ))
        middle_back.append(gather_far(middle_back[2]))
        middle_back.append(near(middle_back[2]))
        middle_back.append(grad("raise_own", all_two, back_before, 0))
        wait(after=middle_back[4:5])

    out_keep, out_received = scatter("lower", [hidden], lower_w, second_back)
    back_middle, gain_second, back_low_middle, even_middle, odd_first, grad_raise = middle_back

    def summed(delta):
        return lax.psum_scatter(delta, "group", scatter_dimension=0, tiled=True)

    def adam_hidden(name, own, far, weight, part, filled=()):
        moment, square, delta = adam(
            name, meta, items, side_by_side, [(own, units, 0)], [(far, units, 0)],
            [(v, v.shape[1], 0) for v in weight],
            first_hidden, second_hidden, part, filled=filled,
        )
        return moment, square, summed(delta)

    *states, lower_delta = adam_hidden("adam_lower", grad_lower, grad_lower_far, [lower_all], 1)
    even_middle[1:] = wait(*even_middle[1:])
    odd_middle = [odd_first] + [near(v) for v in even_middle[1:]]
    wait()

    all_middle = ordered(even_middle, odd_middle)
    back_mixed = rows_matmul("back_mixed", meta, all_middle, outward_w, store_rounded, [], [(BF16, same)])[0]
    grad_out_far = across(grad("out_far", all_middle, mixed, half))
    moment_hidden, square_hidden, raise_delta = adam_hidden(
        "adam_raise", grad_raise, grad_raise_far, raise_own, 0, tuple(states)
    )
    back_triples, grad_in_fars = [], []
    for n in range(calls):
        back_triples.append(
            attend_back(meta, triple, mixed, back_mixed, logs, items, rows_here, heads, pairs, n)
        )
        grad_in_fars.append(across(grad("in_far", all_one, back_triples[n], half)))
        if n == 0:
            grad_out = grad("out_own", all_middle, mixed, 0)
            hidden_out = outer(
                "outer_lower", meta, groups, [lower_delta], weight_hidden, momentum_hidden, average_hidden, 1,
                after=[out_received],
            )
    product = lambda n, received=None: term(
        f"back_first_{n}", meta, back_triples, inward_w, rows_here, ranks, n, received
    )
    far_send = near(product(3))
    far_keep = near(product(1))
    send = product(2, far_send)
    grad_in = grad("in_own", all_one, back_triples, 0)
    in_wide, out_wide = pairs * 3 * HEAD_DIM, heads * HEAD_DIM
    moment_heads, square_heads, *deltas = adam(
        "adam_heads", meta, items, by_head,
        [(grad_in, calls * in_wide, 0), (grad_out, out_wide, 0)],
        [(v, in_wide, 0) for v in grad_in_fars] + [(grad_out_far, out_wide, 0)],
        [(heads_all, calls * in_wide, 0), (heads_all, out_wide, 3)],
        first_heads[:, None], second_heads[:, None], 0, groups,
    )
    heads_deltas = [deltas[0]] + [
        lax.ppermute(deltas[k], "group", [(i, (i + k) % groups) for i in range(groups)])
        for k in range(1, groups)
    ]
    keep = product(0, far_keep)
    keep, received = finish_sum(send, keep, rows_here, ranks)
    block_output = run(
        functools.partial(output_kernel, items, half), "output", (steps,), meta,
        [(v, row_block) for v in (middle, out_keep, out_received)],
        [(row_shape, BF16, row_block)],
    )[0]
    input_grad, gain_first = run(
        functools.partial(first_back_kernel, items, half), "first_back", (steps,), meta,
        [(block_input, row_block), (gains, both)] + [(v, row_block) for v in (back_middle, keep, received)],
        [(row_shape, F32, row_block), ((8, width), F32, gain_block)],
    )
    gain_grad = run(
        functools.partial(gain_total_kernel, items, half), "gain_total", (1,), meta,
        [(v, whole(v)) for v in (gain_first, gain_second)],
        [((2, width), F32, both)],
    )[0]

    def added(value, other):
        return run(
            add_kernel, "add", (1,), meta, [(value, whole(value)), (other, whole(other))],
            [(value.shape, F32, whole(value))],
        )[0]

    far_gain = across(gain_grad)
    wait()
    gain_grad = added(gain_grad, far_gain)
    bit = 1
    while bit < ranks:
        far_gain = swap(gain_grad, "tensor", bit, ranks)
        wait()
        gain_grad = added(gain_grad, far_gain)
        bit *= 2
    moment_gains, square_gains, delta_gains = adam_math(
        plain_gains, gain_grad, first_gains[0], second_gains[0], GAIN_RATE, 0.0
    )
    short = width // groups

    def gain_part(k):
        return lax.dynamic_slice_in_dim(delta_gains, (group ^ k) * short, short, 1)

    change_gains = gain_part(0)
    for k in range(1, groups):
        change_gains = change_gains + swap(gain_part(k), "group", k, groups)
    change_gains = change_gains / groups
    velocity_gains, trail_gains, master_gains = outer_math(
        norm_gains, change_gains, momentum_gains, average_gains
    )
    change_hidden, velocity_hidden, trail_hidden, master_hidden, copy_hidden = outer(
        "outer_raise", meta, groups, [raise_delta], weight_hidden, momentum_hidden, average_hidden, 0,
        filled=hidden_out,
    )
    change_heads, velocity_heads, trail_heads, master_heads, copy_heads = (
        v[0]
        for v in outer(
            "outer_heads", meta, groups, heads_deltas, weight_heads[None], momentum_heads[None],
            average_heads[None], 0,
        )
    )
    return (
        block_output,
        input_grad,
        moment_heads[:, 0],
        moment_hidden,
        moment_gains[None],
        square_heads[:, 0],
        square_hidden,
        square_gains[None],
        change_heads,
        change_hidden,
        change_gains,
        velocity_heads,
        velocity_hidden,
        velocity_gains,
        trail_heads,
        trail_hidden,
        trail_gains,
        master_heads,
        master_hidden,
        master_gains,
        copy_heads,
        copy_hidden,
    )


def solution(mesh):
    rows = P(("group", "dp", "tensor"), None)
    heads, hidden, gains = P(("dp", "group"), "tensor"), P(None, ("dp", "group"), "tensor"), P(None, "group")
    states = (P("group", "dp", "tensor"), P("group", None, "dp", "tensor"), P("group", None, None))
    in_specs = (rows, rows, P(("group", "dp"), None)) + (heads, hidden, gains) * 3 + states * 2
    out_specs = (rows, rows) + states * 2 + (heads, hidden, gains) * 4 + (heads, hidden)
    return jax.shard_map(local, mesh=mesh, in_specs=in_specs, out_specs=out_specs, check_vma=False)
```
